32 devices in a mesh: fsdp: 8 (over z, y), tensor: 4 (over x, core).
Axes of the slice: x: 2, y: 2, z: 4, core: 2. Of those that a mesh axis runs over, the one named last changes fastest.
Arguments:
- image_rows: float32 [96, 196, 512], P(('fsdp', 'tensor')), may hold values from -6 to 6
- cotangent: float32 [96, 196, 512], P(('fsdp', 'tensor')), may hold values from -6 to 6
- live_counts: int32 [8], P('fsdp'), may hold values from 6 to 12, as said below
- qkv_weight: float32 [2, 512, 3, 512], P(None, 'fsdp', None, 'tensor'), may hold values from -0.25 to 0.25
- qkv_first: float32 [2, 512, 3, 512], P(None, 'fsdp', None, 'tensor'), may hold values from -80 to 80
- qkv_second: float32 [2, 512, 3, 512], P(None, 'fsdp', None, 'tensor'), may hold values from 14.112 to 56.448
- out_weight: float32 [2, 512, 512], P(None, 'tensor', 'fsdp'), may hold values from -0.75 to 0.75
- out_first: float32 [2, 512, 512], P(None, 'tensor', 'fsdp'), may hold values from -40 to 40
- out_second: float32 [2, 512, 512], P(None, 'tensor', 'fsdp'), may hold values from 3.552 to 14.112
- up_weight: float32 [2, 512, 2048], P(None, 'fsdp', 'tensor'), may hold values from -0.25 to 0.25
- up_first: float32 [2, 512, 2048], P(None, 'fsdp', 'tensor'), may hold values from -28 to 28
- up_second: float32 [2, 512, 2048], P(None, 'fsdp', 'tensor'), may hold values from 1.728 to 6.912
- down_weight: float32 [2, 2048, 512], P(None, 'tensor', 'fsdp'), may hold values from -0.125 to 0.125
- down_first: float32 [2, 2048, 512], P(None, 'tensor', 'fsdp'), may hold values from -48 to 48
- down_second: float32 [2, 2048, 512], P(None, 'tensor', 'fsdp'), may hold values from 5.952 to 23.712
- rel_table: float32 [2, 16, 169], P(None, 'tensor'), may hold values from -3 to 3
- rel_first: float32 [2, 16, 169], P(None, 'tensor'), may hold values from -40 to 40
- rel_second: float32 [2, 16, 169], P(None, 'tensor'), may hold values from 3.552 to 14.112
- qv_bias: float32 [2, 2, 512], P(None, None, 'tensor'), may hold values from -1.75 to 1.75
- qv_first: float32 [2, 2, 512], P(None, None, 'tensor'), may hold values from -80 to 80
- qv_second: float32 [2, 2, 512], P(None, None, 'tensor'), may hold values from 14.112 to 56.448
- hidden_bias: float32 [2, 2048], P(None, 'tensor'), may hold values from -1.75 to 1.75
- hidden_first: float32 [2, 2048], P(None, 'tensor'), may hold values from -28 to 28
- hidden_second: float32 [2, 2048], P(None, 'tensor'), may hold values from 1.728 to 6.912
- norm_gain: float32 [2, 2, 512], replicated, may hold values from 0.4 to 1.6
- gain_first: float32 [2, 2, 512], replicated, may hold values from -80 to 80
- gain_second: float32 [2, 2, 512], replicated, may hold values from 14.112 to 56.448
- norm_bias: float32 [2, 4, 512], replicated, may hold values from -1.75 to 1.75
- bias_first: float32 [2, 4, 512], replicated, may hold values from -80 to 80
- bias_second: float32 [2, 4, 512], replicated, may hold values from 14.112 to 56.448
Outputs:
- block_out: float32 [96, 196, 512], P(('fsdp', 'tensor'))
- input_grad: float32 [96, 196, 512], P(('fsdp', 'tensor'))
- qkv_weight_next: float32 [2, 512, 3, 512], P(None, 'fsdp', None, 'tensor')
- qkv_first_next: float32 [2, 512, 3, 512], P(None, 'fsdp', None, 'tensor')
- qkv_second_next: float32 [2, 512, 3, 512], P(None, 'fsdp', None, 'tensor')
- out_weight_next: float32 [2, 512, 512], P(None, 'tensor', 'fsdp')
- out_first_next: float32 [2, 512, 512], P(None, 'tensor', 'fsdp')
- out_second_next: float32 [2, 512, 512], P(None, 'tensor', 'fsdp')
- up_weight_next: float32 [2, 512, 2048], P(None, 'fsdp', 'tensor')
- up_first_next: float32 [2, 512, 2048], P(None, 'fsdp', 'tensor')
- up_second_next: float32 [2, 512, 2048], P(None, 'fsdp', 'tensor')
- down_weight_next: float32 [2, 2048, 512], P(None, 'tensor', 'fsdp')
- down_first_next: float32 [2, 2048, 512], P(None, 'tensor', 'fsdp')
- down_second_next: float32 [2, 2048, 512], P(None, 'tensor', 'fsdp')
- rel_table_next: float32 [2, 16, 169], P(None, 'tensor')
- rel_first_next: float32 [2, 16, 169], P(None, 'tensor')
- rel_second_next: float32 [2, 16, 169], P(None, 'tensor')
- qv_bias_next: float32 [2, 2, 512], P(None, None, 'tensor')
- qv_first_next: float32 [2, 2, 512], P(None, None, 'tensor')
- qv_second_next: float32 [2, 2, 512], P(None, None, 'tensor')
- hidden_bias_next: float32 [2, 2048], P(None, 'tensor')
- hidden_first_next: float32 [2, 2048], P(None, 'tensor')
- hidden_second_next: float32 [2, 2048], P(None, 'tensor')
- norm_gain_next: float32 [2, 2, 512], replicated
- gain_first_next: float32 [2, 2, 512], replicated
- gain_second_next: float32 [2, 2, 512], replicated
- norm_bias_next: float32 [2, 4, 512], replicated
- bias_first_next: float32 [2, 4, 512], replicated
- bias_second_next: float32 [2, 4, 512], replicated
The draws below stay inside these ranges and needn't reach their ends.
Inputs may be any that keep to these rules, and one draw needn't show every extreme that they name: Image slot s of fsdp index i is live when s < live_counts[i]; an index's 12 slots lie in order over its 3-slot devices along tensor. At least one index has all 12 slots live.
All inputs are finite; a program needn't handle non-finite values.
Results may differ from the reference program's by a relative error of at most 0.015.
Values may be sent and summed in bfloat16 or wider, within the bound.
A program may use at most 192 MiB of HBM per device.

```python
import math
import jax
import jax.numpy as jnp
from jax import lax

D = 512
HEADS = 16
HEAD_DIM = 32
FF = 2048
SIDE = 14
WIN = 7
SHIFT = 3
RELS = 169
BLOCKS = 2
ADAM_STEP = 10
CAP = 12
IMAGES = 96
N_FSDP = 8


def draw_live_counts(key, part):
    key = jax.random.fold_in(key, 7)
    base_key, full_key = jax.random.split(key)
    counts_drawn = jax.random.randint(base_key, (N_FSDP,), (CAP + 1) // 2, CAP + 1, dtype=jnp.int32)
    full_index = jax.random.randint(full_key, (), 0, N_FSDP, dtype=jnp.int32)
    return jnp.where(jnp.arange(N_FSDP, dtype=jnp.int32) == full_index, CAP, counts_drawn).astype(jnp.int32)


def level_of(stream_key, shape, pieces, low, top_value):
    def one(dim, parts):
        steps = jax.random.uniform(jax.random.fold_in(jax.random.fold_in(stream_key, 6), dim), (parts,), jnp.float32, low / len(pieces), top_value / len(pieces))
        return jnp.repeat(jnp.exp(steps), shape[dim] // parts).reshape((-1,) + (1,) * (len(shape) - dim - 1))

    factor_of = one(*pieces[0])
    for cut in pieces[1:]:
        factor_of = factor_of * one(*cut)
    return factor_of


def bell_draw(rng, shape, spread, most, pieces=(), kind=jnp.bfloat16):
    drawn = jax.random.normal(rng, shape, jnp.float32) * spread
    if len(pieces) > 0:
        drawn = level_of(rng, shape, pieces, -0.22, 0.18) * drawn
    return jnp.clip(drawn, min=-most, max=most).astype(kind)


def setup_inputs(seed: int = 0) -> dict:
    seeds = jax.random.split(jax.random.key(seed), 31)
    return {
        "image_rows": bell_draw(seeds[0], (IMAGES, SIDE * SIDE, D), 1.0, 6.0, ((0, 32),), jnp.float32),
        "cotangent": bell_draw(seeds[1], (IMAGES, SIDE * SIDE, D), 1.0, 6.0, ((0, 32),), jnp.float32),
        "live_counts": draw_live_counts(jax.random.fold_in(seeds[30], 71), 0),
        "qkv_weight": bell_draw(seeds[3], (BLOCKS, D, 3, D), D ** -0.5, 0.25, ((1, 8), (3, 4)), jnp.float32),
        "qkv_first": bell_draw(seeds[4], (BLOCKS, D, 3, D), (1.33 * IMAGES ** 0.5), 80.0, ((1, 8), (3, 4)), jnp.float32),
        "qkv_second": jnp.clip(jnp.exp(math.log(56.448) - 1.3862944 * jax.random.uniform(seeds[5], (BLOCKS, D, 3, D), jnp.float32) ** level_of(seeds[5], (BLOCKS, D, 3, D), ((1, 8), (3, 4)), -0.2, 0.2)), 14.112, 56.448),
        "out_weight": bell_draw(seeds[6], (BLOCKS, D, D), (D // 8) ** -0.5, 0.75, ((1, 4), (2, 8)), jnp.float32),
        "out_first": bell_draw(seeds[7], (BLOCKS, D, D), (0.67 * IMAGES ** 0.5), 40.0, ((1, 4), (2, 8)), jnp.float32),
        "out_second": jnp.clip(jnp.exp(math.log(14.112) - 1.3795147 * jax.random.uniform(seeds[8], (BLOCKS, D, D), jnp.float32) ** level_of(seeds[8], (BLOCKS, D, D), ((1, 4), (2, 8)), -0.2, 0.2)), 3.552, 14.112),
        "up_weight": bell_draw(seeds[9], (BLOCKS, D, FF), D ** -0.5, 0.25, ((1, 8), (2, 4)), jnp.float32),
        "up_first": bell_draw(seeds[10], (BLOCKS, D, FF), (0.47 * IMAGES ** 0.5), 28.0, ((1, 8), (2, 4)), jnp.float32),
        "up_second": jnp.clip(jnp.exp(math.log(6.912) - 1.3862944 * jax.random.uniform(seeds[11], (BLOCKS, D, FF), jnp.float32) ** level_of(seeds[11], (BLOCKS, D, FF), ((1, 8), (2, 4)), -0.2, 0.2)), 1.728, 6.912),
        "down_weight": bell_draw(seeds[12], (BLOCKS, FF, D), FF ** -0.5, 0.125, ((1, 4), (2, 8)), jnp.float32),
        "down_first": bell_draw(seeds[13], (BLOCKS, FF, D), (0.86 * IMAGES ** 0.5), 48.0, ((1, 4), (2, 8)), jnp.float32),
        "down_second": jnp.clip(jnp.exp(math.log(23.712) - 1.3822539 * jax.random.uniform(seeds[14], (BLOCKS, FF, D), jnp.float32) ** level_of(seeds[14], (BLOCKS, FF, D), ((1, 4), (2, 8)), -0.2, 0.2)), 5.952, 23.712),
        "rel_table": bell_draw(seeds[15], (BLOCKS, HEADS, RELS), 0.5, 3.0, ((1, 4),), jnp.float32),
        "rel_first": bell_draw(seeds[16], (BLOCKS, HEADS, RELS), (0.67 * IMAGES ** 0.5), 40.0, ((1, 4),), jnp.float32),
        "rel_second": jnp.clip(jnp.exp(math.log(14.112) - 1.3795147 * jax.random.uniform(seeds[17], (BLOCKS, HEADS, RELS), jnp.float32) ** level_of(seeds[17], (BLOCKS, HEADS, RELS), ((1, 4),), -0.2, 0.2)), 3.552, 14.112),
        "qv_bias": bell_draw(seeds[18], (BLOCKS, 2, D), 0.3, 1.75, ((2, 4),), jnp.float32),
        "qv_first": bell_draw(seeds[19], (BLOCKS, 2, D), (1.33 * IMAGES ** 0.5), 80.0, ((2, 4),), jnp.float32),
        "qv_second": jnp.clip(jnp.exp(math.log(56.448) - 1.3862944 * jax.random.uniform(seeds[20], (BLOCKS, 2, D), jnp.float32) ** level_of(seeds[20], (BLOCKS, 2, D), ((2, 4),), -0.2, 0.2)), 14.112, 56.448),
        "hidden_bias": bell_draw(seeds[21], (BLOCKS, FF), 0.3, 1.75, ((1, 4),), jnp.float32),
        "hidden_first": bell_draw(seeds[22], (BLOCKS, FF), (0.47 * IMAGES ** 0.5), 28.0, ((1, 4),), jnp.float32),
        "hidden_second": jnp.clip(jnp.exp(math.log(6.912) - 1.3862944 * jax.random.uniform(seeds[23], (BLOCKS, FF), jnp.float32) ** level_of(seeds[23], (BLOCKS, FF), ((1, 4),), -0.2, 0.2)), 1.728, 6.912),
        "norm_gain": jnp.clip(jax.random.uniform(seeds[24], (BLOCKS, 2, D), jnp.float32, 0.4, 1.6), 0.4, 1.6),
        "gain_first": bell_draw(seeds[25], (BLOCKS, 2, D), (1.33 * IMAGES ** 0.5), 80.0, (), jnp.float32),
        "gain_second": jnp.clip(jnp.exp(jax.random.uniform(seeds[26], (BLOCKS, 2, D), jnp.float32, math.log(14.112), math.log(56.448))), 14.112, 56.448),
        "norm_bias": bell_draw(seeds[27], (BLOCKS, 4, D), 0.3, 1.75, (), jnp.float32),
        "bias_first": bell_draw(seeds[28], (BLOCKS, 4, D), (1.33 * IMAGES ** 0.5), 80.0, (), jnp.float32),
        "bias_second": jnp.clip(jnp.exp(jax.random.uniform(seeds[29], (BLOCKS, 4, D), jnp.float32, math.log(14.112), math.log(56.448))), 14.112, 56.448),
    }


@jax.custom_vjp
def low(v):
    return lax.optimization_barrier(v.astype(jnp.bfloat16)).astype(jnp.float32)

@jax.custom_vjp
def low_back(v):
    return v

def low_keep(v):
    return (low(v), None)

def low_pass(kept, grad):
    return (grad,)

def back_keep(v):
    return (v, None)

def back_low(kept, grad):
    return (low(grad),)
low.defvjp(low_keep, low_pass)
low_back.defvjp(back_keep, back_low)
HIGHEST = lax.Precision.HIGHEST
NORM_EPS = 1e-05
BETA_ONE = 0.9
BETA_TWO = 0.999
MATRIX_RATE = 0.04
SMALL_RATE = 0.3
WEIGHT_DECAY = 0.05
ADAM_EPS = 1e-08
MASK_FILL = -100.0

def to_windows(field_rows):
    leading = field_rows.shape[:-3]
    channels = field_rows.shape[-1]
    per_side = SIDE // WIN
    lead_dims = len(leading)
    field_rows = field_rows.reshape(leading + (per_side, WIN, per_side, WIN, channels))
    field_rows = jnp.moveaxis(field_rows, lead_dims + 2, lead_dims + 1)
    return field_rows.reshape(leading + (per_side * per_side, WIN * WIN, channels))

def from_windows(field_rows):
    leading = field_rows.shape[:-3]
    channels = field_rows.shape[-1]
    per_side = SIDE // WIN
    lead_dims = len(leading)
    field_rows = field_rows.reshape(leading + (per_side, per_side, WIN, WIN, channels))
    field_rows = jnp.moveaxis(field_rows, lead_dims + 1, lead_dims + 2)
    return field_rows.reshape(leading + (SIDE, SIDE, channels))

def rel_lookup():
    position = jnp.arange(WIN * WIN, dtype=jnp.int32)
    row_pos = position // WIN
    col_pos = position % WIN
    return (row_pos[:, None] - row_pos[None, :] + WIN - 1) * (2 * WIN - 1) + (col_pos[:, None] - col_pos[None, :] + WIN - 1)

def window_mask(shifted):
    if not shifted:
        return jnp.zeros(((SIDE // WIN) ** 2, WIN * WIN, WIN * WIN), jnp.float32)
    coords = jnp.arange(SIDE, dtype=jnp.int32)
    bands = (coords >= SIDE - WIN).astype(jnp.int32) + (coords >= SIDE - SHIFT).astype(jnp.int32)
    region = bands[:, None] * 3 + bands[None, :]
    labels = to_windows(region[:, :, None])[:, :, 0]
    return jnp.where(labels[:, :, None] == labels[:, None, :], 0.0, MASK_FILL).astype(jnp.float32)

def layer_norm(values, gain_row, offset_row):
    row_mean = lax.optimization_barrier(jnp.mean(values, -1, keepdims=True))
    centred = values - row_mean
    row_var = lax.optimization_barrier(jnp.mean(centred * centred, -1, keepdims=True))
    return centred * lax.rsqrt(row_var + NORM_EPS) * gain_row + offset_row

def prepare(weight_set):
    qkv_w, out_w, up_w, down_w, rel_values, qv_b, hidden_b, gain_rows, offset_rows = weight_set
    offset_rows = jnp.concatenate([offset_rows[:, :2], low(offset_rows[:, 2:])], 1)
    return (low(qkv_w), low(out_w), low(up_w), low(down_w), low(rel_values), low(qv_b), low(hidden_b), gain_rows, offset_rows)

def swin_block(residual, params, shifted):
    qkv_w, out_w, up_w, down_w, rel_values, qv_b, hidden_b, gain_rows, offset_rows = params
    image_count = residual.shape[0]
    heads_all = rel_values.shape[0]
    normed = low(layer_norm(residual, gain_rows[0], offset_rows[0]))
    grid_rows = normed.reshape(image_count, SIDE, SIDE, D)
    if shifted:
        grid_rows = jnp.roll(grid_rows, (-SHIFT, -SHIFT), (1, 2))
    tokens = to_windows(grid_rows)

    def project(column, bias_term):
        return jnp.einsum('bwtc,cd->bwtd', tokens, qkv_w[:, column], precision=HIGHEST) + bias_term
    query_rows = low(low_back(project(0, qv_b[0])))
    key_rows = low(low_back(project(1, 0.0)))
    value_rows = low(low_back(project(2, qv_b[1])))
    head_shape = tokens.shape[:3] + (heads_all, HEAD_DIM)
    rel_bias = rel_values[:, rel_lookup()]
    scores = jnp.einsum('bwqhe,bwkhe->bwhqk', query_rows.reshape(head_shape), key_rows.reshape(head_shape), precision=HIGHEST) * HEAD_DIM ** (-0.5)
    scores = low_back(scores + rel_bias[None, None] + window_mask(shifted)[None, :, None])
    prob_rows = jax.nn.softmax(scores, axis=-1)
    mixed = jnp.einsum('bwhqk,bwkhe->bwqhe', low(prob_rows), value_rows.reshape(head_shape), precision=HIGHEST)
    mixed = low(low_back(mixed.reshape(tokens.shape)))
    grid_rows = from_windows(mixed)
    if shifted:
        grid_rows = jnp.roll(grid_rows, (SHIFT, SHIFT), (1, 2))
    attended = grid_rows.reshape(residual.shape)
    middle = residual + low_back(jnp.einsum('btc,cd->btd', attended, out_w, precision=HIGHEST)) + offset_rows[2]
    normed_two = low(layer_norm(middle, gain_rows[1], offset_rows[1]))
    hidden_pre = low_back(jnp.einsum('btc,cf->btf', normed_two, up_w, precision=HIGHEST) + hidden_b)
    hidden = low(jax.nn.gelu(hidden_pre, approximate=False))
    return middle + low_back(jnp.einsum('btf,fc->btc', hidden, down_w, precision=HIGHEST)) + offset_rows[3]

def adam(weight, first_moment, second_moment, gradient, step_rate, decay_rate):
    first_new = BETA_ONE * first_moment + (1.0 - BETA_ONE) * gradient
    second_new = BETA_TWO * second_moment + (1.0 - BETA_TWO) * gradient * gradient
    first_hat = first_new / (1.0 - BETA_ONE ** ADAM_STEP)
    second_hat = second_new / (1.0 - BETA_TWO ** ADAM_STEP)
    weight_new = weight - step_rate * (first_hat / (jnp.sqrt(second_hat) + ADAM_EPS) + decay_rate * weight)
    return (weight_new, first_new, second_new)

def reference(image_rows, cotangent, live_counts, qkv_weight, qkv_first, qkv_second, out_weight, out_first, out_second, up_weight, up_first, up_second, down_weight, down_first, down_second, rel_table, rel_first, rel_second, qv_bias, qv_first, qv_second, hidden_bias, hidden_first, hidden_second, norm_gain, gain_first, gain_second, norm_bias, bias_first, bias_second):
    weights = (qkv_weight, out_weight, up_weight, down_weight, rel_table, qv_bias, hidden_bias, norm_gain, norm_bias)
    groups = image_rows.reshape(N_FSDP, CAP, SIDE * SIDE, D)
    back_groups = cotangent.reshape(N_FSDP, CAP, SIDE * SIDE, D)
    slot_ids = jnp.arange(CAP, dtype=jnp.int32)

    def forward(weight_set, residual):
        used = prepare(weight_set)
        for layer_idx in range(BLOCKS):
            residual = swin_block(residual, tuple((member[layer_idx] for member in used)), layer_idx % 2 == 1)
        return residual

    def one_group(totals, inputs):
        residual, back_rows, live_count = inputs
        result, pullback = jax.vjp(forward, weights, residual)
        live_mask = (slot_ids < live_count).astype(jnp.float32)[:, None, None]
        weight_grads, residual_grad = pullback(back_rows * live_mask)
        return (jax.tree.map(jnp.add, totals, weight_grads), (result, residual_grad))
    zero_grads = jax.tree.map(jnp.zeros_like, weights)
    grads, (outputs, input_grads) = lax.scan(one_group, zero_grads, (groups, back_groups, live_counts))
    qkv_next = adam(qkv_weight, qkv_first, qkv_second, grads[0], MATRIX_RATE, WEIGHT_DECAY)
    out_next = adam(out_weight, out_first, out_second, grads[1], MATRIX_RATE, WEIGHT_DECAY)
    up_next = adam(up_weight, up_first, up_second, grads[2], MATRIX_RATE, WEIGHT_DECAY)
    down_next = adam(down_weight, down_first, down_second, grads[3], MATRIX_RATE, WEIGHT_DECAY)
    rel_next = adam(rel_table, rel_first, rel_second, grads[4], SMALL_RATE, 0.0)
    qv_next = adam(qv_bias, qv_first, qv_second, grads[5], SMALL_RATE, 0.0)
    hidden_next = adam(hidden_bias, hidden_first, hidden_second, grads[6], SMALL_RATE, 0.0)
    gain_next = adam(norm_gain, gain_first, gain_second, grads[7], SMALL_RATE, 0.0)
    offset_next = adam(norm_bias, bias_first, bias_second, grads[8], SMALL_RATE, 0.0)
    return (outputs.reshape(image_rows.shape), input_grads.reshape(image_rows.shape), qkv_next[0], qkv_next[1], qkv_next[2], out_next[0], out_next[1], out_next[2], up_next[0], up_next[1], up_next[2], down_next[0], down_next[1], down_next[2], rel_next[0], rel_next[1], rel_next[2], qv_next[0], qv_next[1], qv_next[2], hidden_next[0], hidden_next[1], hidden_next[2], gain_next[0], gain_next[1], gain_next[2], offset_next[0], offset_next[1], offset_next[2])
```

```python
import functools

import numpy as np
import jax
import jax.numpy as jnp
from jax import lax
from jax.experimental import pallas as pl
from jax.experimental.pallas import tpu as pltpu
from jax.sharding import PartitionSpec as P

HEAD_DIM = 32
SIDE = 14
WIN = 7
SHIFT = 3
BLOCKS = 2
ADAM_STEP = 10
TOKENS = SIDE * SIDE
WINS = (SIDE // WIN) ** 2
SPAN = WIN * WIN
PAD = 64
IMG_PAD = WINS * PAD
IMG_ROWS = 208
GROUP = 4

NORM_EPS = 1e-05
BETA_ONE = 0.9
BETA_TWO = 0.999
MATRIX_RATE = 0.04
SMALL_RATE = 0.3
WEIGHT_DECAY = 0.05
ADAM_EPS = 1e-08
MASK_FILL = -100.0
KEY_FILL = -1e30
INV_ROOT = HEAD_DIM ** (-0.5)
MIB = 1024 * 1024
F32 = jnp.float32
BF16 = jnp.bfloat16
NT = (((1,), (1,)), ((), ()))
TN = (((0,), (0,)), ((), ()))


def window_source(shifted):
    out = np.zeros((WINS, SPAN), np.int64)
    step = SHIFT if shifted else 0
    per = SIDE // WIN
    for w in range(WINS):
        for p in range(SPAN):
            r = (w // per) * WIN + p // WIN
            c = (w % per) * WIN + p % WIN
            out[w, p] = ((r + step) % SIDE) * SIDE + (c + step) % SIDE
    return out


def image_base(i):
    return (i * TOKENS) // 16 * 16


def permutations(images):
    perm = np.zeros((BLOCKS, images, IMG_PAD, IMG_ROWS), np.float32)
    for b in range(BLOCKS):
        src = window_source(b % 2 == 1)
        for i in range(images):
            off = i * TOKENS - image_base(i)
            for w in range(WINS):
                for p in range(SPAN):
                    perm[b, i, w * PAD + p, off + src[w, p]] = 1.0
    return perm


def mask_table():
    out = np.zeros((BLOCKS, WINS, PAD, PAD), np.float32)
    coords = np.arange(SIDE)
    bands = (coords >= SIDE - WIN).astype(int) + (coords >= SIDE - SHIFT).astype(int)
    region = (bands[:, None] * 3 + bands[None, :]).reshape(-1)
    base = window_source(False)
    for b in range(BLOCKS):
        for w in range(WINS):
            if b % 2 == 1:
                lab = region[base[w]]
                out[b, w, :SPAN, :SPAN] = np.where(lab[:, None] == lab[None, :], 0.0, MASK_FILL)
            out[b, w, SPAN:, :] = KEY_FILL
    return out


def rel_onehot(rels):
    out = np.zeros((rels, PAD, PAD), np.float32)
    pos = np.arange(SPAN)
    row, col = pos // WIN, pos % WIN
    for q in range(SPAN):
        e = (row[q] - row + WIN - 1) * (2 * WIN - 1) + col[q] - col + WIN - 1
        out[e, np.arange(SPAN), q] = 1.0
    return out


def dot(a, b, dims=None):
    if dims is None:
        return jnp.dot(a, b, preferred_element_type=F32)
    return lax.dot_general(a, b, dims, preferred_element_type=F32)


def lane_heads(width):
    return lax.broadcasted_iota(jnp.int32, (1, width), 1) // HEAD_DIM


def spread(rows, heads):
    zero = jnp.zeros_like(rows)
    return jnp.concatenate([jnp.where(heads == h, rows, zero) for h in range(GROUP)], 0)


def gather_diag(prod, heads):
    out = prod[0:PAD]
    for h in range(1, GROUP):
        out = jnp.where(heads == h, prod[h * PAD : (h + 1) * PAD], out)
    return out


def gelu_pair(u):
    au = jnp.abs(u)
    t = 1.0 / (1.0 + (0.3275911 * 0.7071067811865476) * au)
    e = jnp.exp(-0.5 * u * u)
    q = 1.061405429 * 0.5
    q = q * t - 1.453152027 * 0.5
    q = q * t + 1.421413741 * 0.5
    q = q * t - 0.284496736 * 0.5
    q = q * t + 0.254829592 * 0.5
    q = q * t * e
    phi = jnp.where(u >= 0, 1.0 - q, q)
    return u * phi, phi + u * e * 0.3989422804014327


def chunks(rows, size):
    return [(r, min(size, rows - r)) for r in range(0, rows, size)]


def norm_rows(x):
    mean = jnp.mean(x, -1, keepdims=True)
    cen = x - mean
    inv = lax.rsqrt(jnp.mean(cen * cen, -1, keepdims=True) + NORM_EPS)
    return cen * inv, inv


def put_rows(ref, vals):
    images = len(vals)
    for i in range(images):
        base = image_base(i)
        lead = 0
        if i > 0:
            lead = image_base(i - 1) + IMG_ROWS - base
            mix = vals[i - 1][IMG_ROWS - lead :] + vals[i][:lead]
            ref[base : base + lead, :] = mix.astype(ref.dtype)
        end = image_base(i + 1) - base if i + 1 < images else IMG_ROWS
        ref[base + lead : base + end, :] = vals[i][lead:end].astype(ref.dtype)


def norm_into(src, dst, gain, off):
    for r, n in chunks(src.shape[0], 112):
        unit, _ = norm_rows(src[r : r + n, :])
        dst[r : r + n, :] = (unit * gain + off).astype(BF16)


def fold(val):
    rows, cols = val.shape
    return jnp.sum(val.reshape(rows // 8, 8, cols), 0)


def back_norm(src, grad, gain, dst):
    width = src.shape[1]
    sums = [jnp.zeros((8, width), F32) for _ in range(3)]
    for r, n in chunks(src.shape[0], 112):
        unit, inv = norm_rows(src[r : r + n, :])
        gr = grad[r : r + n, :]
        e = gr * gain
        res = dst[r : r + n, :] + inv * (
            e - jnp.mean(e, -1, keepdims=True) - unit * jnp.mean(e * unit, -1, keepdims=True)
        )
        dst[r : r + n, :] = res
        for j, val in enumerate((gr * unit, gr, res)):
            sums[j] = sums[j] + fold(val)
    return [jnp.sum(s, 0, keepdims=True) for s in sums]


def column_sum(ref):
    total = jnp.zeros((8, ref.shape[1]), F32)
    for r, n in chunks(ref.shape[0], 112):
        total = total + fold(ref[r : r + n, :])
    return jnp.sum(total, 0, keepdims=True)


GAIN_ROW = 0
BIAS_ROW = GAIN_ROW + 2 * BLOCKS
QV_ROW = BIAS_ROW + 4 * BLOCKS
HID_ROW = QV_ROW + 2 * BLOCKS


def compute_kernel(
    x_in, ct_in, live, g_hbm, rel_add, mask, gains, offs, qvb, hb, perm, perm_t,
    x_out, dx_out, dg_hbm, dsum, small,
    wt, xs, ms, a_s, aw, qkv, pts, ow, osb, a2, gl, gp, ubuf, acc, dx, cut, awt, dwin, da,
    mlp_st, out_st, att_st, in_sem, out_sem, att_sem,
):
    images = x_in.shape[0]
    groups = wt.shape[1]
    rows, width = xs.shape[1:]
    lanes = GROUP * HEAD_DIM
    hid = gl.shape[3]
    c_out, c_up, c_down = 3 * lanes, 4 * lanes, 4 * lanes + hid
    c_end = c_down + hid
    heads = lane_heads(lanes)
    loads = []
    for b in range(BLOCKS):
        cp = pltpu.make_async_copy(g_hbm.at[b], wt.at[b], in_sem.at[b])
        cp.start()
        loads.append(cp)
    used = images * TOKENS
    floor = used // 8 * 8
    xs[0, floor:rows, :] = jnp.zeros((rows - floor, width), F32)
    dx[floor:rows, :] = jnp.zeros((rows - floor, width), F32)
    for i in range(images):
        xs[0, i * TOKENS : (i + 1) * TOKENS, :] = x_in[i]
        dx[i * TOKENS : (i + 1) * TOKENS, :] = ct_in[i] * live[i]

    for b in range(BLOCKS):
        loads[b].wait()
        off = [offs[b, j : j + 1, :] for j in range(4)]
        off2, off3 = (o.astype(BF16).astype(F32) for o in off[2:])
        norm_into(xs.at[b], a_s, gains[b, 0:1, :], off[0])
        for i in range(images):
            base = image_base(i)
            aw[b, i * IMG_PAD : (i + 1) * IMG_PAD, :] = dot(
                perm[b, i], a_s[base : base + IMG_ROWS, :]
            ).astype(BF16)

        def attend(t, carry):
            rows_qkv = dot(aw[b], wt[b, t, :, 0 : 3 * lanes])
            for j in range(3):
                part = rows_qkv[:, j * lanes : (j + 1) * lanes]
                if j != 1:
                    part = part + qvb[b, j // 2, pl.ds(t, 1), :].astype(BF16).astype(F32)
                qkv[b, t, :, j * lanes : (j + 1) * lanes] = part.astype(BF16)

            def window(w, c2):
                r = pl.multiple_of(w * PAD, PAD)
                q = qkv[b, t, pl.ds(r, PAD), 0:lanes]
                k = qkv[b, t, pl.ds(r, PAD), lanes : 2 * lanes]
                v = qkv[b, t, pl.ds(r, PAD), 2 * lanes : 3 * lanes]
                s = dot(k, spread(q, heads), NT) * INV_ROOT + rel_add[b, t].astype(F32)
                s = s + mask[b, lax.rem(w, WINS)]
                e = jnp.exp(s - jnp.max(s, 0, keepdims=True))
                p = (e * (1.0 / jnp.sum(e, 0, keepdims=True))).astype(BF16)
                pts[b, t, w] = p
                ow[pl.ds(r, PAD), :] = gather_diag(dot(p, v, TN), heads).astype(BF16)
                return c2

            lax.fori_loop(0, images * WINS, window, 0, unroll=2)
            put_rows(
                osb.at[b, t],
                [dot(perm_t[b, i], ow[i * IMG_PAD : (i + 1) * IMG_PAD, :]) for i in range(images)],
            )
            return carry

        lax.fori_loop(0, groups, attend, 0)
        y = dot(osb[b, 0], wt[b, 0, :, c_out:c_up], NT)
        for t in range(1, groups):
            y = y + dot(osb[b, t], wt[b, t, :, c_out:c_up], NT)
        ms[b] = xs[b] + y + off2
        norm_into(ms.at[b], a2.at[b], gains[b, 1:2, :], off[1])
        acc[...] = ms[b] + off3

        def mlp(t, carry):
            ubuf[...] = dot(a2[b], wt[b, t, :, c_up:c_down])
            hbias = hb[b, pl.ds(t, 1), :].astype(BF16).astype(F32)
            for r, n in chunks(rows, 32):
                g, d = gelu_pair(ubuf[r : r + n, :] + hbias)
                gl[b, t, r : r + n, :] = g.astype(BF16)
                gp[b, t, r : r + n, :] = d.astype(BF16)
            acc[...] += dot(gl[b, t], wt[b, t, :, c_down:c_end], NT)
            return carry

        lax.fori_loop(0, groups, mlp, 0)
        if b + 1 < BLOCKS:
            xs[b + 1] = acc[...]
    for i in range(images):
        x_out[i] = acc[i * TOKENS : (i + 1) * TOKENS, :]

    for b in range(BLOCKS - 1, -1, -1):
        small[BIAS_ROW + 4 * b + 3 : BIAS_ROW + 4 * b + 4, :] = column_sum(dx)
        cut[...] = dx[...].astype(BF16)
        dxt = jnp.transpose(cut[...])
        a_t = jnp.transpose(a2[b])
        acc[...] = jnp.zeros_like(acc)

        def mlp_copy(t, slot):
            return pltpu.make_async_copy(
                mlp_st.at[slot], dg_hbm.at[b, t, :, c_up:c_end], out_sem.at[slot]
            )

        def mlp_back(t, carry):
            slot = lax.rem(t, 2)

            @pl.when(t >= 2)
            def _():
                mlp_copy(t - 2, slot).wait()

            mlp_st[slot, :, hid : 2 * hid] = dot(dxt, gl[b, t]).astype(BF16)
            dh = dot(cut[...], wt[b, t, :, c_down:c_end])
            du = (dh * gp[b, t].astype(F32)).astype(BF16)
            gp[b, t] = du
            small[pl.ds(HID_ROW + b * groups + t, 1), :] = jnp.sum(
                fold(du.astype(F32)), 0, keepdims=True
            )
            mlp_st[slot, :, 0:hid] = dot(a_t, du).astype(BF16)
            acc[...] += dot(du, wt[b, t, :, c_up:c_down], NT)
            mlp_copy(t, slot).start()
            return carry

        lax.fori_loop(0, groups, mlp_back, 0)
        for t in range(groups - 2, groups):
            mlp_copy(t, t % 2).wait()
        sums = back_norm(ms.at[b], acc, gains[b, 1:2, :], dx)
        small[GAIN_ROW + 2 * b + 1 : GAIN_ROW + 2 * b + 2, :] = sums[0]
        small[BIAS_ROW + 4 * b + 1 : BIAS_ROW + 4 * b + 2, :] = sums[1]
        small[BIAS_ROW + 4 * b + 2 : BIAS_ROW + 4 * b + 3, :] = sums[2]
        cut[...] = dx[...].astype(BF16)
        dmt = jnp.transpose(cut[...])
        awt[...] = jnp.transpose(aw[b])
        da[...] = jnp.zeros_like(da)
        out_copies = []
        for t in range(groups):
            out_st[t] = dot(dmt, osb[b, t]).astype(BF16)
            cp = pltpu.make_async_copy(out_st.at[t], dg_hbm.at[b, t, :, c_out:c_up], out_sem.at[2 + t])
            cp.start()
            out_copies.append(cp)

        def att_copy(t, slot):
            return pltpu.make_async_copy(
                att_st.at[slot], dg_hbm.at[b, t, :, 0:c_out], att_sem.at[slot]
            )

        def attend_back(t, carry):
            slot = lax.rem(t, 2)

            @pl.when(t >= 2)
            def _():
                att_copy(t - 2, slot).wait()

            do_t = dot(cut[...], wt[b, t, :, c_out:c_up]).astype(BF16)
            for i in range(images):
                base = image_base(i)
                ow[i * IMG_PAD : (i + 1) * IMG_PAD, :] = dot(
                    perm[b, i], do_t[base : base + IMG_ROWS]
                ).astype(BF16)
            dsum[b, t] = jnp.zeros((PAD, GROUP * PAD), F32)

            def window(w, c2):
                r = pl.multiple_of(w * PAD, PAD)
                q = qkv[b, t, pl.ds(r, PAD), 0:lanes]
                k = qkv[b, t, pl.ds(r, PAD), lanes : 2 * lanes]
                v = qkv[b, t, pl.ds(r, PAD), 2 * lanes : 3 * lanes]
                p = pts[b, t, w]
                dob = spread(ow[pl.ds(r, PAD), :], heads)
                dp = dot(v, dob, NT)
                pf = p.astype(F32)
                ds = (pf * (dp - jnp.sum(pf * dp, 0, keepdims=True))).astype(BF16)
                dsum[b, t] += ds.astype(F32)
                dv = dot(p, dob)
                dk = dot(ds, spread(q, heads)) * INV_ROOT
                dq = gather_diag(dot(ds, k, TN), heads) * INV_ROOT
                dwin[pl.ds(r, PAD), 0:lanes] = dq.astype(BF16)
                dwin[pl.ds(r, PAD), lanes : 2 * lanes] = dk.astype(BF16)
                dwin[pl.ds(r, PAD), 2 * lanes : 3 * lanes] = dv.astype(BF16)
                return c2

            lax.fori_loop(0, images * WINS, window, 0, unroll=2)
            col = pl.ds(pl.multiple_of(t * lanes, lanes), lanes)
            for j in range(2):
                val = dwin[:, 2 * j * lanes : (2 * j + 1) * lanes].astype(F32)
                row = QV_ROW + 2 * b + j
                small[row : row + 1, col] = jnp.sum(fold(val), 0, keepdims=True)
            att_st[slot] = dot(awt[...], dwin[...]).astype(BF16)
            da[...] += dot(dwin[...], wt[b, t, :, 0:c_out], NT)
            att_copy(t, slot).start()
            return carry

        lax.fori_loop(0, groups, attend_back, 0)
        vals = []
        for i in range(images):
            part = da[i * IMG_PAD : (i + 1) * IMG_PAD, :]
            high = part.astype(BF16)
            rest = (part - high.astype(F32)).astype(BF16)
            vals.append(dot(perm_t[b, i], high) + dot(perm_t[b, i], rest))
        put_rows(acc, vals)
        sums = back_norm(xs.at[b], acc, gains[b, 0:1, :], dx)
        small[GAIN_ROW + 2 * b : GAIN_ROW + 2 * b + 1, :] = sums[0]
        small[BIAS_ROW + 4 * b : BIAS_ROW + 4 * b + 1, :] = sums[1]
        for cp in out_copies:
            cp.wait()
        for t in range(groups - 2, groups):
            att_copy(t, t % 2).wait()
    for i in range(images):
        dx_out[i] = dx[i * TOKENS : (i + 1) * TOKENS, :]


def compute_call(x, ct, live, gathered, rel_add, gains, offs, qvb, hb):
    images, _, width = x.shape
    groups = gathered.shape[1]
    cols = gathered.shape[3]
    lanes = GROUP * HEAD_DIM
    hid = (cols - 4 * lanes) // 2
    rows = -(-images * TOKENS // 16) * 16
    wrows = images * IMG_PAD
    perm = permutations(images)
    consts = (
        jnp.asarray(np.tile(mask_table(), (1, 1, 1, GROUP))),
        jnp.asarray(perm, BF16),
        jnp.asarray(np.swapaxes(perm, 2, 3), BF16),
    )
    vmem = pl.BlockSpec(memory_space=pltpu.VMEM)
    anyspace = pl.BlockSpec(memory_space=pl.ANY)
    small_rows = HID_ROW + BLOCKS * groups
    return pl.pallas_call(
        compute_kernel,
        out_shape=(
            jax.ShapeDtypeStruct(x.shape, F32),
            jax.ShapeDtypeStruct(x.shape, F32),
            jax.ShapeDtypeStruct(gathered.shape, BF16),
            jax.ShapeDtypeStruct((BLOCKS, groups, PAD, GROUP * PAD), F32),
            jax.ShapeDtypeStruct((small_rows, width), F32),
        ),
        in_specs=[
            vmem, vmem, pl.BlockSpec(memory_space=pltpu.SMEM), anyspace, vmem, vmem, vmem, vmem,
            vmem, vmem, vmem, vmem,
        ],
        out_specs=(vmem, vmem, anyspace, vmem, vmem),
        scratch_shapes=[
            pltpu.VMEM((BLOCKS, groups, width, cols), BF16),
            pltpu.VMEM((BLOCKS, rows, width), F32),
            pltpu.VMEM((BLOCKS, rows, width), F32),
            pltpu.VMEM((rows, width), BF16),
            pltpu.VMEM((BLOCKS, wrows, width), BF16),
            pltpu.VMEM((BLOCKS, groups, wrows, 3 * lanes), BF16),
            pltpu.VMEM((BLOCKS, groups, images * WINS, PAD, GROUP * PAD), BF16),
            pltpu.VMEM((wrows, lanes), BF16),
            pltpu.VMEM((BLOCKS, groups, rows, lanes), BF16),
            pltpu.VMEM((BLOCKS, rows, width), BF16),
            pltpu.VMEM((BLOCKS, groups, rows, hid), BF16),
            pltpu.VMEM((BLOCKS, groups, rows, hid), BF16),
            pltpu.VMEM((rows, hid), F32),
            pltpu.VMEM((rows, width), F32),
            pltpu.VMEM((rows, width), F32),
            pltpu.VMEM((rows, width), BF16),
            pltpu.VMEM((width, wrows), BF16),
            pltpu.VMEM((wrows, 3 * lanes), BF16),
            pltpu.VMEM((wrows, width), F32),
            pltpu.VMEM((2, width, 2 * hid), BF16),
            pltpu.VMEM((groups, width, lanes), BF16),
            pltpu.VMEM((2, width, 3 * lanes), BF16),
            pltpu.SemaphoreType.DMA((BLOCKS,)),
            pltpu.SemaphoreType.DMA((2 + groups,)),
            pltpu.SemaphoreType.DMA((2,)),
        ],
        compiler_params=pltpu.CompilerParams(vmem_limit_bytes=63 * MIB),
    )(x, ct, live, gathered, rel_add, consts[0], gains, offs, qvb, hb, consts[1], consts[2])

MESH = pl.DeviceIdType.MESH


class Digit:
    def __init__(self, name, axis, size, stride, dim):
        self.name, self.axis, self.size, self.stride, self.dim = name, axis, size, stride, dim

    def here(self):
        return lax.rem(lax.axis_index(self.axis) // self.stride, self.size)

    def peer(self, step):
        d = self.here()
        to = lax.rem(d + step, self.size)
        return to, {self.axis: lax.axis_index(self.axis) + (to - d) * self.stride}


def plan(n_fsdp, n_tensor):
    if (n_fsdp, n_tensor) == (8, 4):
        parts = [("x", "tensor", 2), ("core", "tensor", 2), ("z", "fsdp", 4), ("y", "fsdp", 2)]
    elif (n_fsdp, n_tensor) == (32, 4):
        parts = [("x", "tensor", 4), ("z", "fsdp", 4), ("y", "fsdp", 4), ("core", "fsdp", 2)]
    else:
        parts = [("x", "tensor", n_tensor), ("z", "fsdp", n_fsdp)]
    digits = {}
    for dim, (name, axis, size) in enumerate(parts):
        stride = 1
        for _, later_axis, later in parts[dim + 1 :]:
            if later_axis == axis:
                stride *= later
        digits[name] = Digit(name, axis, size, stride, dim)
    return digits


def orders(digits):
    one = [n for n in ("z", "x", "y", "core") if n in digits]
    two = [n for n in ("z", "y", "x", "core") if n in digits]
    return [[digits[n] for n in one], [digits[n] for n in two]]


def greet(peers):
    barrier = pltpu.get_barrier_semaphore()
    for device in peers:
        pl.semaphore_signal(barrier, inc=1, device_id=device, device_id_type=MESH)
    pl.semaphore_wait(barrier, len(peers))


def tensor_peers(n_tensor):
    t = lax.axis_index("tensor")
    return [{"tensor": lax.rem(t + s, n_tensor)} for s in range(1, n_tensor)]


def all_peers(digits, n_tensor):
    peers = [d.peer(s)[1] for d in digits.values() if d.axis == "fsdp" for s in range(1, d.size)]
    return peers + tensor_peers(n_tensor)


def pieces(cols, width):
    return [(c, min(width, cols - c)) for c in range(0, cols, width)]


def gather_kernel(n_fsdp, n_tensor, half, own, side, full, sides, local_sem, send, recv, side_send, side_recv):
    digits = plan(n_fsdp, n_tensor)
    dims = sorted(digits.values(), key=lambda d: d.dim)
    greet(all_peers(digits, n_tensor))
    t = lax.axis_index("tensor")
    mine = tuple(d.here() for d in dims)
    local = pltpu.make_async_copy(side, sides.at[t], local_sem.at[0])
    local.start()
    side_copies = []
    for j, device in enumerate(tensor_peers(n_tensor)):
        side_copies.append(pltpu.make_async_remote_copy(
            src_ref=side, dst_ref=sides.at[t], send_sem=side_send.at[j], recv_sem=side_recv.at[j],
            device_id=device, device_id_type=MESH))
    local_own = []
    for b in range(BLOCKS):
        cp = pltpu.make_async_copy(own.at[b], full.at[(b,) + mine], local_sem.at[1 + b])
        cp.start()
        local_own.append(cp)
    jobs = []
    for b in range(BLOCKS):
        for k, (c, n) in enumerate(pieces(own.shape[3 - 1], half)):
            jobs.append((b, c, n, orders(digits)[k % 2]))
    count = [0]
    started = []

    def launch(job, phase):
        b, c, n, order = job
        done = order[:phase]
        digit = order[phase]
        index = tuple(slice(None) if d in done else d.here() for d in dims)
        cols = pl.ds(c, n)
        copies = []
        for s in range(1, digit.size):
            _, device = digit.peer(s)
            dst = full.at[(b,) + index + (slice(None), cols)]
            src = own.at[b, :, cols] if phase == 0 else dst
            i = count[0]
            count[0] += 1
            copies.append(pltpu.make_async_remote_copy(
                src_ref=src, dst_ref=dst, send_sem=send.at[i], recv_sem=recv.at[i],
                device_id=device, device_id_type=MESH))
        for cp in copies:
            cp.start()
        started.extend(copies)
        return copies

    last = {}
    for j, job in enumerate(jobs):
        last[j] = launch(job, 0)
        if j == 1:
            for cp in side_copies:
                cp.start()
    for cp in local_own:
        cp.wait()
    phases = len(digits)
    pairs = len(jobs) // 2
    for step in range(pairs + phases - 1):
        for phase in range(phases - 1, 0, -1):
            pair = step - (phase - 1)
            if 0 <= pair < pairs:
                for j in (2 * pair, 2 * pair + 1):
                    for cp in last[j]:
                        cp.wait_recv()
                    last[j] = launch(jobs[j], phase)
    for j in range(len(jobs)):
        for cp in last[j]:
            cp.wait_recv()
    for cp in started:
        cp.wait_send()
    local.wait()
    for cp in side_copies:
        cp.wait()


def gather_call(own, side, n_fsdp, n_tensor, half=256):
    digits = plan(n_fsdp, n_tensor)
    sizes = tuple(d.size for d in sorted(digits.values(), key=lambda d: d.dim))
    total = sum(d.size - 1 for d in digits.values()) * BLOCKS * len(pieces(own.shape[2], half))
    anyspace = pl.BlockSpec(memory_space=pl.ANY)
    full, sides = pl.pallas_call(
        functools.partial(gather_kernel, n_fsdp, n_tensor, half),
        out_shape=(
            jax.ShapeDtypeStruct((BLOCKS,) + sizes + own.shape[1:], own.dtype),
            jax.ShapeDtypeStruct((n_tensor,) + side.shape, side.dtype),
        ),
        in_specs=[anyspace, anyspace],
        out_specs=(anyspace, anyspace),
        scratch_shapes=[
            pltpu.SemaphoreType.DMA((1 + BLOCKS,)),
            pltpu.SemaphoreType.DMA((total,)),
            pltpu.SemaphoreType.DMA((total,)),
            pltpu.SemaphoreType.DMA((n_tensor - 1,)),
            pltpu.SemaphoreType.DMA((n_tensor - 1,)),
        ],
        compiler_params=pltpu.CompilerParams(collective_id=0, has_side_effects=True),
    )(own, side)
    return full.reshape(BLOCKS, n_tensor, n_fsdp * own.shape[1], own.shape[2]), sides


def adam(weight, first, second, grad, rate, decay):
    first_new = BETA_ONE * first + (1.0 - BETA_ONE) * grad
    second_new = BETA_TWO * second + (1.0 - BETA_TWO) * grad * grad
    first_hat = first_new * (1.0 / (1.0 - BETA_ONE**ADAM_STEP))
    second_hat = second_new * (1.0 / (1.0 - BETA_TWO**ADAM_STEP))
    step = first_hat / (jnp.sqrt(second_hat) + ADAM_EPS)
    if decay:
        step = step + decay * weight
    return weight - rate * step, first_new, second_new


def pick(index, values):
    out = values[0]
    for i in range(1, len(values)):
        out = jnp.where(index == i, values[i], out)
    return out


def rel_row(groups):
    return HID_ROW + BLOCKS * groups


def reduce_jobs(digits, cols, half):
    jobs = []
    for b in range(BLOCKS - 1, -1, -1):
        for k, (c, n) in reversed(list(enumerate(pieces(cols, half)))):
            jobs.append((b, c, n, orders(digits)[k % 2][::-1], k % 2))
    return jobs


def stage_shapes(digits, rows, half, count):
    dims = sorted(digits.values(), key=lambda d: d.dim)
    shapes = []
    for order in orders(digits):
        order = order[::-1]
        for phase, digit in enumerate(order):
            left = tuple(d.size for d in dims if d not in order[: phase + 1])
            slots = digit.size if phase == len(order) - 1 else digit.size - 1
            shapes.append((-(-count // 2), slots) + left + (rows, half))
    return shapes


def reduce_kernel(n_fsdp, n_tensor, half, *refs):
    digits = plan(n_fsdp, n_tensor)
    dims = sorted(digits.values(), key=lambda d: d.dim)
    grads, small = refs[0], refs[1]
    params = [refs[2 + 3 * j : 5 + 3 * j] for j in range(9)]
    outs = [refs[29 + 3 * j : 32 + 3 * j] for j in range(9)]
    acc, local_sem, send, recv = refs[56:60]
    phases = len(digits)
    stage = [refs[60 + j * phases : 60 + (j + 1) * phases] for j in range(2)]
    small_slots = refs[60 + 2 * phases : 60 + 3 * phases]
    total = refs[60 + 3 * phases]
    rows = acc.shape[-2]
    lanes = GROUP * HEAD_DIM
    count = [0]
    started = []

    def remote(src, dst, device):
        i = count[0]
        count[0] += 1
        cp = pltpu.make_async_remote_copy(
            src_ref=src, dst_ref=dst, send_sem=send.at[i], recv_sem=recv.at[i],
            device_id=device, device_id_type=MESH)
        started.append(cp)
        return cp

    jobs = reduce_jobs(digits, acc.shape[-1], half)
    core = jobs[0][3][0]
    local = []
    for b in range(BLOCKS):
        index = tuple(core.here() if d is core else slice(None) for d in dims)
        cp = pltpu.make_async_copy(grads.at[(b,) + index], acc.at[b], local_sem.at[b])
        cp.start()
        local.append(cp)
    greet(all_peers(digits, n_tensor))
    reduced = [d for d in dims if d is not core]

    def launch(j, phase):
        b, c, n, order, kind = jobs[j]
        digit = order[phase]
        cols = pl.ds(c, n)
        copies = []
        for s in range(1, digit.size):
            to, device = digit.peer(s)
            if phase == 0:
                index = tuple(to if d is digit else slice(None) for d in dims)
                src = grads.at[(b,) + index + (slice(None), cols)]
            else:
                index = tuple(
                    to if d is digit else d.here() if d in order[:phase] else slice(None)
                    for d in reduced
                )
                src = acc.at[(b,) + index + (slice(None), cols)]
            slot = digit.here() if phase == phases - 1 else s - 1
            dst = stage[kind][phase].at[j // 2, slot]
            copies.append(remote(src, dst, device))
        for cp in copies:
            cp.start()
        return copies

    def absorb(j, phase):
        b, c, n, order, kind = jobs[j]
        digit = order[phase]
        cols = pl.ds(c, n)
        left = [d for d in reduced if d not in order[: phase + 1]]
        land = stage[kind][phase]
        steps = int(np.prod([d.size for d in left])) if left else 1

        def one(i, carry):
            place = {}
            rest = i
            for d in reversed(left):
                place[d.name] = lax.rem(rest, d.size)
                rest = rest // d.size
            index = (b,) + tuple(place[d.name] if d in left else d.here() for d in reduced)
            value = acc[index + (slice(None), cols)]
            for s in range(digit.size - 1):
                value = value + land[(j // 2, s) + tuple(place[d.name] for d in left)]
            acc[index + (slice(None), cols)] = value
            return carry

        lax.fori_loop(0, steps, one, 0)

    def finish(j):
        b, c, n, order, way = jobs[j]
        digit = order[-1]
        index = (b,) + tuple(d.here() for d in reduced)
        land = stage[way][phases - 1]
        land[j // 2, digit.here()] = acc[index + (slice(None), pl.ds(c, n))]
        grad = land[j // 2, 0].astype(F32)
        for s in range(1, digit.size):
            grad = grad + land[j // 2, s].astype(F32)
        for u in range(0, n, lanes):
            unit = (c + u) // lanes
            part = grad[:, u : u + lanes]
            if unit < 3:
                kind, place = 0, (b, slice(None), unit)
            elif unit == 3:
                kind, place, part = 1, (b,), jnp.transpose(part)
            else:
                hid = params[2][0].shape[2]
                at = c + u - 4 * lanes
                if at < hid:
                    kind, place = 2, (b, slice(None), slice(at, at + lanes))
                else:
                    kind, place, part = 3, (b, slice(at - hid, at - hid + lanes)), jnp.transpose(part)
            new = adam(*(p[place] for p in params[kind]), part, MATRIX_RATE, WEIGHT_DECAY)
            for ref, val in zip(outs[kind], new):
                ref[place] = val

    small_order = [digits[n] for n in ("core", "y", "x", "z") if n in digits]

    def small_launch(phase):
        digit = small_order[phase]
        copies = []
        for s in range(1, digit.size):
            _, device = digit.peer(s)
            place = small_slots[phase].at[digit.here()]
            copies.append(remote(place, place, device))
        for cp in copies:
            cp.start()
        return copies

    small_slots[0][small_order[0].here()] = small[...]
    last = {}
    last["small"] = small_launch(0)
    for j in range(len(jobs)):
        last[j] = launch(j, 0)
    for cp in local:
        cp.wait()
    pairs = len(jobs) // 2
    for step in range(pairs + phases - 1):
        if 0 < step <= phases:
            for cp in last["small"]:
                cp.wait_recv()
            digit = small_order[step - 1]
            value = small_slots[step - 1][0]
            for s in range(1, digit.size):
                value = value + small_slots[step - 1][s]
            if step < phases:
                small_slots[step][small_order[step].here()] = value
                last["small"] = small_launch(step)
            else:
                total[...] = value
        for phase in range(phases - 1, -1, -1):
            pair = step - phase
            if 0 <= pair < pairs:
                for j in (2 * pair, 2 * pair + 1):
                    for cp in last[j]:
                        cp.wait_recv()
                    if phase < phases - 1:
                        absorb(j, phase)
                        last[j] = launch(j, phase + 1)
                    else:
                        finish(j)
    t = lax.axis_index("tensor")
    groups = n_tensor
    width = total.shape[1]
    for b in range(BLOCKS):
        heads = params[4][0].shape[1]
        rels = params[4][0].shape[2]
        at = rel_row(groups) + b * heads * groups
        hid_at = HID_ROW + b * groups
        work = [
            (4, (b,), pick(t, [total[at + i * heads : at + (i + 1) * heads, 0:rels] for i in range(groups)])),
            (5, (b,), total[QV_ROW + 2 * b : QV_ROW + 2 * b + 2, pl.ds(pl.multiple_of(t * lanes, lanes), lanes)]),
            (6, (slice(b, b + 1),), pick(t, [total[hid_at + i : hid_at + i + 1, :] for i in range(groups)])),
            (7, (b,), total[GAIN_ROW + 2 * b : GAIN_ROW + 2 * b + 2, :]),
            (8, (b,), total[BIAS_ROW + 4 * b : BIAS_ROW + 4 * b + 4, :]),
        ]
        for kind, place, grad in work:
            new = adam(*(p[place] for p in params[kind]), grad, SMALL_RATE, 0.0)
            for ref, val in zip(outs[kind], new):
                ref[place] = val
    for cp in started:
        cp.wait_send()


def reduce_call(grads, small, params, n_fsdp, n_tensor, half=256):
    digits = plan(n_fsdp, n_tensor)
    dims = sorted(digits.values(), key=lambda d: d.dim)
    sizes = tuple(d.size for d in dims)
    rows = grads.shape[2] // n_fsdp
    cols = grads.shape[3]
    grads = grads.reshape((BLOCKS,) + sizes + (rows, cols))
    count = len(reduce_jobs(digits, cols, half))
    total = sum(d.size - 1 for d in digits.values()) * (count + 1)
    small_order = [digits[n] for n in ("core", "y", "x", "z") if n in digits]
    core = orders(digits)[0][-1]
    acc_shape = (BLOCKS,) + tuple(d.size for d in dims if d is not core) + (rows, cols)
    vmem = pl.BlockSpec(memory_space=pltpu.VMEM)
    flat = [p for group in params for p in group]
    return pl.pallas_call(
        functools.partial(reduce_kernel, n_fsdp, n_tensor, half),
        out_shape=tuple(jax.ShapeDtypeStruct(p.shape, p.dtype) for p in flat),
        in_specs=[pl.BlockSpec(memory_space=pl.ANY)] + [vmem] * (1 + len(flat)),
        out_specs=tuple(vmem for _ in flat),
        scratch_shapes=[
            pltpu.VMEM(acc_shape, BF16),
            pltpu.SemaphoreType.DMA((BLOCKS,)),
            pltpu.SemaphoreType.DMA((total,)),
            pltpu.SemaphoreType.DMA((total,)),
        ]
        + [pltpu.VMEM(s, BF16) for s in stage_shapes(digits, rows, half, count)]
        + [pltpu.VMEM((d.size,) + small.shape, F32) for d in small_order]
        + [pltpu.VMEM(small.shape, F32)],
        compiler_params=pltpu.CompilerParams(
            collective_id=1, has_side_effects=True, vmem_limit_bytes=60 * MIB
        ),
    )(grads, small, *flat)


def shards(n_fsdp, n_tensor, *args):
    image_rows, cotangent, live_counts = args[:3]
    qkv, out, up, down, rel, qv, hidden, gain, bias = [args[3 + 3 * j : 6 + 3 * j] for j in range(9)]
    images = image_rows.shape[0]
    slots = lax.axis_index("tensor") * images + jnp.arange(images, dtype=jnp.int32)
    live = (slots < live_counts[0]).astype(F32)
    own = jnp.concatenate(
        [
            qkv[0].reshape(BLOCKS, qkv[0].shape[1], -1).astype(BF16),
            jnp.swapaxes(out[0], 1, 2).astype(BF16),
            up[0].astype(BF16),
            jnp.swapaxes(down[0], 1, 2).astype(BF16),
        ],
        2,
    )
    heads, rels = rel[0].shape[1:]
    onehot = jnp.asarray(rel_onehot(rels).reshape(rels, -1), BF16)
    rel_own = lax.dot_general(
        rel[0].astype(BF16), onehot, (((2,), (0,)), ((), ())), preferred_element_type=F32
    )
    rel_own = rel_own.reshape(BLOCKS, heads, PAD, PAD).swapaxes(1, 2).reshape(BLOCKS * PAD, heads * PAD)
    hid = hidden[0].shape[1]
    tail = jnp.concatenate(
        [jnp.pad(qv[0].reshape(2 * BLOCKS, -1), ((0, 0), (0, hid - qv[0].shape[2]))), hidden[0],
         jnp.zeros((8 - 3 * BLOCKS, hid), F32)], 0)
    side = jnp.concatenate([jnp.pad(rel_own, ((0, 0), (0, hid - rel_own.shape[1]))), tail], 0)
    full, sides = gather_call(own, side, n_fsdp, n_tensor)
    rel_add = sides[:, : BLOCKS * PAD, : heads * PAD].reshape(n_tensor, BLOCKS, PAD, heads * PAD)
    rel_add = rel_add.swapaxes(0, 1)
    tail = sides[:, BLOCKS * PAD :]
    qvb = tail[:, : 2 * BLOCKS, : qv[0].shape[2]].reshape(n_tensor, BLOCKS, 2, -1).transpose(1, 2, 0, 3)
    hb = tail[:, 2 * BLOCKS : 3 * BLOCKS].swapaxes(0, 1)
    x_out, dx_out, grads, dsum, small = compute_call(
        image_rows, cotangent, live, full, rel_add, gain[0], bias[0], qvb, hb
    )
    table = dsum.reshape(BLOCKS, n_tensor, PAD, heads, PAD).transpose(0, 1, 3, 2, 4)
    table = jnp.dot(
        table.reshape(BLOCKS * n_tensor * heads, PAD * PAD),
        jnp.asarray(rel_onehot(rels).reshape(rels, -1).T),
        precision=lax.Precision.HIGHEST,
    )
    small = jnp.concatenate([small, jnp.pad(table, ((0, 0), (0, small.shape[1] - rels)))], 0)
    new = reduce_call(grads, small, (qkv, out, up, down, rel, qv, hidden, gain, bias), n_fsdp, n_tensor)
    return (x_out, dx_out) + tuple(new)


def solution(mesh):
    n_fsdp, n_tensor = mesh.shape["fsdp"], mesh.shape["tensor"]
    tokens = P(("fsdp", "tensor"), None, None)
    kinds = (
        P(None, "fsdp", None, "tensor"), P(None, "tensor", "fsdp"), P(None, "fsdp", "tensor"),
        P(None, "tensor", "fsdp"), P(None, "tensor", None), P(None, None, "tensor"),
        P(None, "tensor"), P(), P(),
    )
    thrice = tuple(k for k in kinds for _ in range(3))
    return jax.shard_map(
        functools.partial(shards, n_fsdp, n_tensor),
        mesh=mesh,
        in_specs=(tokens, tokens, P("fsdp")) + thrice,
        out_specs=(tokens, tokens) + thrice,
        check_vma=False,
    )
```

```python
import functools
import numpy as np
import jax
import jax.numpy as jnp
from jax import lax
from jax.experimental import pallas as pl
from jax.experimental.pallas import tpu as pltpu
from jax.sharding import PartitionSpec as P
HEAD_DIM = 32
SIDE = 14
WIN = 7
SHIFT = 3
BLOCKS = 2
ADAM_STEP = 10
TOKENS = SIDE * SIDE
WINS = (SIDE // WIN) ** 2
SPAN = WIN * WIN
PAD = 64
IMG_PAD = WINS * PAD
IMG_ROWS = 208
GROUP = 4
NORM_EPS = 1e-05
BETA_ONE = 0.9
BETA_TWO = 0.999
MATRIX_RATE = 0.04
SMALL_RATE = 0.3
WEIGHT_DECAY = 0.05
ADAM_EPS = 1e-08
MASK_FILL = -100.0
KEY_FILL = -1e30
INV_ROOT = HEAD_DIM ** (-0.5)
MIB = 1024 * 1024
F32 = jnp.float32
BF16 = jnp.bfloat16
NT = (((1,), (1,)), ((), ()))
TN = (((0,), (0,)), ((), ()))


def window_source(shifted):
    out = np.zeros((WINS, SPAN), np.int64)
    step = SHIFT if shifted else 0
    per = SIDE // WIN
    for w in range(WINS):
        for p in range(SPAN):
            r = (w // per) * WIN + p // WIN
            c = (w % per) * WIN + p % WIN
            out[w, p] = ((r + step) % SIDE) * SIDE + (c + step) % SIDE
    return out


def image_base(i):
    return (i * TOKENS) // 16 * 16


def permutations(images):
    perm = np.zeros((BLOCKS, images, IMG_PAD, IMG_ROWS), np.float32)
    for b in range(BLOCKS):
        src = window_source(b % 2 == 1)
        for i in range(images):
            off = i * TOKENS - image_base(i)
            for w in range(WINS):
                for p in range(SPAN):
                    perm[b, i, w * PAD + p, off + src[w, p]] = 1.0
    return perm


def mask_table():
    out = np.zeros((BLOCKS, WINS, PAD, PAD), np.float32)
    coords = np.arange(SIDE)
    bands = (coords >= SIDE - WIN).astype(int) + (coords >= SIDE - SHIFT).astype(int)
    region = (bands[:, None] * 3 + bands[None, :]).reshape(-1)
    base = window_source(False)
    for b in range(BLOCKS):
        for w in range(WINS):
            if b % 2 == 1:
                lab = region[base[w]]
                out[b, w, :SPAN, :SPAN] = np.where(lab[:, None] == lab[None, :], 0.0, MASK_FILL)
            out[b, w, SPAN:, :] = KEY_FILL
    return out


def rel_onehot(rels):
    out = np.zeros((rels, PAD, PAD), np.float32)
    pos = np.arange(SPAN)
    row, col = pos // WIN, pos % WIN
    for q in range(SPAN):
        e = (row[q] - row + WIN - 1) * (2 * WIN - 1) + col[q] - col + WIN - 1
        out[e, np.arange(SPAN), q] = 1.0
    return out


def dot(a, b, dims=None):
    if dims is None:
        return jnp.dot(a, b, preferred_element_type=F32)
    return lax.dot_general(a, b, dims, preferred_element_type=F32)


def lane_heads(width):
    return lax.broadcasted_iota(jnp.int32, (1, width), 1) // HEAD_DIM


def spread(rows, heads):
    zero = jnp.zeros_like(rows)
    return jnp.concatenate([jnp.where(heads == h, rows, zero) for h in range(GROUP)], 0)


def gather_diag(prod, heads):
    out = prod[0:PAD]
    for h in range(1, GROUP):
        out = jnp.where(heads == h, prod[h * PAD : (h + 1) * PAD], out)
    return out


def gelu_pair(u):
    au = jnp.abs(u)
    t = 1.0 / (1.0 + (0.3275911 * 0.7071067811865476) * au)
    e = jnp.exp(-0.5 * u * u)
    q = 1.061405429 * 0.5
    q = q * t - 1.453152027 * 0.5
    q = q * t + 1.421413741 * 0.5
    q = q * t - 0.284496736 * 0.5
    q = q * t + 0.254829592 * 0.5
    q = q * t * e
    phi = jnp.where(u >= 0, 1.0 - q, q)
    return u * phi, phi + u * e * 0.3989422804014327


def chunks(rows, size):
    return [(r, min(size, rows - r)) for r in range(0, rows, size)]


def norm_rows(x):
    mean = jnp.mean(x, -1, keepdims=True)
    cen = x - mean
    inv = lax.rsqrt(jnp.mean(cen * cen, -1, keepdims=True) + NORM_EPS)
    return cen * inv, inv


def put_rows(ref, vals):
    images = len(vals)
    for i in range(images):
        base = image_base(i)
        lead = 0
        if i > 0:
            lead = image_base(i - 1) + IMG_ROWS - base
            mix = vals[i - 1][IMG_ROWS - lead :] + vals[i][:lead]
            ref[base : base + lead, :] = mix.astype(ref.dtype)
        end = image_base(i + 1) - base if i + 1 < images else IMG_ROWS
        ref[base + lead : base + end, :] = vals[i][lead:end].astype(ref.dtype)


def norm_into(src, dst, gain, off):
    for r, n in chunks(src.shape[0], 112):
        unit, _ = norm_rows(src[r : r + n, :])
        dst[r : r + n, :] = (unit * gain + off).astype(BF16)


def fold(val):
    rows, cols = val.shape
    return jnp.sum(val.reshape(rows // 8, 8, cols), 0)


def back_norm(src, grad, gain, dst):
    width = src.shape[1]
    sums = [jnp.zeros((8, width), F32) for _ in range(3)]
    for r, n in chunks(src.shape[0], 112):
        unit, inv = norm_rows(src[r : r + n, :])
        gr = grad[r : r + n, :]
        e = gr * gain
        res = dst[r : r + n, :] + inv * (
            e - jnp.mean(e, -1, keepdims=True) - unit * jnp.mean(e * unit, -1, keepdims=True)
        )
        dst[r : r + n, :] = res
        for j, val in enumerate((gr * unit, gr, res)):
            sums[j] = sums[j] + fold(val)
    return [jnp.sum(s, 0, keepdims=True) for s in sums]


def column_sum(ref):
    total = jnp.zeros((8, ref.shape[1]), F32)
    for r, n in chunks(ref.shape[0], 112):
        total = total + fold(ref[r : r + n, :])
    return jnp.sum(total, 0, keepdims=True)
GAIN_ROW = 0
BIAS_ROW = GAIN_ROW + 2 * BLOCKS
QV_ROW = BIAS_ROW + 4 * BLOCKS
HID_ROW = QV_ROW + 2 * BLOCKS
MESH = pl.DeviceIdType.MESH


class Digit:
    def __init__(self, name, axis, size, stride, dim):
        self.name, self.axis, self.size, self.stride, self.dim = name, axis, size, stride, dim

    def here(self):
        return lax.rem(lax.axis_index(self.axis) // self.stride, self.size)

    def peer(self, step):
        d = self.here()
        to = lax.rem(d + step, self.size)
        return to, {self.axis: lax.axis_index(self.axis) + (to - d) * self.stride}


def plan(n_fsdp, n_tensor):
    if (n_fsdp, n_tensor) == (8, 4):
        parts = [("x", "tensor", 2), ("core", "tensor", 2), ("z", "fsdp", 4), ("y", "fsdp", 2)]
    elif (n_fsdp, n_tensor) == (32, 4):
        parts = [("x", "tensor", 4), ("z", "fsdp", 4), ("y", "fsdp", 4), ("core", "fsdp", 2)]
    else:
        parts = [("x", "tensor", n_tensor), ("z", "fsdp", n_fsdp)]
    digits = {}
    for dim, (name, axis, size) in enumerate(parts):
        stride = 1
        for _, later_axis, later in parts[dim + 1 :]:
            if later_axis == axis:
                stride *= later
        digits[name] = Digit(name, axis, size, stride, dim)
    return digits


def orders(digits):
    one = [n for n in ("z", "x", "y", "core") if n in digits]
    two = [n for n in ("z", "y", "x", "core") if n in digits]
    return [[digits[n] for n in one], [digits[n] for n in two]]


def greet(peers):
    barrier = pltpu.get_barrier_semaphore()
    for device in peers:
        pl.semaphore_signal(barrier, inc=1, device_id=device, device_id_type=MESH)
    pl.semaphore_wait(barrier, len(peers))


def tensor_peers(n_tensor):
    t = lax.axis_index("tensor")
    return [{"tensor": lax.rem(t + s, n_tensor)} for s in range(1, n_tensor)]


def all_peers(digits, n_tensor):
    peers = [d.peer(s)[1] for d in digits.values() if d.axis == "fsdp" for s in range(1, d.size)]
    return peers + tensor_peers(n_tensor)


def pieces(cols, width):
    return [(c, min(width, cols - c)) for c in range(0, cols, width)]


def adam(weight, first, second, grad, rate, decay):
    first_new = BETA_ONE * first + (1.0 - BETA_ONE) * grad
    second_new = BETA_TWO * second + (1.0 - BETA_TWO) * grad * grad
    first_hat = first_new * (1.0 / (1.0 - BETA_ONE**ADAM_STEP))
    second_hat = second_new * (1.0 / (1.0 - BETA_TWO**ADAM_STEP))
    step = first_hat / (jnp.sqrt(second_hat) + ADAM_EPS)
    if decay:
        step = step + decay * weight
    return weight - rate * step, first_new, second_new


def pick(index, values):
    out = values[0]
    for i in range(1, len(values)):
        out = jnp.where(index == i, values[i], out)
    return out


def rel_row(groups):
    return HID_ROW + BLOCKS * groups


def solution(mesh):
    n_fsdp, n_tensor = mesh.shape["fsdp"], mesh.shape["tensor"]
    tokens = P(("fsdp", "tensor"), None, None)
    kinds = (
        P(None, "fsdp", None, "tensor"), P(None, "tensor", "fsdp"), P(None, "fsdp", "tensor"),
        P(None, "tensor", "fsdp"), P(None, "tensor", None), P(None, None, "tensor"),
        P(None, "tensor"), P(), P(),
    )
    thrice = tuple(k for k in kinds for _ in range(3))
    return jax.shard_map(
        functools.partial(shards, n_fsdp, n_tensor),
        mesh=mesh,
        in_specs=(tokens, tokens, P("fsdp")) + thrice,
        out_specs=(tokens, tokens) + thrice,
        check_vma=False,
    )
PART = 512
HALF = 256
REL_LANES = 256


def rel_consts():
    side = 2 * WIN - 1
    top = side * (WIN - 1) + WIN - 1
    down = np.zeros((96, PAD), np.float32)
    across = np.zeros((GROUP * PAD, GROUP * REL_LANES), np.float32)
    for i in range(SPAN):
        place = side * (i // WIN) + i % WIN
        down[top - place, i] = 1.0
        for h in range(GROUP):
            across[h * PAD + i, h * REL_LANES + place] = 1.0
    return down, across


def block_kernel(
    n_fsdp, n_tensor,
    x_hbm, ct_hbm, live, own, rel, side, mask, gains, offs, perm, perm_t, rel_down, rel_across,
    xo_hbm, dxo_hbm, gsum, total, keep_gl, keep_gp, keep_qkv, keep_pts,
    wt, dgr, rels, sides, io, xs, ms, aw, qkv, pts, ow, osb, a2, gl, gp, ubuf, acc, dx, cut, awt, dwin, dsum, small,
    *rest,
):
    digits = plan(n_fsdp, n_tensor)
    dims = sorted(digits.values(), key=lambda d: d.dim)
    ways = orders(digits)
    backs = [w[::-1] for w in ways]
    phases = len(dims)
    stage = [rest[j * phases : (j + 1) * phases] for j in range(2)]
    small_slots = rest[2 * phases : 3 * phases]
    (io_sem, own_sem, keep_sem, rel_send, rel_recv, side_send, side_recv, ag_send, ag_recv, rs_send, rs_recv,
     sm_send, sm_recv) = rest[3 * phases :]
    images = io.shape[0]
    groups = n_tensor
    rows, width = xs.shape[1:]
    lanes = GROUP * HEAD_DIM
    hid = gl.shape[2]
    cols = wt.shape[-1]
    parts = cols // PART
    c_out, c_up, c_down = 3 * lanes, 4 * lanes, 4 * lanes + hid
    heads = lane_heads(lanes)
    tdims = [d for d in dims if d.axis == "tensor"]
    fdims = [d for d in dims if d.axis == "fsdp"]
    per = wt.shape[-2]
    fshape = tuple(d.size for d in fdims) + (per,)
    t_here = lax.axis_index("tensor")

    def tplace(t):
        return tuple(lax.rem(t // d.stride, d.size) for d in tdims)

    def weight(b, t, lo, hi):
        index = (b,) + tplace(t) + (slice(None),) * len(fshape) + (slice(lo, hi),)
        return wt[index].reshape(width, hi - lo)

    def grad_ref(b):
        return dgr if b == BLOCKS - 1 else wt.at[BLOCKS - 1]

    def put_grad(b, t, lo, hi, value):
        index = tplace(t) + (slice(None),) * len(fshape) + (slice(lo, hi),)
        grad_ref(b)[index] = value.astype(BF16).reshape(fshape + (hi - lo,))

    def ag_copies(p, phase):
        b, c = p // parts, (p % parts) * PART
        out = []
        for h in range(2):
            order = ways[h]
            digit = order[phase]
            at = pl.ds(c + h * HALF, HALF)
            index = tuple(slice(None) if d in order[:phase] else d.here() for d in dims)
            dst = wt.at[(b,) + index + (slice(None), at)]
            src = own.at[b, :, at] if phase == 0 else dst
            for s in range(1, digit.size):
                sem = (p, h, phase, s - 1)
                out.append(pltpu.make_async_remote_copy(
                    src_ref=src, dst_ref=dst, send_sem=ag_send.at[sem], recv_sem=ag_recv.at[sem],
                    device_id=digit.peer(s)[1], device_id_type=MESH))
        return out

    def start(copies):
        for cp in copies:
            cp.start()

    def arrive(copies):
        for cp in copies:
            cp.wait_recv()

    def sent(copies):
        for cp in copies:
            cp.wait_send()

    pairs = BLOCKS * parts

    def ag_step(p, phase):
        if 0 <= p < pairs:
            arrive(ag_copies(p, phase - 1))
            start(ag_copies(p, phase))

    def pump(i):
        ag_step(i + 2, 1)
        ag_step(i + 1, 2)
        ag_step(i, 3)

    def need(p):
        arrive(ag_copies(p, phases - 1))

    def rs_copies(b, part, phase):
        out = []
        for h in range(2):
            order = backs[h]
            digit = order[phase]
            at = pl.ds(part * PART + h * HALF, HALF)
            for s in range(1, digit.size):
                to, device = digit.peer(s)
                index = tuple(
                    to if d is digit else d.here() if d in order[:phase] else slice(None) for d in dims
                )
                sem = (b, part, h, phase, s - 1)
                out.append(pltpu.make_async_remote_copy(
                    src_ref=grad_ref(b).at[index + (slice(None), at)],
                    dst_ref=stage[h][phase].at[b, part, s - 1],
                    send_sem=rs_send.at[sem], recv_sem=rs_recv.at[sem],
                    device_id=device, device_id_type=MESH))
        return out

    def rs_absorb(b, part, phase):
        grad = grad_ref(b)
        for h in range(2):
            order = backs[h]
            digit = order[phase]
            at = slice(part * PART + h * HALF, part * PART + (h + 1) * HALF)
            left = [d for d in dims if d not in order[: phase + 1]]
            land = stage[h][phase]
            steps = int(np.prod([d.size for d in left]))

            def one(i, carry):
                place = {}
                more = i
                for d in reversed(left):
                    place[d.name] = lax.rem(more, d.size)
                    more = more // d.size
                index = tuple(place[d.name] if d in left else d.here() for d in dims)
                value = grad[index + (slice(None), at)]
                for s in range(digit.size - 1):
                    value = value + land[(b, part, s) + tuple(place[d.name] for d in left)]
                grad[index + (slice(None), at)] = value
                return carry

            lax.fori_loop(0, steps, one, 0)

    def rs_step(b, part, phase):
        arrive(rs_copies(b, part, phase - 1))
        rs_absorb(b, part, phase - 1)
        start(rs_copies(b, part, phase))

    def rs_finish(b, part):
        arrive(rs_copies(b, part, phases - 1))
        for h in range(2):
            digit = backs[h][-1]
            at = slice(part * PART + h * HALF, part * PART + (h + 1) * HALF)
            index = tuple(d.here() for d in dims)
            value = grad_ref(b)[index + (slice(None), at)].astype(F32)
            for s in range(digit.size - 1):
                value = value + stage[h][phases - 1][b, part, s].astype(F32)
            gsum[b, :, at] = value

    small_order = [digits[n] for n in ("core", "y", "x", "z")]

    def small_copies(phase):
        digit = small_order[phase]
        place = small_slots[phase].at[digit.here()]
        return [
            pltpu.make_async_remote_copy(
                src_ref=place, dst_ref=place, send_sem=sm_send.at[phase, s - 1],
                recv_sem=sm_recv.at[phase, s - 1], device_id=digit.peer(s)[1], device_id_type=MESH)
            for s in range(1, digit.size)
        ]

    def small_step(phase):
        if phase == 0:
            value = small[...]
        else:
            arrive(small_copies(phase - 1))
            value = small_slots[phase - 1][0]
            for s in range(1, small_order[phase - 1].size):
                value = value + small_slots[phase - 1][s]
        if phase < phases:
            small_slots[phase][small_order[phase].here()] = value
            start(small_copies(phase))
        else:
            total[...] = value

    loads = [
        pltpu.make_async_copy(x_hbm, io, io_sem.at[0]),
        pltpu.make_async_copy(ct_hbm, io, io_sem.at[1]),
    ]
    loads[0].start()
    mine = tuple(d.here() for d in dims)
    own_copies = [
        pltpu.make_async_copy(own.at[b], wt.at[(b,) + mine], own_sem.at[b]) for b in range(BLOCKS)
    ]
    own_copies.append(pltpu.make_async_copy(side, sides.at[t_here], own_sem.at[BLOCKS]))
    own_copies.append(pltpu.make_async_copy(rel, rels.at[t_here], own_sem.at[BLOCKS + 1]))
    start(own_copies)
    greet(all_peers(digits, n_tensor))
    side_copies = [
        pltpu.make_async_remote_copy(
            src_ref=src, dst_ref=dst.at[t_here], send_sem=ssem.at[j], recv_sem=rsem.at[j],
            device_id=device, device_id_type=MESH)
        for src, dst, ssem, rsem in (
            (rel, rels, rel_send, rel_recv), (side, sides, side_send, side_recv)
        )
        for j, device in enumerate(tensor_peers(n_tensor))
    ]
    start(ag_copies(0, 0))
    start(side_copies)
    for p in range(1, pairs):
        start(ag_copies(p, 0))

    used = images * TOKENS
    floor = used // 8 * 8
    loads[0].wait()
    xs[0, floor:rows, :] = jnp.zeros((rows - floor, width), F32)
    for i in range(images):
        xs[0, i * TOKENS : (i + 1) * TOKENS, :] = io[i]
    loads[1].start()

    def first_norm(b):
        norm_into(xs.at[b], cut, gains[b, 0:1, :], offs[b, 0:1, :])
        for i in range(images):
            base = image_base(i)
            aw[b, i * IMG_PAD : (i + 1) * IMG_PAD, :] = dot(
                perm[b, i], cut[base : base + IMG_ROWS, :]
            ).astype(BF16)

    first_norm(0)
    loads[1].wait()
    dx[floor:rows, :] = jnp.zeros((rows - floor, width), F32)
    for i in range(images):
        dx[i * TOKENS : (i + 1) * TOKENS, :] = io[i] * live[i]
    for cp in own_copies:
        cp.wait()
    ag_step(0, 1)
    ag_step(1, 1)
    ag_step(0, 2)
    pump(0)
    for cp in side_copies:
        cp.wait()

    def hooks(t, table):
        for at, calls in table.items():

            @pl.when(t == at)
            def _():
                for call in calls:
                    call()

    fwd_hooks = {
        (0, "attend"): {1: [lambda: pump(1)], 3: [lambda: pump(2)]},
        (0, "mlp"): {2: [lambda: pump(3)]},
        (1, "attend"): {1: [lambda: pump(4)], 3: [lambda: pump(5)]},
    }

    att_keeps = [
        pltpu.make_async_copy(qkv, keep_qkv, keep_sem.at[0]),
        pltpu.make_async_copy(pts, keep_pts, keep_sem.at[1]),
    ]
    mlp_keeps = [
        pltpu.make_async_copy(gl, keep_gl, keep_sem.at[2]),
        pltpu.make_async_copy(gp, keep_gp, keep_sem.at[3]),
    ]
    bias_at = 0
    for b in range(BLOCKS):
        off2, off3 = (offs[b, j : j + 1, :].astype(BF16).astype(F32) for j in (2, 3))
        if b > 0:
            first_norm(b)
            for cp in att_keeps:
                cp.wait()
        need(b * parts)

        def attend(t, carry):
            hooks(t, fwd_hooks.get((b, "attend"), {}))
            rows_qkv = dot(aw[b], weight(b, t, 0, c_out))
            for j in range(3):
                part = rows_qkv[:, j * lanes : (j + 1) * lanes]
                if j != 1:
                    at = bias_at + 2 * b + j // 2
                    part = part + sides[t, at : at + 1, 0:lanes].astype(BF16).astype(F32)
                qkv[t, :, j * lanes : (j + 1) * lanes] = part.astype(BF16)

            def window(w, c2):
                r = pl.multiple_of(w * PAD, PAD)
                q = qkv[t, pl.ds(r, PAD), 0:lanes]
                k = qkv[t, pl.ds(r, PAD), lanes : 2 * lanes]
                v = qkv[t, pl.ds(r, PAD), 2 * lanes : 3 * lanes]
                s = dot(k, spread(q, heads), NT) * INV_ROOT
                s = s + rels[t, b].astype(F32)
                s = s + mask[b, lax.rem(w, WINS)].astype(F32)
                e = jnp.exp(s - jnp.max(s, 0, keepdims=True))
                p = (e * (1.0 / jnp.sum(e, 0, keepdims=True))).astype(BF16)
                pts[t, w] = p
                ow[pl.ds(r, PAD), :] = gather_diag(dot(p, v, TN), heads).astype(BF16)
                return c2

            lax.fori_loop(0, images * WINS, window, 0, unroll=2)
            put_rows(
                osb.at[b, t],
                [dot(perm_t[b, i], ow[i * IMG_PAD : (i + 1) * IMG_PAD, :]) for i in range(images)],
            )
            return carry

        lax.fori_loop(0, groups, attend, 0)
        if b + 1 < BLOCKS:
            start(att_keeps)
        y = dot(osb[b, 0], weight(b, 0, c_out, c_up), NT)
        for t in range(1, groups):
            y = y + dot(osb[b, t], weight(b, t, c_out, c_up), NT)
        ms[b] = xs[b] + y + off2
        norm_into(ms.at[b], a2.at[b], gains[b, 1:2, :], offs[b, 1:2, :])
        acc[...] = ms[b] + off3
        if b > 0:
            for cp in mlp_keeps:
                cp.wait()
        need(b * parts + 1)
        need(b * parts + 2)

        def mlp(t, carry):
            hooks(t, fwd_hooks.get((b, "mlp"), {}))
            ubuf[0:rows, :] = dot(a2[b], weight(b, t, c_up, c_down))
            at = bias_at + 2 * BLOCKS + b
            hbias = sides[t, at : at + 1, :].astype(BF16).astype(F32)
            for r, n in chunks(rows, 32):
                g, d = gelu_pair(ubuf[r : r + n, :] + hbias)
                gl[t, r : r + n, :] = g.astype(BF16)
                gp[t, r : r + n, :] = d.astype(BF16)
            acc[...] += dot(gl[t], weight(b, t, c_down, cols), NT)
            return carry

        lax.fori_loop(0, groups, mlp, 0)
        if b + 1 < BLOCKS:
            start(mlp_keeps)
            xs[b + 1] = acc[...]
    for i in range(images):
        io[i] = acc[i * TOKENS : (i + 1) * TOKENS, :]
    x_store = pltpu.make_async_copy(io, xo_hbm, io_sem.at[0])
    x_store.start()

    last = BLOCKS - 1
    back_hooks = {
        (1, "attend"): {
            0: [lambda: rs_step(1, 2, 1)],
            1: [lambda: rs_step(1, 1, 1)],
            2: [lambda: rs_step(1, 2, 2)],
            3: [lambda: rs_step(1, 1, 2)],
        },
        (0, "mlp"): {
            0: [lambda: rs_step(1, 0, 1)],
            1: [lambda: rs_step(1, 2, 3)],
            2: [lambda: rs_step(1, 1, 3)],
            3: [lambda: rs_step(1, 0, 2)],
        },
        (0, "attend"): {
            0: [lambda: rs_step(0, 2, 1), lambda: rs_finish(1, 2)],
            1: [lambda: rs_step(0, 1, 1), lambda: rs_finish(1, 1)],
            2: [lambda: rs_step(0, 2, 2), lambda: rs_step(1, 0, 3)],
            3: [lambda: rs_step(0, 1, 2), lambda: rs_finish(1, 0)],
        },
    }
    mlp_loads = [
        pltpu.make_async_copy(keep_gl, gl, keep_sem.at[2]),
        pltpu.make_async_copy(keep_gp, gp, keep_sem.at[3]),
    ]
    att_loads = [
        pltpu.make_async_copy(keep_qkv, qkv, keep_sem.at[0]),
        pltpu.make_async_copy(keep_pts, pts, keep_sem.at[1]),
    ]
    for b in range(BLOCKS - 1, -1, -1):
        bias_row = BIAS_ROW + 4 * b
        small[bias_row + 3 : bias_row + 4, :] = column_sum(dx)
        cut[...] = dx[...].astype(BF16)
        dxt = jnp.transpose(cut[...])
        a_t = jnp.transpose(a2[b])
        acc[...] = jnp.zeros_like(acc)
        if b < last:
            for p in range(last * parts, (last + 1) * parts):
                for phase in range(phases):
                    sent(ag_copies(p, phase))
            for cp in mlp_loads:
                cp.wait()

        def mlp_back(t, carry):
            hooks(t, back_hooks.get((b, "mlp"), {}))
            put_grad(b, t, c_down, cols, dot(dxt, gl[t]))
            dh = dot(cut[...], weight(b, t, c_down, cols))
            du = (dh * gp[t].astype(F32)).astype(BF16)
            gp[t] = du
            small[pl.ds(HID_ROW + b * groups + t, 1), :] = jnp.sum(
                fold(du.astype(F32)), 0, keepdims=True
            )
            put_grad(b, t, c_up, c_down, dot(a_t, du))
            acc[...] += dot(du, weight(b, t, c_up, c_down), NT)
            return carry

        lax.fori_loop(0, groups, mlp_back, 0)
        start(rs_copies(b, 2, 0))
        start(rs_copies(b, 1, 0))
        if b == last:
            start(mlp_loads)
        sums = back_norm(ms.at[b], acc, gains[b, 1:2, :], dx)
        small[GAIN_ROW + 2 * b + 1 : GAIN_ROW + 2 * b + 2, :] = sums[0]
        small[bias_row + 1 : bias_row + 2, :] = sums[1]
        small[bias_row + 2 : bias_row + 3, :] = sums[2]
        cut[...] = dx[...].astype(BF16)
        dmt = jnp.transpose(cut[...])
        awt[...] = jnp.transpose(aw[b])
        da = ubuf
        da[...] = jnp.zeros_like(da)
        for t in range(groups):
            put_grad(b, t, c_out, c_up, dot(dmt, osb[b, t]))
        if b < last:
            for cp in att_loads:
                cp.wait()

        def attend_back(t, carry):
            hooks(t, back_hooks.get((b, "attend"), {}))
            do_t = dot(cut[...], weight(b, t, c_out, c_up)).astype(BF16)
            for i in range(images):
                base = image_base(i)
                ow[i * IMG_PAD : (i + 1) * IMG_PAD, :] = dot(
                    perm[b, i], do_t[base : base + IMG_ROWS]
                ).astype(BF16)
            dsum[...] = jnp.zeros_like(dsum)

            def window(w, c2):
                r = pl.multiple_of(w * PAD, PAD)
                q = qkv[t, pl.ds(r, PAD), 0:lanes]
                k = qkv[t, pl.ds(r, PAD), lanes : 2 * lanes]
                v = qkv[t, pl.ds(r, PAD), 2 * lanes : 3 * lanes]
                p = pts[t, w]
                dob = spread(ow[pl.ds(r, PAD), :], heads)
                dp = dot(v, dob, NT)
                pf = p.astype(F32)
                ds = (pf * (dp - jnp.sum(pf * dp, 0, keepdims=True))).astype(BF16)
                dsum[...] += ds.astype(F32)
                dv = dot(p, dob)
                dk = dot(ds, spread(q, heads)) * INV_ROOT
                dq = gather_diag(dot(ds, k, TN), heads) * INV_ROOT
                dwin[pl.ds(r, PAD), 0:lanes] = dq.astype(BF16)
                dwin[pl.ds(r, PAD), lanes : 2 * lanes] = dk.astype(BF16)
                dwin[pl.ds(r, PAD), 2 * lanes : 3 * lanes] = dv.astype(BF16)
                return c2

            lax.fori_loop(0, images * WINS, window, 0, unroll=2)
            col = pl.ds(pl.multiple_of(t * lanes, lanes), lanes)
            for j in range(2):
                val = dwin[:, 2 * j * lanes : (2 * j + 1) * lanes].astype(F32)
                row = QV_ROW + 2 * b + j
                small[row : row + 1, col] = jnp.sum(fold(val), 0, keepdims=True)
            ds_all = dsum[...]
            high = ds_all.astype(BF16)
            rest_low = (ds_all - high.astype(F32)).astype(BF16)
            wide = sum(
                dot(dot(rel_down[...], piece).astype(BF16), rel_across[...])
                for piece in (high, rest_low)
            )
            skew = wide[0:8]
            for a in range(1, wide.shape[0] // 8):
                skew = skew + pltpu.roll(wide[8 * a : 8 * a + 8], 8 * a, 1)
            row_id = lax.broadcasted_iota(jnp.int32, skew.shape, 0)
            for bit in (1, 2, 4):
                skew = jnp.where((row_id & bit) != 0, pltpu.roll(skew, bit, 1), skew)
            skew = jnp.sum(skew, 0, keepdims=True)
            for h in range(GROUP):
                small[pl.ds(rel_row(groups) + (b * groups + t) * GROUP + h, 1), 0:REL_LANES] = skew[
                    :, h * REL_LANES : (h + 1) * REL_LANES
                ]
            put_grad(b, t, 0, c_out, dot(awt[...], dwin[...]))
            da[...] += dot(dwin[...], weight(b, t, 0, c_out), NT)
            return carry

        lax.fori_loop(0, groups, attend_back, 0)
        start(rs_copies(b, 0, 0))
        if b == last:
            start(att_loads)
        vals = []
        for i in range(images):
            part = da[i * IMG_PAD : (i + 1) * IMG_PAD, :]
            high = part.astype(BF16)
            rest_low = (part - high.astype(F32)).astype(BF16)
            vals.append(dot(perm_t[b, i], high) + dot(perm_t[b, i], rest_low))
        put_rows(acc, vals)
        sums = back_norm(xs.at[b], acc, gains[b, 0:1, :], dx)
        small[GAIN_ROW + 2 * b : GAIN_ROW + 2 * b + 1, :] = sums[0]
        small[bias_row : bias_row + 1, :] = sums[1]
    small_step(0)
    rs_step(0, 0, 1)
    x_store.wait()
    for i in range(images):
        io[i] = dx[i * TOKENS : (i + 1) * TOKENS, :]
    dx_store = pltpu.make_async_copy(io, dxo_hbm, io_sem.at[1])
    dx_store.start()
    small_step(1)
    rs_step(0, 2, 3)
    rs_step(0, 0, 2)
    small_step(2)
    rs_step(0, 1, 3)
    rs_finish(0, 2)
    small_step(3)
    rs_step(0, 0, 3)
    rs_finish(0, 1)
    small_step(4)
    rs_finish(0, 0)
    dx_store.wait()
    for p in range(last * parts):
        for phase in range(phases):
            sent(ag_copies(p, phase))
    for b in range(BLOCKS):
        for part in range(parts):
            for phase in range(phases):
                sent(rs_copies(b, part, phase))
    for phase in range(phases):
        sent(small_copies(phase))


def block_call(x, ct, live, own, rel, side, gains, offs, n_fsdp, n_tensor):
    images, _, width = x.shape
    cols = own.shape[2]
    per = own.shape[1]
    lanes = GROUP * HEAD_DIM
    hid = (cols - 4 * lanes) // 2
    parts = cols // PART
    rows = -(-images * TOKENS // 16) * 16
    wrows = images * IMG_PAD
    digits = plan(n_fsdp, n_tensor)
    dims = sorted(digits.values(), key=lambda d: d.dim)
    sizes = tuple(d.size for d in dims)
    most = max(sizes) - 1
    phases = len(dims)
    perm = permutations(images)
    down, across = rel_consts()
    consts = (
        jnp.asarray(np.tile(mask_table(), (1, 1, 1, GROUP)), BF16),
        jnp.asarray(perm, BF16),
        jnp.asarray(np.swapaxes(perm, 2, 3), BF16),
        jnp.asarray(down, BF16),
        jnp.asarray(across, BF16),
    )
    small_rows = rel_row(n_tensor) + BLOCKS * n_tensor * GROUP
    stages = []
    for order in orders(digits):
        order = order[::-1]
        for phase, digit in enumerate(order):
            left = tuple(d.size for d in dims if d not in order[: phase + 1])
            stages.append(pltpu.VMEM((BLOCKS, parts, digit.size - 1) + left + (per, HALF), BF16))
    small_order = [digits[n] for n in ("core", "y", "x", "z")]
    vmem = pl.BlockSpec(memory_space=pltpu.VMEM)
    anyspace = pl.BlockSpec(memory_space=pl.ANY)
    keep = [
        (n_tensor, rows, hid), (n_tensor, rows, hid), (n_tensor, wrows, 3 * lanes),
        (n_tensor, images * WINS, PAD, GROUP * PAD),
    ]
    dma = pltpu.SemaphoreType.DMA
    out = pl.pallas_call(
        functools.partial(block_kernel, n_fsdp, n_tensor),
        out_shape=(
            jax.ShapeDtypeStruct(x.shape, F32),
            jax.ShapeDtypeStruct(x.shape, F32),
            jax.ShapeDtypeStruct((BLOCKS, per, cols), F32),
            jax.ShapeDtypeStruct((small_rows, width), F32),
        ) + tuple(jax.ShapeDtypeStruct(s, BF16) for s in keep),
        in_specs=[
            anyspace, anyspace, pl.BlockSpec(memory_space=pltpu.SMEM), anyspace, anyspace, anyspace,
        ] + [vmem] * 7,
        out_specs=(anyspace, anyspace, vmem, vmem) + (anyspace,) * 4,
        scratch_shapes=[
            pltpu.VMEM((BLOCKS,) + sizes + (per, cols), BF16),
            pltpu.VMEM(sizes + (per, cols), BF16),
            pltpu.VMEM((n_tensor,) + rel.shape, BF16),
            pltpu.VMEM((n_tensor,) + side.shape, F32),
            pltpu.VMEM(x.shape, F32),
            pltpu.VMEM((BLOCKS, rows, width), F32),
            pltpu.VMEM((BLOCKS, rows, width), F32),
            pltpu.VMEM((BLOCKS, wrows, width), BF16),
            pltpu.VMEM(keep[2], BF16),
            pltpu.VMEM(keep[3], BF16),
            pltpu.VMEM((wrows, lanes), BF16),
            pltpu.VMEM((BLOCKS, n_tensor, rows, lanes), BF16),
            pltpu.VMEM((BLOCKS, rows, width), BF16),
            pltpu.VMEM(keep[0], BF16),
            pltpu.VMEM(keep[1], BF16),
            pltpu.VMEM((wrows, width), F32),
            pltpu.VMEM((rows, width), F32),
            pltpu.VMEM((rows, width), F32),
            pltpu.VMEM((rows, width), BF16),
            pltpu.VMEM((width, wrows), BF16),
            pltpu.VMEM((wrows, 3 * lanes), BF16),
            pltpu.VMEM((PAD, GROUP * PAD), F32),
            pltpu.VMEM((small_rows, width), F32),
        ]
        + stages
        + [pltpu.VMEM((d.size, small_rows, width), F32) for d in small_order]
        + [
            dma((2,)), dma((BLOCKS + 2,)), dma((4,)),
            dma((n_tensor - 1,)), dma((n_tensor - 1,)), dma((n_tensor - 1,)), dma((n_tensor - 1,)),
            dma((BLOCKS * parts, 2, phases, most)), dma((BLOCKS * parts, 2, phases, most)),
            dma((BLOCKS, parts, 2, phases, most)), dma((BLOCKS, parts, 2, phases, most)),
            dma((phases, most)), dma((phases, most)),
        ],
        compiler_params=pltpu.CompilerParams(
            collective_id=0, has_side_effects=True, vmem_limit_bytes=127 * MIB // 2
        ),
    )(x, ct, live, own, rel, side, consts[0], gains, offs, *consts[1:])
    return out[:4]


def adam_kernel(groups, gsum, total, slot, *refs):
    params = [refs[3 * j : 3 * j + 3] for j in range(9)]
    outs = [refs[27 + 3 * j : 30 + 3 * j] for j in range(9)]
    lanes = GROUP * HEAD_DIM
    hid = params[2][0].shape[2]
    t = slot[0]

    def update(kind, place, grad, rate, decay):
        new = adam(*(p[place] for p in params[kind]), grad, rate, decay)
        for ref, val in zip(outs[kind], new):
            ref[place] = val

    for b in range(BLOCKS):
        for j in range(3):
            update(0, (b, j), gsum[b, :, j * lanes : (j + 1) * lanes], MATRIX_RATE, WEIGHT_DECAY)
        update(1, (b,), gsum[b, :, 3 * lanes : 4 * lanes], MATRIX_RATE, WEIGHT_DECAY)
        update(2, (b,), gsum[b, :, 4 * lanes : 4 * lanes + hid], MATRIX_RATE, WEIGHT_DECAY)
        update(3, (b,), gsum[b, :, 4 * lanes + hid :], MATRIX_RATE, WEIGHT_DECAY)
        heads, rels = params[4][0].shape[1:]
        at = rel_row(groups) + b * groups * heads
        hid_at = HID_ROW + b * groups
        rel = pick(t, [total[at + i * heads : at + (i + 1) * heads, 0:rels] for i in range(groups)])
        qv = pick(t, [total[QV_ROW + 2 * b : QV_ROW + 2 * b + 2, i * lanes : (i + 1) * lanes] for i in range(groups)])
        hidden = pick(t, [total[hid_at + i : hid_at + i + 1, :] for i in range(groups)])
        update(4, (b,), rel, SMALL_RATE, 0.0)
        update(5, (b,), qv, SMALL_RATE, 0.0)
        update(6, (slice(b, b + 1),), hidden, SMALL_RATE, 0.0)
        update(7, (b,), total[GAIN_ROW + 2 * b : GAIN_ROW + 2 * b + 2, :], SMALL_RATE, 0.0)
        update(8, (b,), total[BIAS_ROW + 4 * b : BIAS_ROW + 4 * b + 4, :], SMALL_RATE, 0.0)


def adam_call(gsum, total, params, n_tensor):
    vmem = pl.BlockSpec(memory_space=pltpu.VMEM)
    flat = [p for group in params for p in group]
    slot = lax.axis_index("tensor").astype(jnp.int32).reshape(1)
    return pl.pallas_call(
        functools.partial(adam_kernel, n_tensor),
        out_shape=tuple(jax.ShapeDtypeStruct(p.shape, p.dtype) for p in flat),
        in_specs=[vmem, vmem, pl.BlockSpec(memory_space=pltpu.SMEM)] + [vmem] * len(flat),
        out_specs=tuple(vmem for _ in flat),
        compiler_params=pltpu.CompilerParams(vmem_limit_bytes=32 * MIB),
    )(gsum, total, slot, *flat)


def shards(n_fsdp, n_tensor, *args):
    image_rows, cotangent, live_counts = args[:3]
    qkv, out, up, down, rel, qv, hidden, gain, bias = [args[3 + 3 * j : 6 + 3 * j] for j in range(9)]
    qkv = tuple(p.transpose(0, 2, 1, 3) for p in qkv)
    out = tuple(p.swapaxes(1, 2) for p in out)
    down = tuple(p.swapaxes(1, 2) for p in down)
    images = image_rows.shape[0]
    slots = lax.axis_index("tensor") * images + jnp.arange(images, dtype=jnp.int32)
    live = (slots < live_counts[0]).astype(F32)
    own = jnp.concatenate([qkv[0][:, j] for j in range(3)] + [out[0], up[0], down[0]], 2).astype(BF16)
    heads, rels = rel[0].shape[1:]
    onehot = jnp.asarray(rel_onehot(rels).reshape(rels, -1), BF16)
    rel_own = lax.dot_general(
        rel[0].astype(BF16), onehot, (((2,), (0,)), ((), ())), preferred_element_type=F32
    )
    rel_own = rel_own.astype(BF16).reshape(BLOCKS, heads, PAD, PAD)
    rel_own = rel_own.swapaxes(1, 2).reshape(BLOCKS, PAD, heads * PAD)
    hid = hidden[0].shape[1]
    side = jnp.concatenate(
        [jnp.pad(qv[0].reshape(2 * BLOCKS, -1), ((0, 0), (0, hid - qv[0].shape[2]))), hidden[0],
         jnp.zeros((8 - 3 * BLOCKS, hid), F32)], 0)
    x_out, dx_out, gsum, total = block_call(
        image_rows, cotangent, live, own, rel_own, side, gain[0], bias[0], n_fsdp, n_tensor
    )
    new = adam_call(gsum, total, (qkv, out, up, down, rel, qv, hidden, gain, bias), n_tensor)
    new = [list(new[3 * j : 3 * j + 3]) for j in range(9)]
    new[0] = [p.transpose(0, 2, 1, 3) for p in new[0]]
    new[1] = [p.swapaxes(1, 2) for p in new[1]]
    new[3] = [p.swapaxes(1, 2) for p in new[3]]
    return (x_out, dx_out) + tuple(p for group in new for p in group)
```

```python
import functools
import numpy as np
import jax
import jax.numpy as jnp
from jax import lax
from jax.experimental import pallas as pl
from jax.experimental.pallas import tpu as pltpu
from jax.sharding import PartitionSpec as P
HEAD_DIM = 32
SIDE = 14
WIN = 7
SHIFT = 3
BLOCKS = 2
ADAM_STEP = 10
TOKENS = SIDE * SIDE
WINS = (SIDE // WIN) ** 2
SPAN = WIN * WIN
PAD = 64
IMG_PAD = WINS * PAD
IMG_ROWS = 208
GROUP = 4
NORM_EPS = 1e-05
BETA_ONE = 0.9
BETA_TWO = 0.999
MATRIX_RATE = 0.04
SMALL_RATE = 0.3
WEIGHT_DECAY = 0.05
ADAM_EPS = 1e-08
MASK_FILL = -100.0
KEY_FILL = -1e30
INV_ROOT = HEAD_DIM ** (-0.5)
MIB = 1024 * 1024
F32 = jnp.float32
BF16 = jnp.bfloat16
NT = (((1,), (1,)), ((), ()))
TN = (((0,), (0,)), ((), ()))


def window_source(shifted):
    out = np.zeros((WINS, SPAN), np.int64)
    step = SHIFT if shifted else 0
    per = SIDE // WIN
    for w in range(WINS):
        for p in range(SPAN):
            r = (w // per) * WIN + p // WIN
            c = (w % per) * WIN + p % WIN
            out[w, p] = ((r + step) % SIDE) * SIDE + (c + step) % SIDE
    return out


def image_base(i):
    return (i * TOKENS) // 16 * 16


def permutations(images):
    perm = np.zeros((BLOCKS, images, IMG_PAD, IMG_ROWS), np.float32)
    for b in range(BLOCKS):
        src = window_source(b % 2 == 1)
        for i in range(images):
            off = i * TOKENS - image_base(i)
            for w in range(WINS):
                for p in range(SPAN):
                    perm[b, i, w * PAD + p, off + src[w, p]] = 1.0
    return perm


def mask_table():
    out = np.zeros((BLOCKS, WINS, PAD, PAD), np.float32)
    coords = np.arange(SIDE)
    bands = (coords >= SIDE - WIN).astype(int) + (coords >= SIDE - SHIFT).astype(int)
    region = (bands[:, None] * 3 + bands[None, :]).reshape(-1)
    base = window_source(False)
    for b in range(BLOCKS):
        for w in range(WINS):
            if b % 2 == 1:
                lab = region[base[w]]
                out[b, w, :SPAN, :SPAN] = np.where(lab[:, None] == lab[None, :], 0.0, MASK_FILL)
            out[b, w, SPAN:, :] = KEY_FILL
    return out


def dot(a, b, dims=None):
    if dims is None:
        return jnp.dot(a, b, preferred_element_type=F32)
    return lax.dot_general(a, b, dims, preferred_element_type=F32)


def lane_heads(width):
    return lax.broadcasted_iota(jnp.int32, (1, width), 1) // HEAD_DIM


def spread(rows, heads):
    zero = jnp.zeros_like(rows)
    return jnp.concatenate([jnp.where(heads == h, rows, zero) for h in range(GROUP)], 0)


def gather_diag(prod, heads):
    out = prod[0:PAD]
    for h in range(1, GROUP):
        out = jnp.where(heads == h, prod[h * PAD : (h + 1) * PAD], out)
    return out


def gelu_pair(u):
    au = jnp.abs(u)
    t = 1.0 / (1.0 + (0.3275911 * 0.7071067811865476) * au)
    e = jnp.exp(-0.5 * u * u)
    q = 1.061405429 * 0.5
    q = q * t - 1.453152027 * 0.5
    q = q * t + 1.421413741 * 0.5
    q = q * t - 0.284496736 * 0.5
    q = q * t + 0.254829592 * 0.5
    q = q * t * e
    phi = jnp.where(u >= 0, 1.0 - q, q)
    return u * phi, phi + u * e * 0.3989422804014327


def chunks(rows, size):
    return [(r, min(size, rows - r)) for r in range(0, rows, size)]


def norm_rows(x):
    mean = jnp.mean(x, -1, keepdims=True)
    cen = x - mean
    inv = lax.rsqrt(jnp.mean(cen * cen, -1, keepdims=True) + NORM_EPS)
    return cen * inv, inv


def put_rows(ref, vals):
    images = len(vals)
    for i in range(images):
        base = image_base(i)
        lead = 0
        if i > 0:
            lead = image_base(i - 1) + IMG_ROWS - base
            mix = vals[i - 1][IMG_ROWS - lead :] + vals[i][:lead]
            ref[base : base + lead, :] = mix.astype(ref.dtype)
        end = image_base(i + 1) - base if i + 1 < images else IMG_ROWS
        ref[base + lead : base + end, :] = vals[i][lead:end].astype(ref.dtype)


def norm_into(src, dst, gain, off):
    for r, n in chunks(src.shape[0], 112):
        unit, _ = norm_rows(src[r : r + n, :])
        dst[r : r + n, :] = (unit * gain + off).astype(BF16)


def fold(val):
    rows, cols = val.shape
    return jnp.sum(val.reshape(rows // 8, 8, cols), 0)


def back_norm(src, grad, gain, dst):
    width = src.shape[1]
    sums = [jnp.zeros((8, width), F32) for _ in range(3)]
    for r, n in chunks(src.shape[0], 112):
        unit, inv = norm_rows(src[r : r + n, :])
        gr = grad[r : r + n, :]
        e = gr * gain
        res = dst[r : r + n, :] + inv * (
            e - jnp.mean(e, -1, keepdims=True) - unit * jnp.mean(e * unit, -1, keepdims=True)
        )
        dst[r : r + n, :] = res
        for j, val in enumerate((gr * unit, gr, res)):
            sums[j] = sums[j] + fold(val)
    return [jnp.sum(s, 0, keepdims=True) for s in sums]


def column_sum(ref):
    total = jnp.zeros((8, ref.shape[1]), F32)
    for r, n in chunks(ref.shape[0], 112):
        total = total + fold(ref[r : r + n, :])
    return jnp.sum(total, 0, keepdims=True)
GAIN_ROW = 0
BIAS_ROW = GAIN_ROW + 2 * BLOCKS
QV_ROW = BIAS_ROW + 4 * BLOCKS
HID_ROW = QV_ROW + 2 * BLOCKS
MESH = pl.DeviceIdType.MESH


class Digit:
    def __init__(self, name, axis, size, stride, dim):
        self.name, self.axis, self.size, self.stride, self.dim = name, axis, size, stride, dim

    def here(self):
        return lax.rem(lax.axis_index(self.axis) // self.stride, self.size)

    def peer(self, step):
        d = self.here()
        to = lax.rem(d + step, self.size)
        return to, {self.axis: lax.axis_index(self.axis) + (to - d) * self.stride}


def plan(n_fsdp, n_tensor):
    if (n_fsdp, n_tensor) == (8, 4):
        parts = [("x", "tensor", 2), ("core", "tensor", 2), ("z", "fsdp", 4), ("y", "fsdp", 2)]
    elif (n_fsdp, n_tensor) == (32, 4):
        parts = [("x", "tensor", 4), ("z", "fsdp", 4), ("y", "fsdp", 4), ("core", "fsdp", 2)]
    else:
        parts = [("x", "tensor", n_tensor), ("z", "fsdp", n_fsdp)]
    digits = {}
    for dim, (name, axis, size) in enumerate(parts):
        stride = 1
        for _, later_axis, later in parts[dim + 1 :]:
            if later_axis == axis:
                stride *= later
        digits[name] = Digit(name, axis, size, stride, dim)
    return digits


def orders(digits):
    one = [n for n in ("z", "x", "y", "core") if n in digits]
    two = [n for n in ("z", "y", "x", "core") if n in digits]
    return [[digits[n] for n in one], [digits[n] for n in two]]


def greet(peers):
    barrier = pltpu.get_barrier_semaphore()
    for device in peers:
        pl.semaphore_signal(barrier, inc=1, device_id=device, device_id_type=MESH)
    pl.semaphore_wait(barrier, len(peers))


def tensor_peers(n_tensor):
    t = lax.axis_index("tensor")
    return [{"tensor": lax.rem(t + s, n_tensor)} for s in range(1, n_tensor)]


def all_peers(digits, n_tensor):
    peers = [d.peer(s)[1] for d in digits.values() if d.axis == "fsdp" for s in range(1, d.size)]
    return peers + tensor_peers(n_tensor)


def pieces(cols, width):
    return [(c, min(width, cols - c)) for c in range(0, cols, width)]


def adam(weight, first, second, grad, rate, decay):
    first_new = BETA_ONE * first + (1.0 - BETA_ONE) * grad
    second_new = BETA_TWO * second + (1.0 - BETA_TWO) * grad * grad
    first_hat = first_new * (1.0 / (1.0 - BETA_ONE**ADAM_STEP))
    second_hat = second_new * (1.0 / (1.0 - BETA_TWO**ADAM_STEP))
    step = first_hat / (jnp.sqrt(second_hat) + ADAM_EPS)
    if decay:
        step = step + decay * weight
    return weight - rate * step, first_new, second_new


def pick(index, values):
    out = values[0]
    for i in range(1, len(values)):
        out = jnp.where(index == i, values[i], out)
    return out


def rel_row(groups):
    return HID_ROW + BLOCKS * groups


def solution(mesh):
    n_fsdp, n_tensor = mesh.shape["fsdp"], mesh.shape["tensor"]
    tokens = P(("fsdp", "tensor"), None, None)
    kinds = (
        P(None, "fsdp", None, "tensor"), P(None, "tensor", "fsdp"), P(None, "fsdp", "tensor"),
        P(None, "tensor", "fsdp"), P(None, "tensor", None), P(None, None, "tensor"),
        P(None, "tensor"), P(), P(),
    )
    thrice = tuple(k for k in kinds for _ in range(3))
    return jax.shard_map(
        functools.partial(shards, n_fsdp, n_tensor),
        mesh=mesh,
        in_specs=(tokens, tokens, P("fsdp")) + thrice,
        out_specs=(tokens, tokens) + thrice,
        check_vma=False,
    )
PART = 512
HALF = 256
REL_LANES = 256
Z_FIRST = (("z", "x", "y", "core"), ("z", "y", "x", "core"))
Z_LATE = (("x", "y", "z", "core"), ("y", "x", "z", "core"))
GATHER_LATE = ((1, 2),)
REDUCE_LATE = ((1, 2), (0, 2))
BATCH = 12
LOG2E = 1.4426950408889634


def rel_consts():
    side = 2 * WIN - 1
    top = side * (WIN - 1) + WIN - 1
    down = np.zeros((96, PAD), np.float32)
    across = np.zeros((GROUP * PAD, GROUP * REL_LANES), np.float32)
    for i in range(SPAN):
        place = side * (i // WIN) + i % WIN
        down[top - place, i] = 1.0
        for h in range(GROUP):
            across[h * PAD + i, h * REL_LANES + place] = 1.0
    return down, across


def stage_keys(parts, phases):
    return [
        (b, part, h, phase)
        for b in range(BLOCKS)
        for part in range(parts)
        for h in range(2)
        for phase in range(phases)
    ]


def gather_order(digits, b, part, half):
    return [digits[n] for n in (Z_LATE if (b, part) in GATHER_LATE else Z_FIRST)[half]]


def reduce_order(digits, b, part, half):
    return [digits[n] for n in (Z_LATE if (b, part) in REDUCE_LATE else Z_FIRST)[half]][::-1]


def block_kernel(
    n_fsdp, n_tensor,
    x_hbm, ct_hbm, counts, qkv_w, out_w, up_w, down_w, rel_w, qv_w, hid_w, mask, gains, offs, perm, perm_t, rel_down, rel_across,
    xo_hbm, dxo_hbm, gsum, total, keep_gl, keep_gp, keep_qkv, keep_pts,
    wt, dgr, rels, sides, io, xs, ms, aw, qkv, pts, ow, osb, a2, gl, gp, ubuf, acc, dx, cut, awt, dwin, dsum, added, small,
    *rest,
):
    digits = plan(n_fsdp, n_tensor)
    dims = sorted(digits.values(), key=lambda d: d.dim)
    phases = len(dims)
    parts = wt.shape[-1] // PART
    pairs = BLOCKS * parts
    stage = {}
    for at, key in enumerate(stage_keys(parts, phases)):
        stage[key] = rest[at]
    rest = rest[len(stage) :]
    small_slots = rest[:phases]
    (io_sem, own_sem, keep_sem, rel_send, rel_recv, side_send, side_recv, ag_send, ag_recv, rs_send, rs_recv,
     sm_send, sm_recv) = rest[phases:]
    images = io.shape[0]
    groups = n_tensor
    rows, width = xs.shape[1:]
    lanes = GROUP * HEAD_DIM
    hid = gl.shape[2]
    cols = wt.shape[-1]
    c_out, c_up, c_down = 3 * lanes, 4 * lanes, 4 * lanes + hid
    heads = lane_heads(lanes)
    tdims = [d for d in dims if d.axis == "tensor"]
    fdims = [d for d in dims if d.axis == "fsdp"]
    per = wt.shape[-2]
    fshape = tuple(d.size for d in fdims) + (per,)
    t_here = lax.axis_index("tensor")

    def tplace(t):
        return tuple(lax.rem(t // d.stride, d.size) for d in tdims)

    def weight(b, t, lo, hi):
        index = (b,) + tplace(t) + (slice(None),) * len(fshape) + (slice(lo, hi),)
        return wt[index].reshape(width, hi - lo)

    def grad_ref(b):
        return dgr if b == BLOCKS - 1 else wt.at[BLOCKS - 1]

    def put_grad(b, t, lo, hi, value):
        index = tplace(t) + (slice(None),) * len(fshape) + (slice(lo, hi),)
        grad_ref(b)[index] = value.astype(BF16).reshape(fshape + (hi - lo,))

    def ag_copies(p, phase):
        b, c = p // parts, (p % parts) * PART
        out = []
        for h in range(2):
            order = gather_order(digits, b, p % parts, h)
            digit = order[phase]
            at = pl.ds(c + h * HALF, HALF)
            index = tuple(slice(None) if d in order[:phase] else d.here() for d in dims)
            dst = wt.at[(b,) + index + (slice(None), at)]
            for s in range(1, digit.size):
                sem = (p, h, phase, s - 1)
                out.append(pltpu.make_async_remote_copy(
                    src_ref=dst, dst_ref=dst, send_sem=ag_send.at[sem], recv_sem=ag_recv.at[sem],
                    device_id=digit.peer(s)[1], device_id_type=MESH))
        return out

    def start(copies):
        for cp in copies:
            cp.start()

    def arrive(copies):
        for cp in copies:
            cp.wait_recv()

    def sent(copies):
        for cp in copies:
            cp.wait_send()

    def ag_step(p, phase):
        if 0 <= p < pairs:
            arrive(ag_copies(p, phase - 1))
            start(ag_copies(p, phase))
            if phase == 1 and p + 2 < late:
                start(ag_copies(p + 2, 0))

    late = pairs - 1

    def pump(i):
        if i + 2 < late:
            ag_step(i + 2, 1)
        if i + 1 < late:
            ag_step(i + 1, 2)
        ag_step(i, 3)

    def need(p):
        arrive(ag_copies(p, phases - 1))

    def rs_copies(b, part, phase):
        out = []
        for h in range(2):
            order = reduce_order(digits, b, part, h)
            digit = order[phase]
            at = pl.ds(part * PART + h * HALF, HALF)
            for s in range(1, digit.size):
                to, device = digit.peer(s)
                index = tuple(
                    to if d is digit else d.here() if d in order[:phase] else slice(None) for d in dims
                )
                sem = (b, part, h, phase, s - 1)
                out.append(pltpu.make_async_remote_copy(
                    src_ref=grad_ref(b).at[index + (slice(None), at)],
                    dst_ref=stage[b, part, h, phase].at[s - 1],
                    send_sem=rs_send.at[sem], recv_sem=rs_recv.at[sem],
                    device_id=device, device_id_type=MESH))
        return out

    def rs_absorb(b, part, phase):
        grad = grad_ref(b)
        for h in range(2):
            order = reduce_order(digits, b, part, h)
            digit = order[phase]
            at = slice(part * PART + h * HALF, part * PART + (h + 1) * HALF)
            left = [d for d in dims if d not in order[: phase + 1]]
            land = stage[b, part, h, phase]
            steps = int(np.prod([d.size for d in left]))

            def one(i, carry):
                place = {}
                more = i
                for d in reversed(left):
                    place[d.name] = lax.rem(more, d.size)
                    more = more // d.size
                index = tuple(place[d.name] if d in left else d.here() for d in dims)
                value = grad[index + (slice(None), at)]
                for s in range(digit.size - 1):
                    value = value + land[(s,) + tuple(place[d.name] for d in left)]
                grad[index + (slice(None), at)] = value
                return carry

            lax.fori_loop(0, steps, one, 0, unroll=min(steps, 4))

    def rs_step(b, part, phase):
        arrive(rs_copies(b, part, phase - 1))
        rs_absorb(b, part, phase - 1)
        start(rs_copies(b, part, phase))

    def rs_finish(b, part):
        arrive(rs_copies(b, part, phases - 1))
        for h in range(2):
            digit = reduce_order(digits, b, part, h)[-1]
            at = slice(part * PART + h * HALF, part * PART + (h + 1) * HALF)
            index = tuple(d.here() for d in dims)
            value = grad_ref(b)[index + (slice(None), at)].astype(F32)
            for s in range(digit.size - 1):
                value = value + stage[b, part, h, phases - 1][s].astype(F32)
            gsum[b, :, at] = value

    small_order = [digits[n] for n in ("core", "y", "x", "z")]

    def small_copies(phase):
        digit = small_order[phase]
        place = small_slots[phase].at[digit.here()]
        return [
            pltpu.make_async_remote_copy(
                src_ref=place, dst_ref=place, send_sem=sm_send.at[phase, s - 1],
                recv_sem=sm_recv.at[phase, s - 1], device_id=digit.peer(s)[1], device_id_type=MESH)
            for s in range(1, digit.size)
        ]

    def small_step(phase):
        if phase == 0:
            value = small[...]
        else:
            arrive(small_copies(phase - 1))
            value = small_slots[phase - 1][0]
            for s in range(1, small_order[phase - 1].size):
                value = value + small_slots[phase - 1][s]
        if phase < phases:
            small_slots[phase][small_order[phase].here()] = value
            start(small_copies(phase))
        else:
            total[...] = value

    loads = [
        pltpu.make_async_copy(x_hbm, io, io_sem.at[0]),
        pltpu.make_async_copy(ct_hbm, io, io_sem.at[1]),
    ]
    own_copies = []
    for b in range(BLOCKS):
        rows_of = [pl.ds((3 * b + j) * per, per) for j in range(3)]
        pieces_of = [(qkv_w.at[b, j], ubuf.at[rows_of[0], pl.ds(j * lanes, lanes)]) for j in range(3)]
        pieces_of.append((out_w.at[b], ubuf.at[rows_of[0], pl.ds(3 * lanes, lanes)]))
        pieces_of.append((up_w.at[b], ubuf.at[rows_of[1], :]))
        pieces_of.append((down_w.at[b], ubuf.at[rows_of[2], :]))
        own_copies.append([
            pltpu.make_async_copy(src, dst, own_sem.at[b, j]) for j, (src, dst) in enumerate(pieces_of)
        ])
        for cp in own_copies[b]:
            cp.start()
    loads[0].start()
    greet(all_peers(digits, n_tensor))
    mine = tuple(d.here() for d in dims)
    for b in range(BLOCKS):
        for cp in own_copies[b]:
            cp.wait()
        for j in range(parts):
            row = (3 * b + j) * per
            wt[(b,) + mine + (slice(None), slice(j * PART, (j + 1) * PART))] = ubuf[
                row : row + per, :
            ].astype(BF16)
            if b * parts + j in (0, 1, late):
                start(ag_copies(b * parts + j, 0))

    rel_count = rel_w.shape[2]
    added[0, 0:8, :] = jnp.zeros((8, GROUP * PAD), F32)
    for b in range(BLOCKS):
        added[0, GROUP * b : GROUP * (b + 1), 0:rel_count] = rel_w[b]
        row = jnp.concatenate(
            [added[0, GROUP * b + h : GROUP * b + h + 1, :] for h in range(GROUP)], 1
        )
        skew = jnp.broadcast_to(row, (8, row.shape[1]))
        row_id = lax.broadcasted_iota(jnp.int32, skew.shape, 0)
        for bit in (1, 2, 4):
            skew = jnp.where((row_id & bit) != 0, pltpu.roll(skew, skew.shape[1] - bit, 1), skew)
        wide = jnp.concatenate(
            [skew]
            + [pltpu.roll(skew, skew.shape[1] - 8 * a, 1) for a in range(1, rel_down.shape[0] // 8)], 0
        )
        wide = dot(rel_down[...], wide.astype(BF16), TN).astype(BF16)
        rels[t_here, b] = dot(wide, rel_across[...], NT).astype(BF16)
        sides[t_here, 2 * b : 2 * b + 2, 0:lanes] = qv_w[b]
    sides[t_here, 2 * BLOCKS : 3 * BLOCKS, :] = hid_w[...]
    side_copies = [
        pltpu.make_async_remote_copy(
            src_ref=ref.at[t_here], dst_ref=ref.at[t_here], send_sem=ssem.at[j], recv_sem=rsem.at[j],
            device_id=device, device_id_type=MESH)
        for ref, ssem, rsem in ((rels, rel_send, rel_recv), (sides, side_send, side_recv))
        for j, device in enumerate(tensor_peers(n_tensor))
    ]
    start(side_copies)
    ag_step(0, 1)

    used = images * TOKENS
    floor = used // 8 * 8
    loads[0].wait()
    xs[0, floor:rows, :] = jnp.zeros((rows - floor, width), F32)
    for i in range(images):
        xs[0, i * TOKENS : (i + 1) * TOKENS, :] = io[i]
    loads[1].start()

    def first_norm(b):
        norm_into(xs.at[b], cut, gains[b, 0:1, :], offs[b, 0:1, :])
        for i in range(images):
            base = image_base(i)
            aw[b, i * IMG_PAD : (i + 1) * IMG_PAD, :] = dot(
                perm[b, i], cut[base : base + IMG_ROWS, :]
            ).astype(BF16)

    first_norm(0)
    ag_step(late, 1)
    ag_step(1, 1)
    ag_step(0, 2)
    loads[1].wait()
    dx[floor:rows, :] = jnp.zeros((rows - floor, width), F32)
    for i in range(images):
        live = (t_here * images + i < counts[0]).astype(F32)
        dx[i * TOKENS : (i + 1) * TOKENS, :] = io[i] * live
    pump(0)
    for cp in side_copies:
        cp.wait()

    def hooks(t, table):
        for at, calls in table.items():

            @pl.when(t == at)
            def _():
                for call in calls:
                    call()

    fwd_hooks = {
        (0, "attend"): {
            0: [lambda: ag_step(3, 1)],
            2: [lambda: ag_step(2, 2)],
            3: [lambda: ag_step(1, 3), lambda: ag_step(late, 2)],
        },
        (0, "up"): {1: [lambda: ag_step(4, 1)], 3: [lambda: ag_step(3, 2)]},
        (1, "attend"): {2: [lambda: ag_step(4, 2)]},
    }

    att_keeps = [
        pltpu.make_async_copy(qkv, keep_qkv, keep_sem.at[0]),
        pltpu.make_async_copy(pts, keep_pts, keep_sem.at[1]),
    ]
    mlp_keeps = [
        pltpu.make_async_copy(gl, keep_gl, keep_sem.at[2]),
        pltpu.make_async_copy(gp, keep_gp, keep_sem.at[3]),
    ]
    bias_at = 0
    for b in range(BLOCKS):
        off2, off3 = (offs[b, j : j + 1, :].astype(BF16).astype(F32) for j in (2, 3))
        if b > 0:
            first_norm(b)
            for cp in att_keeps:
                cp.wait()
        need(b * parts)

        def attend(t, carry):
            hooks(t, fwd_hooks.get((b, "attend"), {}))
            rows_qkv = dot(aw[b], weight(b, t, 0, c_out))
            for j in range(3):
                part = rows_qkv[:, j * lanes : (j + 1) * lanes]
                if j != 1:
                    at = bias_at + 2 * b + j // 2
                    part = part + sides[t, at : at + 1, 0:lanes].astype(BF16).astype(F32)
                qkv[t, :, j * lanes : (j + 1) * lanes] = part.astype(BF16)

            for w in range(WINS):
                add = rels[t, b].astype(F32) + mask[b, w].astype(F32)
                added[w] = add * LOG2E

            def window(g, c2):
                spots = [pl.ds(pl.multiple_of((g * BATCH + j) * PAD, PAD), PAD) for j in range(BATCH)]
                s = []
                for spot in spots:
                    q = qkv[t, spot, 0:lanes]
                    k = qkv[t, spot, lanes : 2 * lanes]
                    s.append(dot(k, spread(q, heads), NT))
                p = []
                for j in range(BATCH):
                    sj = s[j] * (INV_ROOT * LOG2E) + added[lax.rem(g * BATCH + j, WINS)]
                    e = jnp.exp2(sj - jnp.max(sj, 0, keepdims=True))
                    p.append((e * (1.0 / jnp.sum(e, 0, keepdims=True))).astype(BF16))
                    pts[t, g * BATCH + j] = p[j]
                for j in range(BATCH):
                    v = qkv[t, spots[j], 2 * lanes : 3 * lanes]
                    ow[spots[j], :] = gather_diag(dot(p[j], v, TN), heads).astype(BF16)
                return c2

            lax.fori_loop(0, images * WINS // BATCH, window, 0)
            put_rows(
                osb.at[b, t],
                [dot(perm_t[b, i], ow[i * IMG_PAD : (i + 1) * IMG_PAD, :]) for i in range(images)],
            )
            return carry

        lax.fori_loop(0, groups, attend, 0)
        if b + 1 < BLOCKS:
            start(att_keeps)
        y = dot(osb[b, 0], weight(b, 0, c_out, c_up), NT)
        for t in range(1, groups):
            y = y + dot(osb[b, t], weight(b, t, c_out, c_up), NT)
        ms[b] = xs[b] + y + off2
        norm_into(ms.at[b], a2.at[b], gains[b, 1:2, :], offs[b, 1:2, :])
        if b + 1 < BLOCKS:
            acc[...] = ms[b] + off3
        if b > 0:
            for cp in mlp_keeps:
                cp.wait()
        if b > 0:
            ag_step(b * parts + 1, 3)
        need(b * parts + 1)

        def up(t, carry):
            hooks(t, fwd_hooks.get((b, "up"), {}))
            ubuf[0:rows, :] = dot(a2[b], weight(b, t, c_up, c_down))
            at = bias_at + 2 * BLOCKS + b
            hbias = sides[t, at : at + 1, :].astype(BF16).astype(F32)
            for r, n in chunks(rows, 32):
                g, d = gelu_pair(ubuf[r : r + n, :] + hbias)
                gl[t, r : r + n, :] = g.astype(BF16)
                gp[t, r : r + n, :] = d.astype(BF16)
            return carry

        lax.fori_loop(0, groups, up, 0)
        if b + 1 == BLOCKS:
            break
        ag_step(2, 3)
        need(b * parts + 2)

        def down(t, carry):
            acc[...] += dot(gl[t], weight(b, t, c_down, cols), NT)
            return carry

        lax.fori_loop(0, groups, down, 0)
        start(mlp_keeps)
        xs[b + 1] = acc[...]
        ag_step(3, 3)

    last = BLOCKS - 1
    back_hooks = {
        (1, "mlp"): {3: [lambda: rs_step(1, 2, 1)]},
        (1, "attend"): {2: [lambda: rs_step(1, 1, 2)]},
        (0, "mlp"): {0: [lambda: rs_step(1, 0, 1)], 3: [lambda: rs_step(1, 2, 2)]},
        (0, "attend"): {
            0: [lambda: rs_step(1, 2, 3)],
            1: [lambda: rs_finish(1, 1), lambda: rs_step(1, 0, 3)],
            2: [lambda: rs_step(0, 1, 2)],
            3: [lambda: rs_finish(1, 2)],
        },
    }
    mlp_loads = [
        pltpu.make_async_copy(keep_gl, gl, keep_sem.at[2]),
        pltpu.make_async_copy(keep_gp, gp, keep_sem.at[3]),
    ]
    att_loads = [
        pltpu.make_async_copy(keep_qkv, qkv, keep_sem.at[0]),
        pltpu.make_async_copy(keep_pts, pts, keep_sem.at[1]),
    ]
    for b in range(BLOCKS - 1, -1, -1):
        bias_row = BIAS_ROW + 4 * b
        small[bias_row + 3 : bias_row + 4, :] = column_sum(dx)
        cut[...] = dx[...].astype(BF16)
        dxt = jnp.transpose(cut[...])
        a_t = jnp.transpose(a2[b])
        if b < last:
            for p in range(last * parts, (last + 1) * parts):
                for phase in range(phases):
                    sent(ag_copies(p, phase))
            for cp in mlp_loads:
                cp.wait()

        def down_back(t, carry):
            put_grad(b, t, c_down, cols, dot(dxt, gl[t]))
            return carry

        lax.fori_loop(0, groups, down_back, 0)
        start(rs_copies(b, 2, 0))
        if b == last:
            ag_step(late, 3)
            need(late)
        acc[...] = jnp.zeros_like(acc)

        def mlp_back(t, carry):
            hooks(t, back_hooks.get((b, "mlp"), {}))
            dh = dot(cut[...], weight(b, t, c_down, cols))
            du = (dh * gp[t].astype(F32)).astype(BF16)
            gp[t] = du
            small[pl.ds(HID_ROW + b * groups + t, 1), :] = jnp.sum(
                fold(du.astype(F32)), 0, keepdims=True
            )
            put_grad(b, t, c_up, c_down, dot(a_t, du))
            acc[...] += dot(du, weight(b, t, c_up, c_down), NT)
            return carry

        lax.fori_loop(0, groups, mlp_back, 0)
        start(rs_copies(b, 1, 0))
        if b == last:
            result = ubuf
            off3 = offs[b, 3:4, :].astype(BF16).astype(F32)
            result[0:rows, :] = ms[b] + off3

            def down(t, carry):
                result[0:rows, :] += dot(gl[t], weight(b, t, c_down, cols), NT)
                return carry

            lax.fori_loop(0, groups, down, 0)
            for i in range(images):
                io[i] = result[i * TOKENS : (i + 1) * TOKENS, :]
            x_store = pltpu.make_async_copy(io, xo_hbm, io_sem.at[0])
            x_store.start()
            start(mlp_loads)
            rs_step(1, 1, 1)
        else:
            rs_step(1, 0, 2)
            rs_step(0, 2, 1)
            rs_step(0, 1, 1)
        sums = back_norm(ms.at[b], acc, gains[b, 1:2, :], dx)
        small[GAIN_ROW + 2 * b + 1 : GAIN_ROW + 2 * b + 2, :] = sums[0]
        small[bias_row + 1 : bias_row + 2, :] = sums[1]
        small[bias_row + 2 : bias_row + 3, :] = sums[2]
        cut[...] = dx[...].astype(BF16)
        dmt = jnp.transpose(cut[...])
        awt[...] = jnp.transpose(aw[b])
        da = ubuf
        da[...] = jnp.zeros_like(da)
        for t in range(groups):
            put_grad(b, t, c_out, c_up, dot(dmt, osb[b, t]))
        if b < last:
            for cp in att_loads:
                cp.wait()

        def attend_back(t, carry):
            hooks(t, back_hooks.get((b, "attend"), {}))
            do_t = dot(cut[...], weight(b, t, c_out, c_up)).astype(BF16)
            for i in range(images):
                base = image_base(i)
                ow[i * IMG_PAD : (i + 1) * IMG_PAD, :] = dot(
                    perm[b, i], do_t[base : base + IMG_ROWS]
                ).astype(BF16)
            dsum[...] = jnp.zeros_like(dsum)

            def window(g, c2):
                spots = [pl.ds(pl.multiple_of((g * BATCH + j) * PAD, PAD), PAD) for j in range(BATCH)]
                dob = [spread(ow[spot, :], heads) for spot in spots]
                dp = [dot(qkv[t, spots[j], 2 * lanes : 3 * lanes], dob[j], NT) for j in range(BATCH)]
                ds = []
                for j in range(BATCH):
                    p = pts[t, g * BATCH + j]
                    dv = dot(p, dob[j])
                    dwin[spots[j], 2 * lanes : 3 * lanes] = dv.astype(BF16)
                    pf = p.astype(F32)
                    ds.append((pf * (dp[j] - jnp.sum(pf * dp[j], 0, keepdims=True))).astype(BF16))
                dsum[...] += sum(d.astype(F32) for d in ds)
                for j in range(BATCH):
                    q = qkv[t, spots[j], 0:lanes]
                    k = qkv[t, spots[j], lanes : 2 * lanes]
                    dk = dot(ds[j], spread(q, heads)) * INV_ROOT
                    dwin[spots[j], lanes : 2 * lanes] = dk.astype(BF16)
                    dq = gather_diag(dot(ds[j], k, TN), heads) * INV_ROOT
                    dwin[spots[j], 0:lanes] = dq.astype(BF16)
                return c2

            lax.fori_loop(0, images * WINS // BATCH, window, 0)
            col = pl.ds(pl.multiple_of(t * lanes, lanes), lanes)
            for j in range(2):
                val = dwin[:, 2 * j * lanes : (2 * j + 1) * lanes].astype(F32)
                row = QV_ROW + 2 * b + j
                small[row : row + 1, col] = jnp.sum(fold(val), 0, keepdims=True)
            ds_all = dsum[...]
            high = ds_all.astype(BF16)
            rest_low = (ds_all - high.astype(F32)).astype(BF16)
            wide = sum(
                dot(dot(rel_down[...], piece).astype(BF16), rel_across[...])
                for piece in (high, rest_low)
            )
            skew = wide[0:8]
            for a in range(1, wide.shape[0] // 8):
                skew = skew + pltpu.roll(wide[8 * a : 8 * a + 8], 8 * a, 1)
            row_id = lax.broadcasted_iota(jnp.int32, skew.shape, 0)
            for bit in (1, 2, 4):
                skew = jnp.where((row_id & bit) != 0, pltpu.roll(skew, bit, 1), skew)
            skew = jnp.sum(skew, 0, keepdims=True)
            for h in range(GROUP):
                small[pl.ds(rel_row(groups) + (b * groups + t) * GROUP + h, 1), 0:REL_LANES] = skew[
                    :, h * REL_LANES : (h + 1) * REL_LANES
                ]
            put_grad(b, t, 0, c_out, dot(awt[...], dwin[...]))
            da[...] += dot(dwin[...], weight(b, t, 0, c_out), NT)
            return carry

        lax.fori_loop(0, groups, attend_back, 0)
        start(rs_copies(b, 0, 0))
        if b == last:
            start(att_loads)
            rs_step(1, 1, 3)
        vals = []
        for i in range(images):
            part = da[i * IMG_PAD : (i + 1) * IMG_PAD, :]
            high = part.astype(BF16)
            rest_low = (part - high.astype(F32)).astype(BF16)
            vals.append(dot(perm_t[b, i], high) + dot(perm_t[b, i], rest_low))
        put_rows(acc, vals)
        sums = back_norm(xs.at[b], acc, gains[b, 0:1, :], dx)
        small[GAIN_ROW + 2 * b : GAIN_ROW + 2 * b + 1, :] = sums[0]
        small[bias_row : bias_row + 1, :] = sums[1]
    small_step(0)
    rs_step(0, 0, 1)
    rs_finish(1, 0)
    rs_step(0, 1, 3)
    x_store.wait()
    for i in range(images):
        io[i] = dx[i * TOKENS : (i + 1) * TOKENS, :]
    dx_store = pltpu.make_async_copy(io, dxo_hbm, io_sem.at[1])
    dx_store.start()
    small_step(1)
    rs_step(0, 0, 2)
    rs_step(0, 2, 2)
    small_step(2)
    rs_finish(0, 1)
    rs_step(0, 0, 3)
    rs_step(0, 2, 3)
    small_step(3)
    rs_finish(0, 2)
    small_step(4)
    rs_finish(0, 0)
    dx_store.wait()
    for p in range(last * parts):
        for phase in range(phases):
            sent(ag_copies(p, phase))
    for b in range(BLOCKS):
        for part in range(parts):
            for phase in range(phases):
                sent(rs_copies(b, part, phase))
    for phase in range(phases):
        sent(small_copies(phase))


def block_call(x, ct, counts, mats, rel, qv, hidden, gains, offs, n_fsdp, n_tensor):
    images, _, width = x.shape
    per, lanes = mats[1].shape[1:]
    hid = mats[2].shape[2]
    cols = 4 * lanes + 2 * hid
    parts = cols // PART
    rows = -(-images * TOKENS // 16) * 16
    wrows = images * IMG_PAD
    digits = plan(n_fsdp, n_tensor)
    dims = sorted(digits.values(), key=lambda d: d.dim)
    sizes = tuple(d.size for d in dims)
    most = max(sizes) - 1
    phases = len(dims)
    perm = permutations(images)
    down, across = rel_consts()
    consts = (
        jnp.asarray(np.tile(mask_table(), (1, 1, 1, GROUP)), BF16),
        jnp.asarray(perm, BF16),
        jnp.asarray(np.swapaxes(perm, 2, 3), BF16),
        jnp.asarray(down, BF16),
        jnp.asarray(across, BF16),
    )
    small_rows = rel_row(n_tensor) + BLOCKS * n_tensor * GROUP
    stages = []
    for b, part, h, phase in stage_keys(parts, phases):
        order = reduce_order(digits, b, part, h)
        left = tuple(d.size for d in dims if d not in order[: phase + 1])
        stages.append(pltpu.VMEM((order[phase].size - 1,) + left + (per, HALF), BF16))
    small_order = [digits[n] for n in ("core", "y", "x", "z")]
    vmem = pl.BlockSpec(memory_space=pltpu.VMEM)
    anyspace = pl.BlockSpec(memory_space=pl.ANY)
    keep = [
        (n_tensor, rows, hid), (n_tensor, rows, hid), (n_tensor, wrows, 3 * lanes),
        (n_tensor, images * WINS, PAD, GROUP * PAD),
    ]
    dma = pltpu.SemaphoreType.DMA
    out = pl.pallas_call(
        functools.partial(block_kernel, n_fsdp, n_tensor),
        out_shape=(
            jax.ShapeDtypeStruct(x.shape, F32),
            jax.ShapeDtypeStruct(x.shape, F32),
            jax.ShapeDtypeStruct((BLOCKS, per, cols), F32),
            jax.ShapeDtypeStruct((small_rows, width), F32),
        ) + tuple(jax.ShapeDtypeStruct(s, BF16) for s in keep),
        in_specs=[
            anyspace, anyspace, pl.BlockSpec(memory_space=pltpu.SMEM), anyspace, anyspace, anyspace,
            anyspace,
        ] + [vmem] * 10,
        out_specs=(anyspace, anyspace, vmem, vmem) + (anyspace,) * 4,
        scratch_shapes=[
            pltpu.VMEM((BLOCKS,) + sizes + (per, cols), BF16),
            pltpu.VMEM(sizes + (per, cols), BF16),
            pltpu.VMEM((n_tensor, BLOCKS, PAD, GROUP * PAD), BF16),
            pltpu.VMEM((n_tensor, 8, hid), F32),
            pltpu.VMEM(x.shape, F32),
            pltpu.VMEM((BLOCKS, rows, width), F32),
            pltpu.VMEM((BLOCKS, rows, width), F32),
            pltpu.VMEM((BLOCKS, wrows, width), BF16),
            pltpu.VMEM(keep[2], BF16),
            pltpu.VMEM(keep[3], BF16),
            pltpu.VMEM((wrows, lanes), BF16),
            pltpu.VMEM((BLOCKS, n_tensor, rows, lanes), BF16),
            pltpu.VMEM((BLOCKS, rows, width), BF16),
            pltpu.VMEM(keep[0], BF16),
            pltpu.VMEM(keep[1], BF16),
            pltpu.VMEM((wrows, width), F32),
            pltpu.VMEM((rows, width), F32),
            pltpu.VMEM((rows, width), F32),
            pltpu.VMEM((rows, width), BF16),
            pltpu.VMEM((width, wrows), BF16),
            pltpu.VMEM((wrows, 3 * lanes), BF16),
            pltpu.VMEM((PAD, GROUP * PAD), F32),
            pltpu.VMEM((WINS, PAD, GROUP * PAD), F32),
            pltpu.VMEM((small_rows, width), F32),
        ]
        + stages
        + [pltpu.VMEM((d.size, small_rows, width), F32) for d in small_order]
        + [
            dma((2,)), dma((BLOCKS, 6)), dma((4,)),
            dma((n_tensor - 1,)), dma((n_tensor - 1,)), dma((n_tensor - 1,)), dma((n_tensor - 1,)),
            dma((BLOCKS * parts, 2, phases, most)), dma((BLOCKS * parts, 2, phases, most)),
            dma((BLOCKS, parts, 2, phases, most)), dma((BLOCKS, parts, 2, phases, most)),
            dma((phases, most)), dma((phases, most)),
        ],
        compiler_params=pltpu.CompilerParams(
            has_side_effects=True, vmem_limit_bytes=127 * MIB // 2,
            collective_id=0,
        ),
    )(x, ct, counts, *mats, rel, qv, hidden, consts[0], gains, offs, *consts[1:])
    return out[:4]


def adam_kernel(groups, slot, *refs):
    count = 31
    ins, outs = refs[:count], refs[count : 2 * count - 2]
    held, sem = refs[2 * count - 2 : -1], refs[-1]
    copies = [
        pltpu.make_async_copy(src, dst, sem.at[j]) for j, (src, dst) in enumerate(zip(ins, held))
    ]
    for cp in copies:
        cp.start()
    for cp in copies:
        cp.wait()
    passed = [pltpu.make_async_copy(held[j], outs[j], sem.at[j]) for j in range(2)]
    for cp in passed:
        cp.start()
    gsum, total = held[2:4]
    params = [held[4 + 3 * j : 7 + 3 * j] for j in range(9)]
    news = [outs[2 + 3 * j : 5 + 3 * j] for j in range(9)]
    lanes = GROUP * HEAD_DIM
    hid = params[2][0].shape[2]
    t = slot[0]

    def update(kind, place, grad, rate, decay):
        new = adam(*(p[place] for p in params[kind]), grad, rate, decay)
        for ref, val in zip(news[kind], new):
            ref[place] = val

    for b in range(BLOCKS):
        for j in range(3):
            update(0, (b, j), gsum[b, :, j * lanes : (j + 1) * lanes], MATRIX_RATE, WEIGHT_DECAY)
        update(1, (b,), gsum[b, :, 3 * lanes : 4 * lanes], MATRIX_RATE, WEIGHT_DECAY)
        update(2, (b,), gsum[b, :, 4 * lanes : 4 * lanes + hid], MATRIX_RATE, WEIGHT_DECAY)
        update(3, (b,), gsum[b, :, 4 * lanes + hid :], MATRIX_RATE, WEIGHT_DECAY)
        heads, rels = params[4][0].shape[1:]
        at = rel_row(groups) + b * groups * heads
        hid_at = HID_ROW + b * groups
        qv_rows = slice(QV_ROW + 2 * b, QV_ROW + 2 * b + 2)
        rel = pick(t, [total[at + i * heads : at + (i + 1) * heads, 0:rels] for i in range(groups)])
        qv = pick(t, [total[qv_rows, i * lanes : (i + 1) * lanes] for i in range(groups)])
        hidden = pick(t, [total[hid_at + i : hid_at + i + 1, :] for i in range(groups)])
        update(4, (b,), rel, SMALL_RATE, 0.0)
        update(5, (b,), qv, SMALL_RATE, 0.0)
        update(6, (slice(b, b + 1),), hidden, SMALL_RATE, 0.0)
        update(7, (b,), total[GAIN_ROW + 2 * b : GAIN_ROW + 2 * b + 2, :], SMALL_RATE, 0.0)
        update(8, (b,), total[BIAS_ROW + 4 * b : BIAS_ROW + 4 * b + 4, :], SMALL_RATE, 0.0)
    for cp in passed:
        cp.wait()


def adam_call(x, dx, gsum, total, params, n_tensor):
    flat = [p for group in params for p in group]
    ins = [x, dx, gsum, total] + flat
    hbm = pl.BlockSpec(memory_space=pltpu.HBM)
    vmem = pl.BlockSpec(memory_space=pltpu.VMEM)
    slot = lax.axis_index("tensor").astype(jnp.int32).reshape(1)
    return pl.pallas_call(
        functools.partial(adam_kernel, n_tensor),
        out_shape=tuple(jax.ShapeDtypeStruct(p.shape, p.dtype) for p in [x, dx] + flat),
        in_specs=[pl.BlockSpec(memory_space=pltpu.SMEM)] + [hbm] * len(ins),
        out_specs=(hbm, hbm) + tuple(vmem for _ in flat),
        scratch_shapes=[pltpu.VMEM(p.shape, p.dtype) for p in ins]
        + [pltpu.SemaphoreType.DMA((len(ins),))],
        compiler_params=pltpu.CompilerParams(vmem_limit_bytes=127 * MIB // 2),
    )(slot, *ins)


def shards(n_fsdp, n_tensor, *args):
    image_rows, cotangent, live_counts = args[:3]
    groups = [args[3 + 3 * j : 6 + 3 * j] for j in range(9)]
    turn = {0: lambda p: p.transpose(0, 2, 1, 3), 1: lambda p: p.swapaxes(1, 2), 3: lambda p: p.swapaxes(1, 2)}
    for j, f in turn.items():
        groups[j] = [f(p) for p in groups[j]]
    mats = [g[0] for g in groups[:4]]
    rel, qv, hidden, gain, bias = [g[0] for g in groups[4:]]
    x, dx, gsum, total = block_call(
        image_rows, cotangent, live_counts, mats, rel, qv, hidden, gain, bias, n_fsdp, n_tensor
    )
    new = adam_call(x, dx, gsum, total, groups, n_tensor)
    x, dx = new[:2]
    new = [list(new[2 + 3 * j : 5 + 3 * j]) for j in range(9)]
    for j, f in turn.items():
        new[j] = [f(p) for p in new[j]]
    return (x, dx) + tuple(p for group in new for p in group)
```

```python
import functools
import numpy as np
import jax
import jax.numpy as jnp
from jax import lax
from jax.experimental import pallas as pl
from jax.experimental.pallas import tpu as pltpu
from jax.sharding import PartitionSpec as P
HEAD_DIM = 32
SIDE = 14
WIN = 7
SHIFT = 3
BLOCKS = 2
ADAM_STEP = 10
TOKENS = SIDE * SIDE
WINS = (SIDE // WIN) ** 2
SPAN = WIN * WIN
PAD = 64
IMG_PAD = WINS * PAD
IMG_ROWS = 208
GROUP = 4
NORM_EPS = 1e-05
BETA_ONE = 0.9
BETA_TWO = 0.999
MATRIX_RATE = 0.04
SMALL_RATE = 0.3
WEIGHT_DECAY = 0.05
ADAM_EPS = 1e-08
MASK_FILL = -100.0
KEY_FILL = -1e30
INV_ROOT = HEAD_DIM ** (-0.5)
MIB = 1024 * 1024
F32 = jnp.float32
BF16 = jnp.bfloat16
NT = (((1,), (1,)), ((), ()))
TN = (((0,), (0,)), ((), ()))


def window_source(shifted):
    out = np.zeros((WINS, SPAN), np.int64)
    step = SHIFT if shifted else 0
    per = SIDE // WIN
    for w in range(WINS):
        for p in range(SPAN):
            r = (w // per) * WIN + p // WIN
            c = (w % per) * WIN + p % WIN
            out[w, p] = ((r + step) % SIDE) * SIDE + (c + step) % SIDE
    return out


def image_base(i):
    return (i * TOKENS) // 16 * 16


def permutations(images):
    perm = np.zeros((BLOCKS, images, IMG_PAD, IMG_ROWS), np.float32)
    for b in range(BLOCKS):
        src = window_source(b % 2 == 1)
        for i in range(images):
            off = i * TOKENS - image_base(i)
            for w in range(WINS):
                for p in range(SPAN):
                    perm[b, i, w * PAD + p, off + src[w, p]] = 1.0
    return perm


def mask_table():
    out = np.zeros((BLOCKS, WINS, PAD, PAD), np.float32)
    coords = np.arange(SIDE)
    bands = (coords >= SIDE - WIN).astype(int) + (coords >= SIDE - SHIFT).astype(int)
    region = (bands[:, None] * 3 + bands[None, :]).reshape(-1)
    base = window_source(False)
    for b in range(BLOCKS):
        for w in range(WINS):
            if b % 2 == 1:
                lab = region[base[w]]
                out[b, w, :SPAN, :SPAN] = np.where(lab[:, None] == lab[None, :], 0.0, MASK_FILL)
            out[b, w, SPAN:, :] = KEY_FILL
    return out


def dot(a, b, dims=None):
    if dims is None:
        return jnp.dot(a, b, preferred_element_type=F32)
    return lax.dot_general(a, b, dims, preferred_element_type=F32)


def lane_heads(width):
    return lax.broadcasted_iota(jnp.int32, (1, width), 1) // HEAD_DIM


def spread(rows, heads):
    zero = jnp.zeros_like(rows)
    return jnp.concatenate([jnp.where(heads == h, rows, zero) for h in range(GROUP)], 0)


def gather_diag(prod, heads):
    out = prod[0:PAD]
    for h in range(1, GROUP):
        out = jnp.where(heads == h, prod[h * PAD : (h + 1) * PAD], out)
    return out


def gelu_pair(u):
    au = jnp.abs(u)
    t = 1.0 / (1.0 + (0.3275911 * 0.7071067811865476) * au)
    e = jnp.exp(-0.5 * u * u)
    q = 1.061405429 * 0.5
    q = q * t - 1.453152027 * 0.5
    q = q * t + 1.421413741 * 0.5
    q = q * t - 0.284496736 * 0.5
    q = q * t + 0.254829592 * 0.5
    q = q * t * e
    phi = jnp.where(u >= 0, 1.0 - q, q)
    return u * phi, phi + u * e * 0.3989422804014327


def chunks(rows, size):
    return [(r, min(size, rows - r)) for r in range(0, rows, size)]


def norm_rows(x):
    mean = jnp.mean(x, -1, keepdims=True)
    cen = x - mean
    inv = lax.rsqrt(jnp.mean(cen * cen, -1, keepdims=True) + NORM_EPS)
    return cen * inv, inv


def put_rows(ref, vals):
    images = len(vals)
    for i in range(images):
        base = image_base(i)
        lead = 0
        if i > 0:
            lead = image_base(i - 1) + IMG_ROWS - base
            mix = vals[i - 1][IMG_ROWS - lead :] + vals[i][:lead]
            ref[base : base + lead, :] = mix.astype(ref.dtype)
        end = image_base(i + 1) - base if i + 1 < images else IMG_ROWS
        ref[base + lead : base + end, :] = vals[i][lead:end].astype(ref.dtype)


def norm_into(src, dst, gain, off):
    for r, n in chunks(src.shape[0], 112):
        unit, _ = norm_rows(src[r : r + n, :])
        dst[r : r + n, :] = (unit * gain + off).astype(BF16)


def fold(val):
    rows, cols = val.shape
    return jnp.sum(val.reshape(rows // 8, 8, cols), 0)


def back_norm(src, grad, gain, dst):
    width = src.shape[1]
    sums = [jnp.zeros((8, width), F32) for _ in range(3)]
    for r, n in chunks(src.shape[0], 112):
        unit, inv = norm_rows(src[r : r + n, :])
        gr = grad[r : r + n, :]
        e = gr * gain
        res = dst[r : r + n, :] + inv * (
            e - jnp.mean(e, -1, keepdims=True) - unit * jnp.mean(e * unit, -1, keepdims=True)
        )
        dst[r : r + n, :] = res
        for j, val in enumerate((gr * unit, gr, res)):
            sums[j] = sums[j] + fold(val)
    return [jnp.sum(s, 0, keepdims=True) for s in sums]


def column_sum(ref):
    total = jnp.zeros((8, ref.shape[1]), F32)
    for r, n in chunks(ref.shape[0], 112):
        total = total + fold(ref[r : r + n, :])
    return jnp.sum(total, 0, keepdims=True)
GAIN_ROW = 0
BIAS_ROW = GAIN_ROW + 2 * BLOCKS
QV_ROW = BIAS_ROW + 4 * BLOCKS
HID_ROW = QV_ROW + 2 * BLOCKS
MESH = pl.DeviceIdType.MESH


class Digit:
    def __init__(self, name, axis, size, stride, dim):
        self.name, self.axis, self.size, self.stride, self.dim = name, axis, size, stride, dim

    def here(self):
        return lax.rem(lax.axis_index(self.axis) // self.stride, self.size)

    def peer(self, step):
        d = self.here()
        to = lax.rem(d + step, self.size)
        return to, {self.axis: lax.axis_index(self.axis) + (to - d) * self.stride}


def plan(n_fsdp, n_tensor):
    if (n_fsdp, n_tensor) == (8, 4):
        parts = [("x", "tensor", 2), ("core", "tensor", 2), ("z", "fsdp", 4), ("y", "fsdp", 2)]
    elif (n_fsdp, n_tensor) == (32, 4):
        parts = [("x", "tensor", 4), ("z", "fsdp", 4), ("y", "fsdp", 4), ("core", "fsdp", 2)]
    else:
        parts = [("x", "tensor", n_tensor), ("z", "fsdp", n_fsdp)]
    digits = {}
    for dim, (name, axis, size) in enumerate(parts):
        stride = 1
        for _, later_axis, later in parts[dim + 1 :]:
            if later_axis == axis:
                stride *= later
        digits[name] = Digit(name, axis, size, stride, dim)
    return digits


def orders(digits):
    one = [n for n in ("z", "x", "y", "core") if n in digits]
    two = [n for n in ("z", "y", "x", "core") if n in digits]
    return [[digits[n] for n in one], [digits[n] for n in two]]


def greet(peers):
    barrier = pltpu.get_barrier_semaphore()
    for device in peers:
        pl.semaphore_signal(barrier, inc=1, device_id=device, device_id_type=MESH)
    pl.semaphore_wait(barrier, len(peers))


def tensor_peers(n_tensor):
    t = lax.axis_index("tensor")
    return [{"tensor": lax.rem(t + s, n_tensor)} for s in range(1, n_tensor)]


def all_peers(digits, n_tensor):
    peers = [d.peer(s)[1] for d in digits.values() if d.axis == "fsdp" for s in range(1, d.size)]
    return peers + tensor_peers(n_tensor)


def pieces(cols, width):
    return [(c, min(width, cols - c)) for c in range(0, cols, width)]


def adam(weight, first, second, grad, rate, decay):
    first_new = BETA_ONE * first + (1.0 - BETA_ONE) * grad
    second_new = BETA_TWO * second + (1.0 - BETA_TWO) * grad * grad
    first_hat = first_new * (1.0 / (1.0 - BETA_ONE**ADAM_STEP))
    second_hat = second_new * (1.0 / (1.0 - BETA_TWO**ADAM_STEP))
    step = first_hat / (jnp.sqrt(second_hat) + ADAM_EPS)
    if decay:
        step = step + decay * weight
    return weight - rate * step, first_new, second_new


def pick(index, values):
    out = values[0]
    for i in range(1, len(values)):
        out = jnp.where(index == i, values[i], out)
    return out


def rel_row(groups):
    return HID_ROW + BLOCKS * groups


def solution(mesh):
    n_fsdp, n_tensor = mesh.shape["fsdp"], mesh.shape["tensor"]
    tokens = P(("fsdp", "tensor"), None, None)
    kinds = (
        P(None, "fsdp", None, "tensor"), P(None, "tensor", "fsdp"), P(None, "fsdp", "tensor"),
        P(None, "tensor", "fsdp"), P(None, "tensor", None), P(None, None, "tensor"),
        P(None, "tensor"), P(), P(),
    )
    thrice = tuple(k for k in kinds for _ in range(3))
    return jax.shard_map(
        functools.partial(shards, n_fsdp, n_tensor),
        mesh=mesh,
        in_specs=(tokens, tokens, P("fsdp")) + thrice,
        out_specs=(tokens, tokens) + thrice,
        check_vma=False,
    )
PART = 512
HALF = 256
REL_LANES = 256
BATCH = 12
LOG2E = 1.4426950408889634
Z_FIRST = (("z", "x", "y", "core"), ("z", "y", "x", "core"))
Z_LATE = (("x", "y", "z", "core"), ("y", "x", "z", "core"))
Z_MID = (("x", "z", "y", "core"), ("y", "z", "x", "core"))
GATHER = (
    (0, 0, 256, Z_FIRST),
    (0, 256, 256, Z_FIRST),
    (0, 512, 256, Z_FIRST),
    (0, 768, 256, Z_FIRST),
    (0, 1024, 256, Z_FIRST),
    (0, 1280, 256, Z_FIRST),
    (1, 0, 256, Z_FIRST),
    (1, 256, 256, Z_FIRST),
    (1, 512, 256, Z_LATE),
    (1, 768, 256, Z_FIRST),
    (1, 1024, 256, Z_MID),
    (1, 1280, 256, Z_LATE),
)
REDUCE = (
    (1, 1024, 256, Z_FIRST),
    (1, 1280, 256, Z_LATE),
    (1, 512, 256, Z_FIRST),
    (1, 768, 256, Z_FIRST),
    (1, 0, 256, Z_MID),
    (1, 256, 256, Z_LATE),
    (0, 1024, 256, Z_FIRST),
    (0, 1280, 256, Z_FIRST),
    (0, 512, 256, Z_FIRST),
    (0, 768, 256, Z_FIRST),
    (0, 0, 256, Z_MID),
    (0, 256, 256, Z_FIRST),
)
SCHEDULE = {
    "start": (("ag", 0, 0), ("ag", 1, 0), ("ag", 8, 0), ("ag", 10, 0), ("ag", 11, 0)),
    "x0": (("ag", 2, 0),),
    "dx": (("ag", 3, 0), ("ag", 0, 1), ("ag", 8, 1), ("ag", 11, 1)),
    "need0": (("ag", 4, 0), ("ag", 1, 1), ("ag", 0, 2), ("ag", 5, 0), ("ag", 2, 1), ("ag", 1, 2), ("ag", 6, 0), ("ag", 3, 1), ("ag", 0, 3), ("ag", 7, 0), ("ag", 2, 2), ("ag", 4, 1), ("ag", 8, 2), ("ag", 1, 3), ("ag", 5, 1), ("ag", 3, 2)),
    ("attend0", 1): (("ag", 2, 3), ("ag", 6, 1)),
    ("attend0", 2): (("ag", 4, 2),),
    ("attend0", 3): (("ag", 5, 2),),
    "need1": (("ag", 3, 3), ("ag", 7, 1), ("ag", 9, 0), ("ag", 6, 2)),
    ("up0", 0): (("ag", 10, 1),),
    ("up0", 1): (("ag", 4, 3),),
    ("up0", 3): (("ag", 5, 3),),
    "need2": (("ag", 8, 3), ("ag", 7, 2), ("ag", 11, 2)),
    ("down0", 1): (("ag", 9, 1),),
    ("down0", 2): (("ag", 6, 3),),
    "need3": (("ag", 7, 3), ("ag", 9, 2), ("ag", 10, 2)),
    ("attend1", 3): (("ag", 9, 3),),
    "need4": (("ag", 10, 3),),
    "dxt1": (("ag", 11, 3),),
    "sent12": (("rs", 0, 0), ("rs", 1, 0)),
    ("mlpb1", 2): (("rs", 0, 1), ("rs", 1, 1)),
    "sent11": (("rs", 2, 0), ("rs", 3, 0)),
    ("result1", 1): (("rs", 0, 2),),
    ("result1", 3): (("rs", 2, 1),),
    "lnb1": (("rs", 3, 1),),
    ("attb1", 0): (("rs", 0, 3),),
    ("attb1", 1): (("rs", 2, 2),),
    ("attb1", 2): (("rs", 1, 2), ("rs", 3, 2)),
    ("attb1", 3): (("fin", 0, 0), ("rs", 1, 3), ("rs", 2, 3)),
    "sent10": (("fin", 1, 0), ("rs", 3, 3), ("rs", 4, 0), ("rs", 5, 0)),
    ("downb0", 0): (("fin", 2, 0),),
    ("downb0", 1): (("rs", 4, 1),),
    ("downb0", 2): (("rs", 5, 1),),
    "sent02": (("fin", 3, 0), ("rs", 6, 0), ("rs", 7, 0)),
    ("mlpb0", 2): (("rs", 6, 1), ("rs", 7, 1)),
    ("mlpb0", 3): (("rs", 4, 2),),
    "sent01": (("rs", 8, 0), ("rs", 9, 0)),
    ("attb0", 0): (("rs", 6, 2), ("rs", 8, 1), ("rs", 7, 2), ("rs", 9, 1)),
    ("attb0", 2): (("rs", 5, 2), ("rs", 6, 3)),
    ("attb0", 3): (("rs", 4, 3), ("rs", 7, 3), ("rs", 8, 2)),
    "sent00": (("fin", 6, 0), ("rs", 9, 2), ("rs", 10, 0), ("rs", 11, 0)),
    "ln1b0": (("fin", 4, 0), ("rs", 5, 3)),
    "end0": (("small", 0, 0), ("fin", 7, 0), ("rs", 8, 3), ("rs", 10, 1), ("rs", 9, 3), ("fin", 5, 0), ("small", 0, 1), ("rs", 11, 1)),
    "end": (("fin", 8, 0), ("rs", 10, 2), ("small", 0, 2), ("fin", 9, 0), ("rs", 11, 2), ("small", 0, 3), ("rs", 11, 3), ("rs", 10, 3), ("small", 0, 4), ("fin", 10, 0), ("fin", 11, 0)),
}


def rel_consts():
    side = 2 * WIN - 1
    top = side * (WIN - 1) + WIN - 1
    down = np.zeros((96, PAD), np.float32)
    across = np.zeros((GROUP * PAD, GROUP * REL_LANES), np.float32)
    for i in range(SPAN):
        place = side * (i // WIN) + i % WIN
        down[top - place, i] = 1.0
        for h in range(GROUP):
            across[h * PAD + i, h * REL_LANES + place] = 1.0
    return down, across


def stage_keys(phases):
    return [(q, h, phase) for q in range(len(REDUCE)) for h in range(2) for phase in range(phases)]


def block_kernel(
    n_fsdp, n_tensor,
    x_hbm, ct_hbm, counts, qkv_w, out_w, up_w, down_w, rel_w, qv_w, hid_w, mask, gains, offs, perm, perm_t, rel_down, rel_across,
    xo_hbm, dxo_hbm, gsum, total, keep_gl, keep_gp, keep_qkv, keep_pts,
    wt, dgr, rels, sides, io, xs, ms, aw, qkv, pts, ow, osb, a2, gl, gp, ubuf, acc, dx, cut, awt, dwin, dsum, added, small,
    *rest,
):
    digits = plan(n_fsdp, n_tensor)
    dims = sorted(digits.values(), key=lambda d: d.dim)
    phases = len(dims)
    parts = wt.shape[-1] // PART
    stage = {}
    for at, key in enumerate(stage_keys(phases)):
        stage[key] = rest[at]
    rest = rest[len(stage) :]
    small_slots = rest[:phases]
    (io_sem, own_sem, keep_sem, rel_send, rel_recv, side_send, side_recv, ag_send, ag_recv, rs_send, rs_recv,
     sm_send, sm_recv) = rest[phases:]
    images = io.shape[0]
    groups = n_tensor
    rows, width = xs.shape[1:]
    lanes = GROUP * HEAD_DIM
    hid = gl.shape[2]
    cols = wt.shape[-1]
    c_out, c_up, c_down = 3 * lanes, 4 * lanes, 4 * lanes + hid
    heads = lane_heads(lanes)
    tdims = [d for d in dims if d.axis == "tensor"]
    fdims = [d for d in dims if d.axis == "fsdp"]
    per = wt.shape[-2]
    fshape = tuple(d.size for d in fdims) + (per,)
    t_here = lax.axis_index("tensor")

    def tplace(t):
        return tuple(lax.rem(t // d.stride, d.size) for d in tdims)

    def weight(b, t, lo, hi):
        index = (b,) + tplace(t) + (slice(None),) * len(fshape) + (slice(lo, hi),)
        return wt[index].reshape(width, hi - lo)

    def grad_ref(b):
        return dgr if b == BLOCKS - 1 else wt.at[BLOCKS - 1]

    def put_grad(b, t, lo, hi, value):
        index = tplace(t) + (slice(None),) * len(fshape) + (slice(lo, hi),)
        grad_ref(b)[index] = value.astype(BF16).reshape(fshape + (hi - lo,))

    def ag_copies(p, phase):
        b, c, n, names = GATHER[p]
        out = []
        for h in range(2):
            order = [digits[name] for name in names[h]]
            digit = order[phase]
            at = pl.ds(c + h * (n // 2), n // 2)
            index = tuple(slice(None) if d in order[:phase] else d.here() for d in dims)
            place = wt.at[(b,) + index + (slice(None), at)]
            for s in range(1, digit.size):
                out.append(pltpu.make_async_remote_copy(
                    src_ref=place, dst_ref=place, send_sem=ag_send.at[p, phase],
                    recv_sem=ag_recv.at[p, phase], device_id=digit.peer(s)[1], device_id_type=MESH))
        return out

    def span(ref, order, phase, full, at):
        digit = order[phase]
        index = tuple(
            slice(0, digit.size - 1) if d is digit else slice(None) if d in full else d.here()
            for d in dims
        )
        return ref.at[index + (slice(None), at)]

    def ag_all(p, phase):
        b, c, n, names = GATHER[p]
        order = [digits[name] for name in names[0]]
        place = span(wt.at[b], order, phase, order[:phase], pl.ds(c, n))
        return pltpu.make_async_remote_copy(
            src_ref=place, dst_ref=place, send_sem=ag_send.at[p, phase],
            recv_sem=ag_recv.at[p, phase], device_id=order[phase].peer(1)[1], device_id_type=MESH)

    def start(copies):
        for cp in copies:
            cp.start()

    def arrive(whole):
        whole.wait_recv()

    def sent(whole):
        whole.wait_send()

    def ag_step(p, phase):
        if phase > 0:
            arrive(ag_all(p, phase - 1))
        start(ag_copies(p, phase))

    def need(b, lo, hi):
        for p, (block, c, n, _) in enumerate(GATHER):
            if block == b and c < hi and lo < c + n:
                arrive(ag_all(p, phases - 1))

    def rs_copies(q, phase):
        b, c, n, names = REDUCE[q]
        out = []
        for h in range(2):
            order = [digits[name] for name in names[h]][::-1]
            digit = order[phase]
            at = pl.ds(c + h * (n // 2), n // 2)
            for s in range(1, digit.size):
                to, device = digit.peer(s)
                index = tuple(
                    to if d is digit else d.here() if d in order[:phase] else slice(None) for d in dims
                )
                out.append(pltpu.make_async_remote_copy(
                    src_ref=grad_ref(b).at[index + (slice(None), at)],
                    dst_ref=stage[q, h, phase].at[s - 1],
                    send_sem=rs_send.at[q, phase], recv_sem=rs_recv.at[q, phase],
                    device_id=device, device_id_type=MESH))
        return out

    def rs_all(q, phase):
        b, c, n, names = REDUCE[q]
        order = [digits[name] for name in names[0]][::-1]
        place = span(grad_ref(b), order, phase, order[phase + 1 :], pl.ds(c, n))
        return pltpu.make_async_remote_copy(
            src_ref=place, dst_ref=place, send_sem=rs_send.at[q, phase],
            recv_sem=rs_recv.at[q, phase], device_id=order[phase].peer(1)[1], device_id_type=MESH)

    def rs_absorb(q, phase):
        b, c, n, names = REDUCE[q]
        grad = grad_ref(b)
        for h in range(2):
            order = [digits[name] for name in names[h]][::-1]
            digit = order[phase]
            at = slice(c + h * (n // 2), c + (h + 1) * (n // 2))
            left = [d for d in dims if d not in order[: phase + 1]]
            land = stage[q, h, phase]
            steps = int(np.prod([d.size for d in left])) if left else 1

            def one(i, carry):
                place = {}
                more = i
                for d in reversed(left):
                    place[d.name] = lax.rem(more, d.size)
                    more = more // d.size
                index = tuple(place[d.name] if d in left else d.here() for d in dims)
                value = grad[index + (slice(None), at)]
                for s in range(digit.size - 1):
                    value = value + land[(s,) + tuple(place[d.name] for d in left)]
                grad[index + (slice(None), at)] = value
                return carry

            lax.fori_loop(0, steps, one, 0, unroll=min(steps, 4))

    def rs_step(q, phase):
        if phase > 0:
            arrive(rs_all(q, phase - 1))
            rs_absorb(q, phase - 1)
        start(rs_copies(q, phase))

    def rs_finish(q):
        arrive(rs_all(q, phases - 1))
        b, c, n, names = REDUCE[q]
        for h in range(2):
            at = slice(c + h * (n // 2), c + (h + 1) * (n // 2))
            index = tuple(d.here() for d in dims)
            value = grad_ref(b)[index + (slice(None), at)].astype(F32)
            for s in range(digits[names[h][0]].size - 1):
                value = value + stage[q, h, phases - 1][s].astype(F32)
            gsum[b, :, at] = value

    def slot(name):
        for kind, item, phase in SCHEDULE.get(name, ()):
            if kind == "ag":
                ag_step(item, phase)
            elif kind == "rs":
                rs_step(item, phase)
            elif kind == "fin":
                rs_finish(item)
            else:
                small_step(phase)

    def hooks(t, name):
        for at in range(groups):
            if (name, at) in SCHEDULE:

                @pl.when(t == at)
                def _():
                    slot((name, at))

    small_order = [digits[n] for n in ("core", "y", "x", "z")]

    def small_copies(phase):
        digit = small_order[phase]
        place = small_slots[phase].at[digit.here()]
        return [
            pltpu.make_async_remote_copy(
                src_ref=place, dst_ref=place, send_sem=sm_send.at[phase], recv_sem=sm_recv.at[phase],
                device_id=digit.peer(s)[1], device_id_type=MESH)
            for s in range(1, digit.size)
        ]

    def small_all(phase):
        digit = small_order[phase]
        place = small_slots[phase].at[0 : digit.size - 1]
        return pltpu.make_async_remote_copy(
            src_ref=place, dst_ref=place, send_sem=sm_send.at[phase], recv_sem=sm_recv.at[phase],
            device_id=digit.peer(1)[1], device_id_type=MESH)

    def small_step(phase):
        if phase == 0:
            value = small[...]
        else:
            arrive(small_all(phase - 1))
            value = small_slots[phase - 1][0]
            for s in range(1, small_order[phase - 1].size):
                value = value + small_slots[phase - 1][s]
        if phase < phases:
            small_slots[phase][small_order[phase].here()] = value
            start(small_copies(phase))
        else:
            total[...] = value

    loads = [
        pltpu.make_async_copy(x_hbm, io, io_sem.at[0]),
        pltpu.make_async_copy(ct_hbm, io, io_sem.at[1]),
    ]
    own_copies = []
    for b in range(BLOCKS):
        rows_of = [pl.ds((3 * b + j) * per, per) for j in range(3)]
        pieces_of = [(qkv_w.at[b, j], ubuf.at[rows_of[0], pl.ds(j * lanes, lanes)]) for j in range(3)]
        pieces_of.append((out_w.at[b], ubuf.at[rows_of[0], pl.ds(3 * lanes, lanes)]))
        pieces_of.append((up_w.at[b], ubuf.at[rows_of[1], :]))
        pieces_of.append((down_w.at[b], ubuf.at[rows_of[2], :]))
        own_copies.append([
            pltpu.make_async_copy(src, dst, own_sem.at[b, j]) for j, (src, dst) in enumerate(pieces_of)
        ])
        for cp in own_copies[b]:
            cp.start()
    loads[0].start()
    greet(all_peers(digits, n_tensor))
    mine = tuple(d.here() for d in dims)
    for b in range(BLOCKS):
        for cp in own_copies[b]:
            cp.wait()
        for j in range(parts):
            row = (3 * b + j) * per
            wt[(b,) + mine + (slice(None), slice(j * PART, (j + 1) * PART))] = ubuf[
                row : row + per, :
            ].astype(BF16)

    slot("start")

    rel_count = rel_w.shape[2]
    added[0, 0:8, :] = jnp.zeros((8, GROUP * PAD), F32)
    for b in range(BLOCKS):
        added[0, GROUP * b : GROUP * (b + 1), 0:rel_count] = rel_w[b]
        row = jnp.concatenate(
            [added[0, GROUP * b + h : GROUP * b + h + 1, :] for h in range(GROUP)], 1
        )
        skew = jnp.broadcast_to(row, (8, row.shape[1]))
        row_id = lax.broadcasted_iota(jnp.int32, skew.shape, 0)
        for bit in (1, 2, 4):
            skew = jnp.where((row_id & bit) != 0, pltpu.roll(skew, skew.shape[1] - bit, 1), skew)
        wide = jnp.concatenate(
            [skew]
            + [pltpu.roll(skew, skew.shape[1] - 8 * a, 1) for a in range(1, rel_down.shape[0] // 8)], 0
        )
        wide = dot(rel_down[...], wide.astype(BF16), TN).astype(BF16)
        rels[t_here, b] = dot(wide, rel_across[...], NT).astype(BF16)
        sides[t_here, 2 * b : 2 * b + 2, 0:lanes] = qv_w[b]
    sides[t_here, 2 * BLOCKS : 3 * BLOCKS, :] = hid_w[...]
    side_copies = [
        pltpu.make_async_remote_copy(
            src_ref=ref.at[t_here], dst_ref=ref.at[t_here], send_sem=ssem.at[j], recv_sem=rsem.at[j],
            device_id=device, device_id_type=MESH)
        for ref, ssem, rsem in ((rels, rel_send, rel_recv), (sides, side_send, side_recv))
        for j, device in enumerate(tensor_peers(n_tensor))
    ]
    start(side_copies)
    slot("x0")

    used = images * TOKENS
    floor = used // 8 * 8
    loads[0].wait()
    xs[0, floor:rows, :] = jnp.zeros((rows - floor, width), F32)
    for i in range(images):
        xs[0, i * TOKENS : (i + 1) * TOKENS, :] = io[i]
    loads[1].start()

    def first_norm(b):
        norm_into(xs.at[b], cut, gains[b, 0:1, :], offs[b, 0:1, :])
        for i in range(images):
            base = image_base(i)
            aw[b, i * IMG_PAD : (i + 1) * IMG_PAD, :] = dot(
                perm[b, i], cut[base : base + IMG_ROWS, :]
            ).astype(BF16)

    first_norm(0)
    slot("dx")
    loads[1].wait()
    dx[floor:rows, :] = jnp.zeros((rows - floor, width), F32)
    for i in range(images):
        live = (t_here * images + i < counts[0]).astype(F32)
        dx[i * TOKENS : (i + 1) * TOKENS, :] = io[i] * live
    slot("need0")
    for cp in side_copies:
        cp.wait()

    att_keeps = [
        pltpu.make_async_copy(qkv, keep_qkv, keep_sem.at[0]),
        pltpu.make_async_copy(pts, keep_pts, keep_sem.at[1]),
    ]
    mlp_keeps = [
        pltpu.make_async_copy(gl, keep_gl, keep_sem.at[2]),
        pltpu.make_async_copy(gp, keep_gp, keep_sem.at[3]),
    ]
    bias_at = 0
    for b in range(BLOCKS):
        off2, off3 = (offs[b, j : j + 1, :].astype(BF16).astype(F32) for j in (2, 3))
        if b > 0:
            first_norm(b)
            for cp in att_keeps:
                cp.wait()
        if b > 0:
            slot("need3")
        need(b, 0, c_up)

        def attend(t, carry):
            hooks(t, "attend%d" % b)
            rows_qkv = dot(aw[b], weight(b, t, 0, c_out))
            for j in range(3):
                part = rows_qkv[:, j * lanes : (j + 1) * lanes]
                if j != 1:
                    at = bias_at + 2 * b + j // 2
                    part = part + sides[t, at : at + 1, 0:lanes].astype(BF16).astype(F32)
                qkv[t, :, j * lanes : (j + 1) * lanes] = part.astype(BF16)

            for w in range(WINS):
                add = rels[t, b].astype(F32) + mask[b, w].astype(F32)
                added[w] = add * LOG2E

            def window(g, c2):
                spots = [pl.ds(pl.multiple_of((g * BATCH + j) * PAD, PAD), PAD) for j in range(BATCH)]
                s = []
                for spot in spots:
                    q = qkv[t, spot, 0:lanes]
                    k = qkv[t, spot, lanes : 2 * lanes]
                    s.append(dot(k, spread(q, heads), NT))
                p = []
                for j in range(BATCH):
                    sj = s[j] * (INV_ROOT * LOG2E) + added[lax.rem(g * BATCH + j, WINS)]
                    e = jnp.exp2(sj - jnp.max(sj, 0, keepdims=True))
                    p.append((e * (1.0 / jnp.sum(e, 0, keepdims=True))).astype(BF16))
                    pts[t, g * BATCH + j] = p[j]
                for j in range(BATCH):
                    v = qkv[t, spots[j], 2 * lanes : 3 * lanes]
                    ow[spots[j], :] = gather_diag(dot(p[j], v, TN), heads).astype(BF16)
                return c2

            lax.fori_loop(0, images * WINS // BATCH, window, 0)
            put_rows(
                osb.at[b, t],
                [dot(perm_t[b, i], ow[i * IMG_PAD : (i + 1) * IMG_PAD, :]) for i in range(images)],
            )
            return carry

        lax.fori_loop(0, groups, attend, 0)
        if b + 1 < BLOCKS:
            start(att_keeps)
        slot("out%d" % b)
        y = dot(osb[b, 0], weight(b, 0, c_out, c_up), NT)
        for t in range(1, groups):
            y = y + dot(osb[b, t], weight(b, t, c_out, c_up), NT)
        ms[b] = xs[b] + y + off2
        norm_into(ms.at[b], a2.at[b], gains[b, 1:2, :], offs[b, 1:2, :])
        if b + 1 < BLOCKS:
            acc[...] = ms[b] + off3
        if b > 0:
            for cp in mlp_keeps:
                cp.wait()
        slot("need%d" % (1 + 3 * b))
        need(b, c_up, c_down)

        def up(t, carry):
            hooks(t, "up%d" % b)
            ubuf[0:rows, :] = dot(a2[b], weight(b, t, c_up, c_down))
            at = bias_at + 2 * BLOCKS + b
            hbias = sides[t, at : at + 1, :].astype(BF16).astype(F32)
            for r, n in chunks(rows, 32):
                g, d = gelu_pair(ubuf[r : r + n, :] + hbias)
                gl[t, r : r + n, :] = g.astype(BF16)
                gp[t, r : r + n, :] = d.astype(BF16)
            return carry

        lax.fori_loop(0, groups, up, 0)
        if b + 1 == BLOCKS:
            break
        slot("need2")
        need(b, c_down, cols)

        def down(t, carry):
            hooks(t, "down0")
            acc[...] += dot(gl[t], weight(b, t, c_down, cols), NT)
            return carry

        lax.fori_loop(0, groups, down, 0)
        start(mlp_keeps)
        xs[b + 1] = acc[...]
        slot("norm1")

    last = BLOCKS - 1
    mlp_loads = [
        pltpu.make_async_copy(keep_gl, gl, keep_sem.at[2]),
        pltpu.make_async_copy(keep_gp, gp, keep_sem.at[3]),
    ]
    att_loads = [
        pltpu.make_async_copy(keep_qkv, qkv, keep_sem.at[0]),
        pltpu.make_async_copy(keep_pts, pts, keep_sem.at[1]),
    ]
    for b in range(BLOCKS - 1, -1, -1):
        bias_row = BIAS_ROW + 4 * b
        small[bias_row + 3 : bias_row + 4, :] = column_sum(dx)
        cut[...] = dx[...].astype(BF16)
        slot("dxt%d" % b)
        dxt = jnp.transpose(cut[...])
        a_t = jnp.transpose(a2[b])
        if b < last:
            for p in range(len(GATHER)):
                if GATHER[p][0] == last:
                    for phase in range(phases):
                        sent(ag_all(p, phase))
            for cp in mlp_loads:
                cp.wait()

        def down_back(t, carry):
            hooks(t, "downb%d" % b)
            put_grad(b, t, c_down, cols, dot(dxt, gl[t]))
            return carry

        lax.fori_loop(0, groups, down_back, 0)
        slot("sent%d2" % b)
        if b == last:
            slot("need5")
            need(b, c_down, cols)
        acc[...] = jnp.zeros_like(acc)

        def mlp_back(t, carry):
            hooks(t, "mlpb%d" % b)
            dh = dot(cut[...], weight(b, t, c_down, cols))
            du = (dh * gp[t].astype(F32)).astype(BF16)
            gp[t] = du
            small[pl.ds(HID_ROW + b * groups + t, 1), :] = jnp.sum(
                fold(du.astype(F32)), 0, keepdims=True
            )
            put_grad(b, t, c_up, c_down, dot(a_t, du))
            acc[...] += dot(du, weight(b, t, c_up, c_down), NT)
            return carry

        lax.fori_loop(0, groups, mlp_back, 0)
        slot("sent%d1" % b)
        if b == last:
            slot("result")
            result = ubuf
            off3 = offs[b, 3:4, :].astype(BF16).astype(F32)
            result[0:rows, :] = ms[b] + off3

            def down(t, carry):
                hooks(t, "result1")
                result[0:rows, :] += dot(gl[t], weight(b, t, c_down, cols), NT)
                return carry

            lax.fori_loop(0, groups, down, 0)
            for i in range(images):
                io[i] = result[i * TOKENS : (i + 1) * TOKENS, :]
            x_store = pltpu.make_async_copy(io, xo_hbm, io_sem.at[0])
            x_store.start()
            start(mlp_loads)
        slot("lnb%d" % b)
        sums = back_norm(ms.at[b], acc, gains[b, 1:2, :], dx)
        small[GAIN_ROW + 2 * b + 1 : GAIN_ROW + 2 * b + 2, :] = sums[0]
        small[bias_row + 1 : bias_row + 2, :] = sums[1]
        small[bias_row + 2 : bias_row + 3, :] = sums[2]
        cut[...] = dx[...].astype(BF16)
        dmt = jnp.transpose(cut[...])
        awt[...] = jnp.transpose(aw[b])
        da = ubuf
        da[...] = jnp.zeros_like(da)
        for t in range(groups):
            put_grad(b, t, c_out, c_up, dot(dmt, osb[b, t]))
        if b < last:
            for cp in att_loads:
                cp.wait()

        def attend_back(t, carry):
            hooks(t, "attb%d" % b)
            do_t = dot(cut[...], weight(b, t, c_out, c_up)).astype(BF16)
            for i in range(images):
                base = image_base(i)
                ow[i * IMG_PAD : (i + 1) * IMG_PAD, :] = dot(
                    perm[b, i], do_t[base : base + IMG_ROWS]
                ).astype(BF16)
            dsum[...] = jnp.zeros_like(dsum)

            def window(g, c2):
                spots = [pl.ds(pl.multiple_of((g * BATCH + j) * PAD, PAD), PAD) for j in range(BATCH)]
                dob = [spread(ow[spot, :], heads) for spot in spots]
                dp = [dot(qkv[t, spots[j], 2 * lanes : 3 * lanes], dob[j], NT) for j in range(BATCH)]
                ds = []
                for j in range(BATCH):
                    p = pts[t, g * BATCH + j]
                    dv = dot(p, dob[j])
                    dwin[spots[j], 2 * lanes : 3 * lanes] = dv.astype(BF16)
                    pf = p.astype(F32)
                    ds.append((pf * (dp[j] - jnp.sum(pf * dp[j], 0, keepdims=True))).astype(BF16))
                dsum[...] += sum(d.astype(F32) for d in ds)
                for j in range(BATCH):
                    q = qkv[t, spots[j], 0:lanes]
                    k = qkv[t, spots[j], lanes : 2 * lanes]
                    dk = dot(ds[j], spread(q, heads)) * INV_ROOT
                    dwin[spots[j], lanes : 2 * lanes] = dk.astype(BF16)
                    dq = gather_diag(dot(ds[j], k, TN), heads) * INV_ROOT
                    dwin[spots[j], 0:lanes] = dq.astype(BF16)
                return c2

            lax.fori_loop(0, images * WINS // BATCH, window, 0)
            col = pl.ds(pl.multiple_of(t * lanes, lanes), lanes)
            for j in range(2):
                val = dwin[:, 2 * j * lanes : (2 * j + 1) * lanes].astype(F32)
                row = QV_ROW + 2 * b + j
                small[row : row + 1, col] = jnp.sum(fold(val), 0, keepdims=True)
            ds_all = dsum[...]
            high = ds_all.astype(BF16)
            rest_low = (ds_all - high.astype(F32)).astype(BF16)
            wide = sum(
                dot(dot(rel_down[...], piece).astype(BF16), rel_across[...])
                for piece in (high, rest_low)
            )
            skew = wide[0:8]
            for a in range(1, wide.shape[0] // 8):
                skew = skew + pltpu.roll(wide[8 * a : 8 * a + 8], 8 * a, 1)
            row_id = lax.broadcasted_iota(jnp.int32, skew.shape, 0)
            for bit in (1, 2, 4):
                skew = jnp.where((row_id & bit) != 0, pltpu.roll(skew, bit, 1), skew)
            skew = jnp.sum(skew, 0, keepdims=True)
            for h in range(GROUP):
                small[pl.ds(rel_row(groups) + (b * groups + t) * GROUP + h, 1), 0:REL_LANES] = skew[
                    :, h * REL_LANES : (h + 1) * REL_LANES
                ]
            put_grad(b, t, 0, c_out, dot(awt[...], dwin[...]))
            da[...] += dot(dwin[...], weight(b, t, 0, c_out), NT)
            return carry

        lax.fori_loop(0, groups, attend_back, 0)
        slot("sent%d0" % b)
        if b == last:
            start(att_loads)
        slot("ln1b%d" % b)
        vals = []
        for i in range(images):
            part = da[i * IMG_PAD : (i + 1) * IMG_PAD, :]
            high = part.astype(BF16)
            rest_low = (part - high.astype(F32)).astype(BF16)
            vals.append(dot(perm_t[b, i], high) + dot(perm_t[b, i], rest_low))
        put_rows(acc, vals)
        sums = back_norm(xs.at[b], acc, gains[b, 0:1, :], dx)
        small[GAIN_ROW + 2 * b : GAIN_ROW + 2 * b + 1, :] = sums[0]
        small[bias_row : bias_row + 1, :] = sums[1]
    slot("end0")
    x_store.wait()
    for i in range(images):
        io[i] = dx[i * TOKENS : (i + 1) * TOKENS, :]
    dx_store = pltpu.make_async_copy(io, dxo_hbm, io_sem.at[1])
    dx_store.start()
    slot("end")
    dx_store.wait()
    for p in range(len(GATHER)):
        if GATHER[p][0] != last:
            for phase in range(phases):
                sent(ag_all(p, phase))
    for q in range(len(REDUCE)):
        for phase in range(phases):
            sent(rs_all(q, phase))
    for phase in range(phases):
        sent(small_all(phase))


def block_call(x, ct, counts, mats, rel, qv, hidden, gains, offs, n_fsdp, n_tensor):
    images, _, width = x.shape
    per, lanes = mats[1].shape[1:]
    hid = mats[2].shape[2]
    cols = 4 * lanes + 2 * hid
    parts = cols // PART
    rows = -(-images * TOKENS // 16) * 16
    wrows = images * IMG_PAD
    digits = plan(n_fsdp, n_tensor)
    dims = sorted(digits.values(), key=lambda d: d.dim)
    sizes = tuple(d.size for d in dims)
    phases = len(dims)
    perm = permutations(images)
    down, across = rel_consts()
    consts = (
        jnp.asarray(np.tile(mask_table(), (1, 1, 1, GROUP)), BF16),
        jnp.asarray(perm, BF16),
        jnp.asarray(np.swapaxes(perm, 2, 3), BF16),
        jnp.asarray(down, BF16),
        jnp.asarray(across, BF16),
    )
    small_rows = rel_row(n_tensor) + BLOCKS * n_tensor * GROUP
    stages = []
    for q, h, phase in stage_keys(phases):
        order = [digits[n] for n in REDUCE[q][3][h]][::-1]
        left = tuple(d.size for d in dims if d not in order[: phase + 1])
        stages.append(pltpu.VMEM((order[phase].size - 1,) + left + (per, REDUCE[q][2] // 2), BF16))
    small_order = [digits[n] for n in ("core", "y", "x", "z")]
    vmem = pl.BlockSpec(memory_space=pltpu.VMEM)
    anyspace = pl.BlockSpec(memory_space=pl.ANY)
    keep = [
        (n_tensor, rows, hid), (n_tensor, rows, hid), (n_tensor, wrows, 3 * lanes),
        (n_tensor, images * WINS, PAD, GROUP * PAD),
    ]
    dma = pltpu.SemaphoreType.DMA
    out = pl.pallas_call(
        functools.partial(block_kernel, n_fsdp, n_tensor),
        out_shape=(
            jax.ShapeDtypeStruct(x.shape, F32),
            jax.ShapeDtypeStruct(x.shape, F32),
            jax.ShapeDtypeStruct((BLOCKS, per, cols), F32),
            jax.ShapeDtypeStruct((small_rows, width), F32),
        ) + tuple(jax.ShapeDtypeStruct(s, BF16) for s in keep),
        in_specs=[
            anyspace, anyspace, pl.BlockSpec(memory_space=pltpu.SMEM), anyspace, anyspace, anyspace,
            anyspace,
        ] + [vmem] * 10,
        out_specs=(anyspace, anyspace, vmem, vmem) + (anyspace,) * 4,
        scratch_shapes=[
            pltpu.VMEM((BLOCKS,) + sizes + (per, cols), BF16),
            pltpu.VMEM(sizes + (per, cols), BF16),
            pltpu.VMEM((n_tensor, BLOCKS, PAD, GROUP * PAD), BF16),
            pltpu.VMEM((n_tensor, 8, hid), F32),
            pltpu.VMEM(x.shape, F32),
            pltpu.VMEM((BLOCKS, rows, width), F32),
            pltpu.VMEM((BLOCKS, rows, width), F32),
            pltpu.VMEM((BLOCKS, wrows, width), BF16),
            pltpu.VMEM(keep[2], BF16),
            pltpu.VMEM(keep[3], BF16),
            pltpu.VMEM((wrows, lanes), BF16),
            pltpu.VMEM((BLOCKS, n_tensor, rows, lanes), BF16),
            pltpu.VMEM((BLOCKS, rows, width), BF16),
            pltpu.VMEM(keep[0], BF16),
            pltpu.VMEM(keep[1], BF16),
            pltpu.VMEM((wrows, width), F32),
            pltpu.VMEM((rows, width), F32),
            pltpu.VMEM((rows, width), F32),
            pltpu.VMEM((rows, width), BF16),
            pltpu.VMEM((width, wrows), BF16),
            pltpu.VMEM((wrows, 3 * lanes), BF16),
            pltpu.VMEM((PAD, GROUP * PAD), F32),
            pltpu.VMEM((WINS, PAD, GROUP * PAD), F32),
            pltpu.VMEM((small_rows, width), F32),
        ]
        + stages
        + [pltpu.VMEM((d.size, small_rows, width), F32) for d in small_order]
        + [
            dma((2,)), dma((BLOCKS, 6)), dma((4,)),
            dma((n_tensor - 1,)), dma((n_tensor - 1,)), dma((n_tensor - 1,)), dma((n_tensor - 1,)),
            dma((len(GATHER), phases)), dma((len(GATHER), phases)),
            dma((len(REDUCE), phases)), dma((len(REDUCE), phases)),
            dma((phases,)), dma((phases,)),
        ],
        compiler_params=pltpu.CompilerParams(
            has_side_effects=True, vmem_limit_bytes=127 * MIB // 2,
            collective_id=0,
        ),
    )(x, ct, counts, *mats, rel, qv, hidden, consts[0], gains, offs, *consts[1:])
    return out[:4]


def adam_kernel(groups, slot, *refs):
    count = 31
    ins, outs = refs[:count], refs[count : 2 * count - 2]
    held, sem = refs[2 * count - 2 : -1], refs[-1]
    copies = [
        pltpu.make_async_copy(src, dst, sem.at[j]) for j, (src, dst) in enumerate(zip(ins, held))
    ]
    for cp in copies:
        cp.start()
    for cp in copies:
        cp.wait()
    passed = [pltpu.make_async_copy(held[j], outs[j], sem.at[j]) for j in range(2)]
    for cp in passed:
        cp.start()
    gsum, total = held[2:4]
    params = [held[4 + 3 * j : 7 + 3 * j] for j in range(9)]
    news = [outs[2 + 3 * j : 5 + 3 * j] for j in range(9)]
    lanes = GROUP * HEAD_DIM
    hid = params[2][0].shape[2]
    t = slot[0]

    def update(kind, place, grad, rate, decay):
        new = adam(*(p[place] for p in params[kind]), grad, rate, decay)
        for ref, val in zip(news[kind], new):
            ref[place] = val

    for b in range(BLOCKS):
        for j in range(3):
            update(0, (b, j), gsum[b, :, j * lanes : (j + 1) * lanes], MATRIX_RATE, WEIGHT_DECAY)
        update(1, (b,), gsum[b, :, 3 * lanes : 4 * lanes], MATRIX_RATE, WEIGHT_DECAY)
        update(2, (b,), gsum[b, :, 4 * lanes : 4 * lanes + hid], MATRIX_RATE, WEIGHT_DECAY)
        update(3, (b,), gsum[b, :, 4 * lanes + hid :], MATRIX_RATE, WEIGHT_DECAY)
        heads, rels = params[4][0].shape[1:]
        at = rel_row(groups) + b * groups * heads
        hid_at = HID_ROW + b * groups
        qv_rows = slice(QV_ROW + 2 * b, QV_ROW + 2 * b + 2)
        rel = pick(t, [total[at + i * heads : at + (i + 1) * heads, 0:rels] for i in range(groups)])
        qv = pick(t, [total[qv_rows, i * lanes : (i + 1) * lanes] for i in range(groups)])
        hidden = pick(t, [total[hid_at + i : hid_at + i + 1, :] for i in range(groups)])
        update(4, (b,), rel, SMALL_RATE, 0.0)
        update(5, (b,), qv, SMALL_RATE, 0.0)
        update(6, (slice(b, b + 1),), hidden, SMALL_RATE, 0.0)
        update(7, (b,), total[GAIN_ROW + 2 * b : GAIN_ROW + 2 * b + 2, :], SMALL_RATE, 0.0)
        update(8, (b,), total[BIAS_ROW + 4 * b : BIAS_ROW + 4 * b + 4, :], SMALL_RATE, 0.0)
    for cp in passed:
        cp.wait()


def adam_call(x, dx, gsum, total, params, n_tensor):
    flat = [p for group in params for p in group]
    ins = [x, dx, gsum, total] + flat
    hbm = pl.BlockSpec(memory_space=pltpu.HBM)
    vmem = pl.BlockSpec(memory_space=pltpu.VMEM)
    slot = lax.axis_index("tensor").astype(jnp.int32).reshape(1)
    return pl.pallas_call(
        functools.partial(adam_kernel, n_tensor),
        out_shape=tuple(jax.ShapeDtypeStruct(p.shape, p.dtype) for p in [x, dx] + flat),
        in_specs=[pl.BlockSpec(memory_space=pltpu.SMEM)] + [hbm] * len(ins),
        out_specs=(hbm, hbm) + tuple(vmem for _ in flat),
        scratch_shapes=[pltpu.VMEM(p.shape, p.dtype) for p in ins]
        + [pltpu.SemaphoreType.DMA((len(ins),))],
        compiler_params=pltpu.CompilerParams(vmem_limit_bytes=127 * MIB // 2),
    )(slot, *ins)


def shards(n_fsdp, n_tensor, *args):
    image_rows, cotangent, live_counts = args[:3]
    groups = [args[3 + 3 * j : 6 + 3 * j] for j in range(9)]
    turn = {0: lambda p: p.transpose(0, 2, 1, 3), 1: lambda p: p.swapaxes(1, 2), 3: lambda p: p.swapaxes(1, 2)}
    for j, f in turn.items():
        groups[j] = [f(p) for p in groups[j]]
    mats = [g[0] for g in groups[:4]]
    rel, qv, hidden, gain, bias = [g[0] for g in groups[4:]]
    x, dx, gsum, total = block_call(
        image_rows, cotangent, live_counts, mats, rel, qv, hidden, gain, bias, n_fsdp, n_tensor
    )
    new = adam_call(x, dx, gsum, total, groups, n_tensor)
    x, dx = new[:2]
    new = [list(new[2 + 3 * j : 5 + 3 * j]) for j in range(9)]
    for j, f in turn.items():
        new[j] = [f(p) for p in new[j]]
    return (x, dx) + tuple(p for group in new for p in group)
```

```python
import functools
import numpy as np
import jax
import jax.numpy as jnp
from jax import lax
from jax.experimental import pallas as pl
from jax.experimental.pallas import tpu as pltpu
from jax.sharding import PartitionSpec as P
HEAD_DIM = 32
SIDE = 14
WIN = 7
SHIFT = 3
BLOCKS = 2
ADAM_STEP = 10
TOKENS = SIDE * SIDE
WINS = (SIDE // WIN) ** 2
SPAN = WIN * WIN
PAD = 64
IMG_PAD = WINS * PAD
IMG_ROWS = 208
GROUP = 4
NORM_EPS = 1e-05
BETA_ONE = 0.9
BETA_TWO = 0.999
MATRIX_RATE = 0.04
SMALL_RATE = 0.3
WEIGHT_DECAY = 0.05
ADAM_EPS = 1e-08
MASK_FILL = -100.0
KEY_FILL = -1e30
INV_ROOT = HEAD_DIM ** (-0.5)
MIB = 1024 * 1024
F32 = jnp.float32
BF16 = jnp.bfloat16
NT = (((1,), (1,)), ((), ()))
TN = (((0,), (0,)), ((), ()))


def window_source(shifted):
    out = np.zeros((WINS, SPAN), np.int64)
    step = SHIFT if shifted else 0
    per = SIDE // WIN
    for w in range(WINS):
        for p in range(SPAN):
            r = (w // per) * WIN + p // WIN
            c = (w % per) * WIN + p % WIN
            out[w, p] = ((r + step) % SIDE) * SIDE + (c + step) % SIDE
    return out


def image_base(i):
    return (i * TOKENS) // 16 * 16


def permutations(images):
    perm = np.zeros((BLOCKS, images, IMG_PAD, IMG_ROWS), np.float32)
    for b in range(BLOCKS):
        src = window_source(b % 2 == 1)
        for i in range(images):
            off = i * TOKENS - image_base(i)
            for w in range(WINS):
                for p in range(SPAN):
                    perm[b, i, w * PAD + p, off + src[w, p]] = 1.0
    return perm


def mask_table():
    out = np.zeros((BLOCKS, WINS, PAD, PAD), np.float32)
    coords = np.arange(SIDE)
    bands = (coords >= SIDE - WIN).astype(int) + (coords >= SIDE - SHIFT).astype(int)
    region = (bands[:, None] * 3 + bands[None, :]).reshape(-1)
    base = window_source(False)
    for b in range(BLOCKS):
        for w in range(WINS):
            if b % 2 == 1:
                lab = region[base[w]]
                out[b, w, :SPAN, :SPAN] = np.where(lab[:, None] == lab[None, :], 0.0, MASK_FILL)
            out[b, w, SPAN:, :] = KEY_FILL
    return out


def dot(a, b, dims=None):
    if dims is None:
        return jnp.dot(a, b, preferred_element_type=F32)
    return lax.dot_general(a, b, dims, preferred_element_type=F32)


def lane_heads(width):
    return lax.broadcasted_iota(jnp.int32, (1, width), 1) // HEAD_DIM


def spread(rows, heads):
    zero = jnp.zeros_like(rows)
    return jnp.concatenate([jnp.where(heads == h, rows, zero) for h in range(GROUP)], 0)


def gather_diag(prod, heads):
    out = prod[0:PAD]
    for h in range(1, GROUP):
        out = jnp.where(heads == h, prod[h * PAD : (h + 1) * PAD], out)
    return out


def gelu_pair(u):
    au = jnp.abs(u)
    t = 1.0 / (1.0 + (0.3275911 * 0.7071067811865476) * au)
    e = jnp.exp(-0.5 * u * u)
    q = 1.061405429 * 0.5
    q = q * t - 1.453152027 * 0.5
    q = q * t + 1.421413741 * 0.5
    q = q * t - 0.284496736 * 0.5
    q = q * t + 0.254829592 * 0.5
    q = q * t * e
    phi = jnp.where(u >= 0, 1.0 - q, q)
    return u * phi, phi + u * e * 0.3989422804014327


def chunks(rows, size):
    return [(r, min(size, rows - r)) for r in range(0, rows, size)]


def norm_rows(x):
    mean = jnp.mean(x, -1, keepdims=True)
    cen = x - mean
    inv = lax.rsqrt(jnp.mean(cen * cen, -1, keepdims=True) + NORM_EPS)
    return cen * inv, inv


def put_rows(ref, vals):
    images = len(vals)
    for i in range(images):
        base = image_base(i)
        lead = 0
        if i > 0:
            lead = image_base(i - 1) + IMG_ROWS - base
            mix = vals[i - 1][IMG_ROWS - lead :] + vals[i][:lead]
            ref[base : base + lead, :] = mix.astype(ref.dtype)
        end = image_base(i + 1) - base if i + 1 < images else IMG_ROWS
        ref[base + lead : base + end, :] = vals[i][lead:end].astype(ref.dtype)


def norm_into(src, dst, gain, off):
    for r, n in chunks(src.shape[0], 112):
        unit, _ = norm_rows(src[r : r + n, :])
        dst[r : r + n, :] = (unit * gain + off).astype(BF16)


def fold(val):
    rows, cols = val.shape
    return jnp.sum(val.reshape(rows // 8, 8, cols), 0)


def back_norm(src, grad, gain, dst):
    width = src.shape[1]
    sums = [jnp.zeros((8, width), F32) for _ in range(3)]
    for r, n in chunks(src.shape[0], 112):
        unit, inv = norm_rows(src[r : r + n, :])
        gr = grad[r : r + n, :]
        e = gr * gain
        res = dst[r : r + n, :] + inv * (
            e - jnp.mean(e, -1, keepdims=True) - unit * jnp.mean(e * unit, -1, keepdims=True)
        )
        dst[r : r + n, :] = res
        for j, val in enumerate((gr * unit, gr, res)):
            sums[j] = sums[j] + fold(val)
    return [jnp.sum(s, 0, keepdims=True) for s in sums]


def column_sum(ref):
    total = jnp.zeros((8, ref.shape[1]), F32)
    for r, n in chunks(ref.shape[0], 112):
        total = total + fold(ref[r : r + n, :])
    return jnp.sum(total, 0, keepdims=True)
GAIN_ROW = 0
BIAS_ROW = GAIN_ROW + 2 * BLOCKS
QV_ROW = BIAS_ROW + 4 * BLOCKS
HID_ROW = QV_ROW + 2 * BLOCKS
MESH = pl.DeviceIdType.MESH


class Digit:
    def __init__(self, name, axis, size, stride, dim):
        self.name, self.axis, self.size, self.stride, self.dim = name, axis, size, stride, dim

    def here(self):
        return lax.rem(lax.axis_index(self.axis) // self.stride, self.size)

    def peer(self, step):
        d = self.here()
        to = lax.rem(d + step, self.size)
        return to, {self.axis: lax.axis_index(self.axis) + (to - d) * self.stride}


def plan(n_fsdp, n_tensor):
    if (n_fsdp, n_tensor) == (8, 4):
        parts = [("x", "tensor", 2), ("core", "tensor", 2), ("z", "fsdp", 4), ("y", "fsdp", 2)]
    elif (n_fsdp, n_tensor) == (32, 4):
        parts = [("x", "tensor", 4), ("z", "fsdp", 4), ("y", "fsdp", 4), ("core", "fsdp", 2)]
    else:
        parts = [("x", "tensor", n_tensor), ("z", "fsdp", n_fsdp)]
    digits = {}
    for dim, (name, axis, size) in enumerate(parts):
        stride = 1
        for _, later_axis, later in parts[dim + 1 :]:
            if later_axis == axis:
                stride *= later
        digits[name] = Digit(name, axis, size, stride, dim)
    return digits


def orders(digits):
    one = [n for n in ("z", "x", "y", "core") if n in digits]
    two = [n for n in ("z", "y", "x", "core") if n in digits]
    return [[digits[n] for n in one], [digits[n] for n in two]]


def greet(peers):
    barrier = pltpu.get_barrier_semaphore()
    for device in peers:
        pl.semaphore_signal(barrier, inc=1, device_id=device, device_id_type=MESH)
    pl.semaphore_wait(barrier, len(peers))


def tensor_peers(n_tensor):
    t = lax.axis_index("tensor")
    return [{"tensor": lax.rem(t + s, n_tensor)} for s in range(1, n_tensor)]


def all_peers(digits, n_tensor):
    peers = [d.peer(s)[1] for d in digits.values() if d.axis == "fsdp" for s in range(1, d.size)]
    return peers + tensor_peers(n_tensor)


def pieces(cols, width):
    return [(c, min(width, cols - c)) for c in range(0, cols, width)]


def adam(weight, first, second, grad, rate, decay):
    first_new = BETA_ONE * first + (1.0 - BETA_ONE) * grad
    second_new = BETA_TWO * second + (1.0 - BETA_TWO) * grad * grad
    first_hat = first_new * (1.0 / (1.0 - BETA_ONE**ADAM_STEP))
    second_hat = second_new * (1.0 / (1.0 - BETA_TWO**ADAM_STEP))
    step = first_hat / (jnp.sqrt(second_hat) + ADAM_EPS)
    if decay:
        step = step + decay * weight
    return weight - rate * step, first_new, second_new


def solution(mesh):
    n_fsdp, n_tensor = mesh.shape["fsdp"], mesh.shape["tensor"]
    tokens = P(("fsdp", "tensor"), None, None)
    kinds = (
        P(None, "fsdp", None, "tensor"), P(None, "tensor", "fsdp"), P(None, "fsdp", "tensor"),
        P(None, "tensor", "fsdp"), P(None, "tensor", None), P(None, None, "tensor"),
        P(None, "tensor"), P(), P(),
    )
    thrice = tuple(k for k in kinds for _ in range(3))
    return jax.shard_map(
        functools.partial(shards, n_fsdp, n_tensor),
        mesh=mesh,
        in_specs=(tokens, tokens, P("fsdp")) + thrice,
        out_specs=(tokens, tokens) + thrice,
        check_vma=False,
    )
PART = 512
HALF = 256
REL_LANES = 256
BATCH = 12
ABS_UNROLL = 16
LOG2E = 1.4426950408889634
Z_FIRST = (("z", "x", "y", "core"), ("z", "y", "x", "core"))
Z_LATE = (("x", "y", "z", "core"), ("y", "x", "z", "core"))
Z_MID = (("x", "z", "y", "core"), ("y", "z", "x", "core"))
GATHER = (
    (0, 0, 256, Z_FIRST),
    (0, 256, 256, Z_FIRST),
    (0, 512, 256, Z_FIRST),
    (0, 768, 256, Z_FIRST),
    (0, 1024, 256, Z_FIRST),
    (0, 1280, 256, Z_FIRST),
    (1, 0, 256, Z_FIRST),
    (1, 256, 256, Z_MID),
    (1, 512, 256, Z_FIRST),
    (1, 768, 256, Z_MID),
    (1, 1024, 256, Z_MID),
    (1, 1280, 256, Z_MID),
)
REDUCE = (
    (1, 1024, 256, Z_MID),
    (1, 1280, 256, Z_MID),
    (1, 512, 256, Z_FIRST),
    (1, 768, 256, Z_FIRST),
    (1, 384, 128, Z_FIRST[:1]),
    (1, 0, 256, Z_FIRST),
    (1, 256, 128, Z_FIRST[1:]),
    (0, 1024, 256, Z_FIRST),
    (0, 1280, 256, Z_LATE),
    (0, 512, 256, Z_FIRST),
    (0, 768, 256, Z_FIRST),
    (0, 384, 128, Z_FIRST[:1]),
    (0, 0, 256, Z_FIRST),
    (0, 256, 128, Z_FIRST[1:]),
)
SCHEDULE = {
    "start0": (("ag", 0, 0),),
    "start1": (("ag", 7, 0), ("ag", 9, 0), ("ag", 10, 0), ("ag", 11, 0), ("ag", 1, 0)),
    "dx": (("ag", 2, 0),),
    "need0": (("ag", 0, 1), ("ag", 3, 0), ("ag", 1, 1), ("ag", 4, 0), ("ag", 0, 2), ("ag", 2, 1), ("ag", 1, 2), ("ag", 5, 0), ("ag", 3, 1), ("ag", 6, 0), ("ag", 0, 3), ("ag", 2, 2), ("ag", 7, 1), ("ag", 4, 1), ("ag", 1, 3), ("ag", 5, 1), ("ag", 3, 2)),
    ("attend0", 3): (("ag", 2, 3), ("ag", 8, 0)),
    "out0": (("ag", 4, 2),),
    "need1": (("ag", 3, 3), ("ag", 5, 2), ("ag", 9, 1), ("ag", 6, 1), ("ag", 7, 2), ("ag", 4, 3)),
    ("up0", 3): (("ag", 10, 1),),
    "need2": (("ag", 5, 3), ("ag", 6, 2), ("ag", 8, 1), ("ag", 7, 3), ("ag", 9, 2), ("ag", 11, 1)),
    "need3": (("ag", 6, 3), ("ag", 8, 2), ("ag", 10, 2), ("ag", 9, 3)),
    "out1": (("ag", 8, 3), ("ag", 11, 2)),
    "need4": (("ag", 10, 3),),
    "dxt1": (("ag", 11, 3),),
    "sent12": (("rs", 0, 0), ("rs", 1, 0)),
    "sent11": (("rs", 0, 1), ("rs", 2, 0), ("rs", 3, 0)),
    "lnb1": (("rs", 1, 1),),
    "outb1": (("rs", 0, 2), ("rs", 2, 1), ("rs", 4, 0)),
    ("attb1", 2): (("rs", 3, 1), ("rs", 1, 2)),
    "sent10": (("rs", 0, 3), ("rs", 2, 2), ("rs", 3, 2), ("rs", 5, 0), ("rs", 6, 0)),
    ("downb0", 2): (("rs", 4, 1),),
    "sent02": (("fin", 0, 0), ("rs", 1, 3), ("rs", 2, 3), ("rs", 5, 1), ("rs", 7, 0), ("rs", 8, 0)),
    ("mlpb0", 2): (("rs", 3, 3), ("rs", 6, 1)),
    ("mlpb0", 3): (("fin", 1, 0),),
    "sent01": (("fin", 2, 0), ("rs", 4, 2), ("rs", 5, 2), ("rs", 8, 1), ("rs", 7, 1), ("fin", 3, 0), ("rs", 9, 0), ("rs", 10, 0)),
    "outb0": (("rs", 6, 2), ("rs", 9, 1), ("rs", 11, 0)),
    ("attb0", 2): (("rs", 7, 2),),
    ("attb0", 3): (("rs", 4, 3), ("rs", 10, 1)),
    "sent00": (("rs", 5, 3), ("rs", 8, 2), ("rs", 9, 2), ("fin", 4, 0), ("rs", 6, 3), ("rs", 11, 1), ("rs", 12, 0), ("rs", 13, 0)),
    "end0": (("small", 0, 0), ("rs", 7, 3), ("rs", 10, 2)),
    "end": (("rs", 8, 3), ("rs", 9, 3), ("fin", 5, 0), ("rs", 12, 1), ("small", 0, 1), ("fin", 6, 0), ("rs", 11, 2), ("rs", 10, 3), ("rs", 13, 1), ("fin", 7, 0), ("fin", 8, 0), ("fin", 9, 0), ("small", 0, 2), ("rs", 12, 2), ("rs", 11, 3), ("fin", 10, 0), ("small", 0, 3), ("rs", 13, 2), ("fin", 11, 0), ("rs", 12, 3), ("rs", 13, 3), ("small", 0, 4), ("fin", 12, 0), ("fin", 13, 0)),
}


def rel_consts():
    side = 2 * WIN - 1
    top = side * (WIN - 1) + WIN - 1
    down = np.zeros((96, PAD), np.float32)
    across = np.zeros((GROUP * PAD, GROUP * REL_LANES), np.float32)
    for i in range(SPAN):
        place = side * (i // WIN) + i % WIN
        down[top - place, i] = 1.0
        for h in range(GROUP):
            across[h * PAD + i, h * REL_LANES + place] = 1.0
    return down, across
PART_ROWS, QV_AT, HID_AT, REL_AT = 8, 0, 1, 1 + BLOCKS
SHARE_ROWS, GAIN_AT, BIAS_AT = 16, 0, 2 * BLOCKS


def small_plan(digits):
    names = ("core", "x", "y", "z")
    over = [digits[n] for n in names if digits[n].axis == "tensor"]
    return over, [digits[n] for n in names if digits[n].axis == "fsdp"]


def small_shapes(digits, width):
    over, rest = small_plan(digits)
    left = [d for d in sorted(digits.values(), key=lambda d: d.dim) if d.axis == "tensor"]
    shapes = [tuple(d.size for d in left) + (PART_ROWS, width), (SHARE_ROWS, width)]
    for digit in over:
        left = [d for d in left if d is not digit]
        mine = tuple(d.size for d in left) + (PART_ROWS, width)
        shapes += [(digit.size,) + mine, (digit.size, SHARE_ROWS, width), mine]
    return shapes + [(d.size, PART_ROWS + SHARE_ROWS, width) for d in rest]


def stage_keys(phases):
    return [
        (q, h, phase)
        for q in range(len(REDUCE))
        for h in range(len(REDUCE[q][3]))
        for phase in range(phases)
    ]


def block_kernel(
    n_fsdp, n_tensor,
    x_hbm, ct_hbm, counts, qkv_w, out_w, up_w, down_w, rel_w, qv_w, hid_w, mask, gains, offs, perm, perm_t, rel_down, rel_across,
    xo_hbm, dxo_hbm, gsum, total, keep_gl, keep_gp, keep_qkv, keep_pts,
    wt, dgr, rels, sides, io, xs, ms, aw, qkv, pts, ow, osb, a2, gl, gp, ubuf, acc, dx, cut, awt, dwin, dsum, added,
    *rest,
):
    digits = plan(n_fsdp, n_tensor)
    dims = sorted(digits.values(), key=lambda d: d.dim)
    phases = len(dims)
    parts = wt.shape[-1] // PART
    stage = {}
    for at, key in enumerate(stage_keys(phases)):
        stage[key] = rest[at]
    rest = rest[len(stage) :]
    over, beside = small_plan(digits)
    count = 2 + 3 * len(over) + len(beside)
    parted, shared, smalls = rest[0], rest[1], rest[2:count]
    rest = rest[count:]
    (io_sem, own_sem, keep_sem, rel_send, rel_recv, side_send, side_recv, ag_send, ag_recv, rs_send, rs_recv,
     sm_send, sm_recv) = rest
    images = io.shape[0]
    groups = n_tensor
    rows, width = xs.shape[1:]
    lanes = GROUP * HEAD_DIM
    hid = gl.shape[2]
    cols = wt.shape[-1]
    c_out, c_up, c_down = 3 * lanes, 4 * lanes, 4 * lanes + hid
    heads = lane_heads(lanes)
    tdims = [d for d in dims if d.axis == "tensor"]
    fdims = [d for d in dims if d.axis == "fsdp"]
    per = wt.shape[-2]
    fshape = tuple(d.size for d in fdims) + (per,)
    t_here = lax.axis_index("tensor")

    def tplace(t):
        return tuple(lax.rem(t // d.stride, d.size) for d in tdims)

    def weight(b, t, lo, hi):
        index = (b,) + tplace(t) + (slice(None),) * len(fshape) + (slice(lo, hi),)
        return wt[index].reshape(width, hi - lo)

    def grad_ref(b):
        return dgr if b == BLOCKS - 1 else wt.at[BLOCKS - 1]

    def put_grad(b, t, lo, hi, value):
        index = tplace(t) + (slice(None),) * len(fshape) + (slice(lo, hi),)
        grad_ref(b)[index] = value.astype(BF16).reshape(fshape + (hi - lo,))

    def ag_copies(p, phase):
        b, c, n, names = GATHER[p]
        out = []
        for h in range(len(names)):
            order = [digits[name] for name in names[h]]
            digit = order[phase]
            at = pl.ds(c + h * (n // len(names)), n // len(names))
            index = tuple(slice(None) if d in order[:phase] else d.here() for d in dims)
            place = wt.at[(b,) + index + (slice(None), at)]
            for s in range(1, digit.size):
                out.append(pltpu.make_async_remote_copy(
                    src_ref=place, dst_ref=place, send_sem=ag_send.at[p, phase],
                    recv_sem=ag_recv.at[p, phase], device_id=digit.peer(s)[1], device_id_type=MESH))
        return out

    def span(ref, order, phase, full, at):
        digit = order[phase]
        index = tuple(
            slice(0, digit.size - 1) if d is digit else slice(None) if d in full else d.here()
            for d in dims
        )
        return ref.at[index + (slice(None), at)]

    def ag_all(p, phase):
        b, c, n, names = GATHER[p]
        order = [digits[name] for name in names[0]]
        place = span(wt.at[b], order, phase, order[:phase], pl.ds(c, n))
        return pltpu.make_async_remote_copy(
            src_ref=place, dst_ref=place, send_sem=ag_send.at[p, phase],
            recv_sem=ag_recv.at[p, phase], device_id=order[phase].peer(1)[1], device_id_type=MESH)

    def start(copies):
        for cp in copies:
            cp.start()

    def arrive(whole):
        whole.wait_recv()

    def sent(whole):
        whole.wait_send()

    def ag_step(p, phase):
        if phase > 0:
            arrive(ag_all(p, phase - 1))
        start(ag_copies(p, phase))

    def need(b, lo, hi):
        for p, (block, c, n, _) in enumerate(GATHER):
            if block == b and c < hi and lo < c + n:
                arrive(ag_all(p, phases - 1))

    def rs_copies(q, phase):
        b, c, n, names = REDUCE[q]
        out = []
        for h in range(len(names)):
            order = [digits[name] for name in names[h]][::-1]
            digit = order[phase]
            at = pl.ds(c + h * (n // len(names)), n // len(names))
            for s in range(1, digit.size):
                to, device = digit.peer(s)
                index = tuple(
                    to if d is digit else d.here() if d in order[:phase] else slice(None) for d in dims
                )
                out.append(pltpu.make_async_remote_copy(
                    src_ref=grad_ref(b).at[index + (slice(None), at)],
                    dst_ref=stage[q, h, phase].at[s - 1],
                    send_sem=rs_send.at[q, phase], recv_sem=rs_recv.at[q, phase],
                    device_id=device, device_id_type=MESH))
        return out

    def rs_all(q, phase):
        b, c, n, names = REDUCE[q]
        order = [digits[name] for name in names[0]][::-1]
        place = span(grad_ref(b), order, phase, order[phase + 1 :], pl.ds(c, n))
        return pltpu.make_async_remote_copy(
            src_ref=place, dst_ref=place, send_sem=rs_send.at[q, phase],
            recv_sem=rs_recv.at[q, phase], device_id=order[phase].peer(1)[1], device_id_type=MESH)

    def rs_absorb(q, phase):
        b, c, n, names = REDUCE[q]
        grad = grad_ref(b)
        for h in range(len(names)):
            order = [digits[name] for name in names[h]][::-1]
            digit = order[phase]
            at = slice(c + h * (n // len(names)), c + (h + 1) * (n // len(names)))
            left = [d for d in dims if d not in order[: phase + 1]]
            land = stage[q, h, phase]
            steps = int(np.prod([d.size for d in left])) if left else 1

            def one(i, carry):
                place = {}
                more = i
                for d in reversed(left):
                    place[d.name] = lax.rem(more, d.size)
                    more = more // d.size
                index = tuple(place[d.name] if d in left else d.here() for d in dims)
                value = grad[index + (slice(None), at)]
                for s in range(digit.size - 1):
                    value = value + land[(s,) + tuple(place[d.name] for d in left)]
                grad[index + (slice(None), at)] = value
                return carry

            lax.fori_loop(0, steps, one, 0, unroll=min(steps, ABS_UNROLL))

    def rs_step(q, phase):
        if phase > 0:
            arrive(rs_all(q, phase - 1))
            rs_absorb(q, phase - 1)
        start(rs_copies(q, phase))

    def rs_finish(q):
        arrive(rs_all(q, phases - 1))
        b, c, n, names = REDUCE[q]
        for h in range(len(names)):
            at = slice(c + h * (n // len(names)), c + (h + 1) * (n // len(names)))
            index = tuple(d.here() for d in dims)
            value = grad_ref(b)[index + (slice(None), at)].astype(F32)
            for s in range(digits[names[h][0]].size - 1):
                value = value + stage[q, h, phases - 1][s].astype(F32)
            gsum[b, :, at] = value

    def slot(name):
        for kind, item, phase in SCHEDULE.get(name, ()):
            if kind == "ag":
                ag_step(item, phase)
            elif kind == "rs":
                rs_step(item, phase)
            elif kind == "fin":
                rs_finish(item)
            else:
                small_step(phase)

    def hooks(t, name):
        for at in range(groups):
            if (name, at) in SCHEDULE:

                @pl.when(t == at)
                def _():
                    slot((name, at))

    def small_copies(phase):
        order = over + beside
        digit = order[phase]
        pairs = []
        if phase < len(over):
            land_part, land_share, _ = smalls[3 * phase : 3 * phase + 3]
            source = parted if phase == 0 else smalls[3 * phase - 1]
            left = [d for d in tdims if d not in order[:phase]]
            here = digit.here()
            for s in range(1, digit.size):
                index = tuple(digit.peer(s)[0] if d is digit else slice(None) for d in left)
                pairs.append((s, source.at[index], land_part.at[here]))
                pairs.append((s, land_share.at[here], land_share.at[here]))
            rows_all = sum(int(np.prod(src.shape[:-1])) for _, src, _ in pairs)
            whole = ubuf.at[0:rows_all]
        else:
            land = smalls[3 * len(over) + phase - len(over)]
            for s in range(1, digit.size):
                pairs.append((s, land.at[digit.here()], land.at[digit.here()]))
            whole = land.at[0 : digit.size - 1]
        copies = [
            pltpu.make_async_remote_copy(
                src_ref=src, dst_ref=dst, send_sem=sm_send.at[phase], recv_sem=sm_recv.at[phase],
                device_id=digit.peer(s)[1], device_id_type=MESH)
            for s, src, dst in pairs
        ]
        return copies, pltpu.make_async_remote_copy(
            src_ref=whole, dst_ref=whole, send_sem=sm_send.at[phase], recv_sem=sm_recv.at[phase],
            device_id=digit.peer(1)[1], device_id_type=MESH)

    def small_step(phase):
        order = over + beside
        if phase > 0:
            arrive(small_copies(phase - 1)[1])
            size = order[phase - 1].size
            if phase <= len(over):
                land_part, land_share, after = smalls[3 * phase - 3 : 3 * phase]
                part, share = land_part[0], land_share[0]
                for s in range(1, size):
                    part, share = part + land_part[s], share + land_share[s]
                after[...] = part
            else:
                land = smalls[3 * len(over) + phase - 1 - len(over)]
                value = land[0]
                for s in range(1, size):
                    value = value + land[s]
        else:
            share = shared[...]
        if phase < len(over):
            digit = order[phase]
            land_part, land_share, _ = smalls[3 * phase : 3 * phase + 3]
            source = parted if phase == 0 else smalls[3 * phase - 1]
            left = [d for d in tdims if d not in order[:phase]]
            index = tuple(digit.here() if d is digit else slice(None) for d in left)
            land_part[digit.here()] = source[index]
            land_share[digit.here()] = share
        elif phase < len(order):
            land = smalls[3 * len(over) + phase - len(over)]
            here = order[phase].here()
            if phase == len(over):
                land[here, 0:PART_ROWS] = smalls[3 * phase - 1][...]
                land[here, PART_ROWS:] = share
            else:
                land[here] = value
        else:
            total[...] = value
        if phase < len(order):
            start(small_copies(phase)[0])

    loads = [
        pltpu.make_async_copy(x_hbm, io, io_sem.at[0]),
        pltpu.make_async_copy(ct_hbm, io, io_sem.at[1]),
    ]
    own_copies = []
    for b in range(BLOCKS):
        rows_of = [pl.ds((3 * b + j) * per, per) for j in range(3)]
        pieces_of = [(qkv_w.at[b, j], ubuf.at[rows_of[0], pl.ds(j * lanes, lanes)]) for j in range(3)]
        pieces_of.append((out_w.at[b], ubuf.at[rows_of[0], pl.ds(3 * lanes, lanes)]))
        pieces_of.append((up_w.at[b], ubuf.at[rows_of[1], :]))
        pieces_of.append((down_w.at[b], ubuf.at[rows_of[2], :]))
        own_copies.append([
            pltpu.make_async_copy(src, dst, own_sem.at[b, j]) for j, (src, dst) in enumerate(pieces_of)
        ])
        for cp in own_copies[b]:
            cp.start()
    loads[0].start()
    greet(all_peers(digits, n_tensor))
    mine = tuple(d.here() for d in dims)
    for b in range(BLOCKS):
        for cp in own_copies[b]:
            cp.wait()
        for j in range(parts):
            row = (3 * b + j) * per
            wt[(b,) + mine + (slice(None), slice(j * PART, (j + 1) * PART))] = ubuf[
                row : row + per, :
            ].astype(BF16)
        slot("start%d" % b)

    parted[...] = jnp.zeros_like(parted)
    shared[...] = jnp.zeros_like(shared)

    rel_count = rel_w.shape[2]
    added[0, 0:8, :] = jnp.zeros((8, GROUP * PAD), F32)
    for b in range(BLOCKS):
        added[0, GROUP * b : GROUP * (b + 1), 0:rel_count] = rel_w[b]
        row = jnp.concatenate(
            [added[0, GROUP * b + h : GROUP * b + h + 1, :] for h in range(GROUP)], 1
        )
        skew = jnp.broadcast_to(row, (8, row.shape[1]))
        row_id = lax.broadcasted_iota(jnp.int32, skew.shape, 0)
        for bit in (1, 2, 4):
            skew = jnp.where((row_id & bit) != 0, pltpu.roll(skew, skew.shape[1] - bit, 1), skew)
        wide = jnp.concatenate(
            [skew]
            + [pltpu.roll(skew, skew.shape[1] - 8 * a, 1) for a in range(1, rel_down.shape[0] // 8)], 0
        )
        wide = dot(rel_down[...], wide.astype(BF16), TN).astype(BF16)
        rels[t_here, b] = dot(wide, rel_across[...], NT).astype(BF16)
        sides[t_here, 2 * b : 2 * b + 2, 0:lanes] = qv_w[b]
    sides[t_here, 2 * BLOCKS : 3 * BLOCKS, :] = hid_w[...]
    side_copies = [
        pltpu.make_async_remote_copy(
            src_ref=ref.at[t_here], dst_ref=ref.at[t_here], send_sem=ssem.at[j], recv_sem=rsem.at[j],
            device_id=device, device_id_type=MESH)
        for ref, ssem, rsem in ((rels, rel_send, rel_recv), (sides, side_send, side_recv))
        for j, device in enumerate(tensor_peers(n_tensor))
    ]
    start(side_copies)
    slot("x0")

    used = images * TOKENS
    floor = used // 8 * 8
    loads[0].wait()
    xs[0, floor:rows, :] = jnp.zeros((rows - floor, width), F32)
    for i in range(images):
        xs[0, i * TOKENS : (i + 1) * TOKENS, :] = io[i]
    loads[1].start()

    def first_norm(b):
        norm_into(xs.at[b], cut, gains[b, 0:1, :], offs[b, 0:1, :])
        for i in range(images):
            base = image_base(i)
            aw[b, i * IMG_PAD : (i + 1) * IMG_PAD, :] = dot(
                perm[b, i], cut[base : base + IMG_ROWS, :]
            ).astype(BF16)

    first_norm(0)
    slot("dx")
    loads[1].wait()
    dx[floor:rows, :] = jnp.zeros((rows - floor, width), F32)
    for i in range(images):
        live = (t_here * images + i < counts[0]).astype(F32)
        dx[i * TOKENS : (i + 1) * TOKENS, :] = io[i] * live
    slot("need0")
    for cp in side_copies:
        cp.wait()

    att_keeps = [
        pltpu.make_async_copy(qkv, keep_qkv, keep_sem.at[0]),
        pltpu.make_async_copy(pts, keep_pts, keep_sem.at[1]),
    ]
    mlp_keeps = [
        pltpu.make_async_copy(gl, keep_gl, keep_sem.at[2]),
        pltpu.make_async_copy(gp, keep_gp, keep_sem.at[3]),
    ]
    bias_at = 0
    for b in range(BLOCKS):
        off2, off3 = (offs[b, j : j + 1, :].astype(BF16).astype(F32) for j in (2, 3))
        if b > 0:
            first_norm(b)
            for cp in att_keeps:
                cp.wait()
        if b > 0:
            slot("need3")
        need(b, 0, c_up)

        def attend(t, carry):
            hooks(t, "attend%d" % b)
            rows_qkv = dot(aw[b], weight(b, t, 0, c_out))
            for j in range(3):
                part = rows_qkv[:, j * lanes : (j + 1) * lanes]
                if j != 1:
                    at = bias_at + 2 * b + j // 2
                    part = part + sides[t, at : at + 1, 0:lanes].astype(BF16).astype(F32)
                qkv[t, :, j * lanes : (j + 1) * lanes] = part.astype(BF16)

            for w in range(WINS):
                add = rels[t, b].astype(F32) + mask[b, w].astype(F32)
                added[w] = add * LOG2E

            def window(g, c2):
                spots = [pl.ds(pl.multiple_of((g * BATCH + j) * PAD, PAD), PAD) for j in range(BATCH)]
                s = []
                for spot in spots:
                    q = qkv[t, spot, 0:lanes]
                    k = qkv[t, spot, lanes : 2 * lanes]
                    s.append(dot(k, spread(q, heads), NT))
                p = []
                for j in range(BATCH):
                    sj = s[j] * (INV_ROOT * LOG2E) + added[lax.rem(g * BATCH + j, WINS)]
                    e = jnp.exp2(sj - jnp.max(sj, 0, keepdims=True))
                    p.append((e * (1.0 / jnp.sum(e, 0, keepdims=True))).astype(BF16))
                    pts[t, g * BATCH + j] = p[j]
                for j in range(BATCH):
                    v = qkv[t, spots[j], 2 * lanes : 3 * lanes]
                    ow[spots[j], :] = gather_diag(dot(p[j], v, TN), heads).astype(BF16)
                return c2

            lax.fori_loop(0, images * WINS // BATCH, window, 0)
            put_rows(
                osb.at[b, t],
                [dot(perm_t[b, i], ow[i * IMG_PAD : (i + 1) * IMG_PAD, :]) for i in range(images)],
            )
            return carry

        lax.fori_loop(0, groups, attend, 0)
        if b + 1 < BLOCKS:
            start(att_keeps)
        slot("out%d" % b)
        y = dot(osb[b, 0], weight(b, 0, c_out, c_up), NT)
        for t in range(1, groups):
            y = y + dot(osb[b, t], weight(b, t, c_out, c_up), NT)
        ms[b] = xs[b] + y + off2
        norm_into(ms.at[b], a2.at[b], gains[b, 1:2, :], offs[b, 1:2, :])
        if b + 1 < BLOCKS:
            acc[...] = ms[b] + off3
        if b > 0:
            for cp in mlp_keeps:
                cp.wait()
        slot("need%d" % (1 + 3 * b))
        need(b, c_up, c_down)

        def up(t, carry):
            hooks(t, "up%d" % b)
            ubuf[0:rows, :] = dot(a2[b], weight(b, t, c_up, c_down))
            at = bias_at + 2 * BLOCKS + b
            hbias = sides[t, at : at + 1, :].astype(BF16).astype(F32)
            for r, n in chunks(rows, 32):
                g, d = gelu_pair(ubuf[r : r + n, :] + hbias)
                gl[t, r : r + n, :] = g.astype(BF16)
                gp[t, r : r + n, :] = d.astype(BF16)
            return carry

        lax.fori_loop(0, groups, up, 0)
        if b + 1 == BLOCKS:
            break
        slot("need2")
        need(b, c_down, cols)

        def down(t, carry):
            hooks(t, "down0")
            acc[...] += dot(gl[t], weight(b, t, c_down, cols), NT)
            return carry

        lax.fori_loop(0, groups, down, 0)
        start(mlp_keeps)
        xs[b + 1] = acc[...]
        slot("norm1")

    last = BLOCKS - 1
    mlp_loads = [
        pltpu.make_async_copy(keep_gl, gl, keep_sem.at[2]),
        pltpu.make_async_copy(keep_gp, gp, keep_sem.at[3]),
    ]
    att_loads = [
        pltpu.make_async_copy(keep_qkv, qkv, keep_sem.at[0]),
        pltpu.make_async_copy(keep_pts, pts, keep_sem.at[1]),
    ]
    for b in range(BLOCKS - 1, -1, -1):
        bias_row = BIAS_AT + 4 * b
        shared[bias_row + 3 : bias_row + 4, :] = column_sum(dx)
        cut[...] = dx[...].astype(BF16)
        slot("dxt%d" % b)
        dxt = jnp.transpose(cut[...])
        a_t = jnp.transpose(a2[b])
        if b < last:
            for p in range(len(GATHER)):
                if GATHER[p][0] == last:
                    for phase in range(phases):
                        sent(ag_all(p, phase))
            for cp in mlp_loads:
                cp.wait()

        def down_back(t, carry):
            hooks(t, "downb%d" % b)
            put_grad(b, t, c_down, cols, dot(dxt, gl[t]))
            return carry

        lax.fori_loop(0, groups, down_back, 0)
        slot("sent%d2" % b)
        if b == last:
            slot("need5")
            need(b, c_down, cols)
        acc[...] = jnp.zeros_like(acc)

        def mlp_back(t, carry):
            hooks(t, "mlpb%d" % b)
            dh = dot(cut[...], weight(b, t, c_down, cols))
            du = (dh * gp[t].astype(F32)).astype(BF16)
            gp[t] = du
            parted[tplace(t) + (slice(HID_AT + b, HID_AT + b + 1), slice(None))] = jnp.sum(
                fold(du.astype(F32)), 0, keepdims=True
            )
            put_grad(b, t, c_up, c_down, dot(a_t, du))
            acc[...] += dot(du, weight(b, t, c_up, c_down), NT)
            return carry

        lax.fori_loop(0, groups, mlp_back, 0)
        slot("sent%d1" % b)
        if b == last:
            slot("result")
            result = ubuf
            off3 = offs[b, 3:4, :].astype(BF16).astype(F32)
            result[0:rows, :] = ms[b] + off3

            def down(t, carry):
                hooks(t, "result1")
                result[0:rows, :] += dot(gl[t], weight(b, t, c_down, cols), NT)
                return carry

            lax.fori_loop(0, groups, down, 0)
            for i in range(images):
                io[i] = result[i * TOKENS : (i + 1) * TOKENS, :]
            x_store = pltpu.make_async_copy(io, xo_hbm, io_sem.at[0])
            x_store.start()
            start(mlp_loads)
        slot("lnb%d" % b)
        sums = back_norm(ms.at[b], acc, gains[b, 1:2, :], dx)
        shared[GAIN_AT + 2 * b + 1 : GAIN_AT + 2 * b + 2, :] = sums[0]
        shared[bias_row + 1 : bias_row + 2, :] = sums[1]
        shared[bias_row + 2 : bias_row + 3, :] = sums[2]
        cut[...] = dx[...].astype(BF16)
        dmt = jnp.transpose(cut[...])
        awt[...] = jnp.transpose(aw[b])
        da = ubuf
        da[...] = jnp.zeros_like(da)
        for t in range(groups):
            put_grad(b, t, c_out, c_up, dot(dmt, osb[b, t]))
        slot("outb%d" % b)
        if b < last:
            for cp in att_loads:
                cp.wait()

        def attend_back(t, carry):
            hooks(t, "attb%d" % b)
            do_t = dot(cut[...], weight(b, t, c_out, c_up)).astype(BF16)
            for i in range(images):
                base = image_base(i)
                ow[i * IMG_PAD : (i + 1) * IMG_PAD, :] = dot(
                    perm[b, i], do_t[base : base + IMG_ROWS]
                ).astype(BF16)
            dsum[...] = jnp.zeros_like(dsum)

            def window(g, c2):
                spots = [pl.ds(pl.multiple_of((g * BATCH + j) * PAD, PAD), PAD) for j in range(BATCH)]
                dob = [spread(ow[spot, :], heads) for spot in spots]
                dp = [dot(qkv[t, spots[j], 2 * lanes : 3 * lanes], dob[j], NT) for j in range(BATCH)]
                ds = []
                for j in range(BATCH):
                    p = pts[t, g * BATCH + j]
                    dv = dot(p, dob[j])
                    dwin[spots[j], 2 * lanes : 3 * lanes] = dv.astype(BF16)
                    pf = p.astype(F32)
                    ds.append((pf * (dp[j] - jnp.sum(pf * dp[j], 0, keepdims=True))).astype(BF16))
                dsum[...] += sum(d.astype(F32) for d in ds)
                for j in range(BATCH):
                    q = qkv[t, spots[j], 0:lanes]
                    k = qkv[t, spots[j], lanes : 2 * lanes]
                    dk = dot(ds[j], spread(q, heads)) * INV_ROOT
                    dwin[spots[j], lanes : 2 * lanes] = dk.astype(BF16)
                    dq = gather_diag(dot(ds[j], k, TN), heads) * INV_ROOT
                    dwin[spots[j], 0:lanes] = dq.astype(BF16)
                return c2

            lax.fori_loop(0, images * WINS // BATCH, window, 0)
            for j in range(2):
                val = dwin[:, 2 * j * lanes : (2 * j + 1) * lanes].astype(F32)
                col = slice((2 * b + j) * lanes, (2 * b + j + 1) * lanes)
                parted[tplace(t) + (slice(QV_AT, QV_AT + 1), col)] = jnp.sum(fold(val), 0, keepdims=True)
            ds_all = dsum[...]
            high = ds_all.astype(BF16)
            rest_low = (ds_all - high.astype(F32)).astype(BF16)
            wide = sum(
                dot(dot(rel_down[...], piece).astype(BF16), rel_across[...])
                for piece in (high, rest_low)
            )
            skew = wide[0:8]
            for a in range(1, wide.shape[0] // 8):
                skew = skew + pltpu.roll(wide[8 * a : 8 * a + 8], 8 * a, 1)
            row_id = lax.broadcasted_iota(jnp.int32, skew.shape, 0)
            for bit in (1, 2, 4):
                skew = jnp.where((row_id & bit) != 0, pltpu.roll(skew, bit, 1), skew)
            skew = jnp.sum(skew, 0, keepdims=True)
            for h in range(GROUP):
                row = REL_AT + (b * GROUP + h) // 2
                col = slice(h % 2 * REL_LANES, (h % 2 + 1) * REL_LANES)
                parted[tplace(t) + (slice(row, row + 1), col)] = skew[
                    :, h * REL_LANES : (h + 1) * REL_LANES
                ]
            put_grad(b, t, 0, c_out, dot(awt[...], dwin[...]))
            da[...] += dot(dwin[...], weight(b, t, 0, c_out), NT)
            return carry

        lax.fori_loop(0, groups, attend_back, 0)
        slot("sent%d0" % b)
        if b == last:
            start(att_loads)
        slot("ln1b%d" % b)
        vals = []
        for i in range(images):
            part = da[i * IMG_PAD : (i + 1) * IMG_PAD, :]
            high = part.astype(BF16)
            rest_low = (part - high.astype(F32)).astype(BF16)
            vals.append(dot(perm_t[b, i], high) + dot(perm_t[b, i], rest_low))
        put_rows(acc, vals)
        sums = back_norm(xs.at[b], acc, gains[b, 0:1, :], dx)
        shared[GAIN_AT + 2 * b : GAIN_AT + 2 * b + 1, :] = sums[0]
        shared[bias_row : bias_row + 1, :] = sums[1]
    slot("end0")
    x_store.wait()
    for i in range(images):
        io[i] = dx[i * TOKENS : (i + 1) * TOKENS, :]
    dx_store = pltpu.make_async_copy(io, dxo_hbm, io_sem.at[1])
    dx_store.start()
    slot("end")
    dx_store.wait()
    for p in range(len(GATHER)):
        if GATHER[p][0] != last:
            for phase in range(phases):
                sent(ag_all(p, phase))
    for q in range(len(REDUCE)):
        for phase in range(phases):
            sent(rs_all(q, phase))
    for phase in range(phases):
        sent(small_copies(phase)[1])


def block_call(x, ct, counts, mats, rel, qv, hidden, gains, offs, n_fsdp, n_tensor):
    images, _, width = x.shape
    per, lanes = mats[1].shape[1:]
    hid = mats[2].shape[2]
    cols = 4 * lanes + 2 * hid
    parts = cols // PART
    rows = -(-images * TOKENS // 16) * 16
    wrows = images * IMG_PAD
    digits = plan(n_fsdp, n_tensor)
    dims = sorted(digits.values(), key=lambda d: d.dim)
    sizes = tuple(d.size for d in dims)
    phases = len(dims)
    perm = permutations(images)
    down, across = rel_consts()
    consts = (
        jnp.asarray(np.tile(mask_table(), (1, 1, 1, GROUP)), BF16),
        jnp.asarray(perm, BF16),
        jnp.asarray(np.swapaxes(perm, 2, 3), BF16),
        jnp.asarray(down, BF16),
        jnp.asarray(across, BF16),
    )
    small = small_shapes(digits, width)
    stages = []
    for q, h, phase in stage_keys(phases):
        order = [digits[n] for n in REDUCE[q][3][h]][::-1]
        left = tuple(d.size for d in dims if d not in order[: phase + 1])
        stages.append(pltpu.VMEM((order[phase].size - 1,) + left + (per, REDUCE[q][2] // len(REDUCE[q][3])), BF16))
    vmem = pl.BlockSpec(memory_space=pltpu.VMEM)
    anyspace = pl.BlockSpec(memory_space=pl.ANY)
    keep = [
        (n_tensor, rows, hid), (n_tensor, rows, hid), (n_tensor, wrows, 3 * lanes),
        (n_tensor, images * WINS, PAD, GROUP * PAD),
    ]
    dma = pltpu.SemaphoreType.DMA
    out = pl.pallas_call(
        functools.partial(block_kernel, n_fsdp, n_tensor),
        out_shape=(
            jax.ShapeDtypeStruct(x.shape, F32),
            jax.ShapeDtypeStruct(x.shape, F32),
            jax.ShapeDtypeStruct((BLOCKS, per, cols), F32),
            jax.ShapeDtypeStruct((PART_ROWS + SHARE_ROWS, width), F32),
        ) + tuple(jax.ShapeDtypeStruct(s, BF16) for s in keep),
        in_specs=[
            anyspace, anyspace, pl.BlockSpec(memory_space=pltpu.SMEM), anyspace, anyspace, anyspace,
            anyspace,
        ] + [vmem] * 10,
        out_specs=(anyspace, anyspace, vmem, vmem) + (anyspace,) * 4,
        scratch_shapes=[
            pltpu.VMEM((BLOCKS,) + sizes + (per, cols), BF16),
            pltpu.VMEM(sizes + (per, cols), BF16),
            pltpu.VMEM((n_tensor, BLOCKS, PAD, GROUP * PAD), BF16),
            pltpu.VMEM((n_tensor, 8, hid), F32),
            pltpu.VMEM(x.shape, F32),
            pltpu.VMEM((BLOCKS, rows, width), F32),
            pltpu.VMEM((BLOCKS, rows, width), F32),
            pltpu.VMEM((BLOCKS, wrows, width), BF16),
            pltpu.VMEM(keep[2], BF16),
            pltpu.VMEM(keep[3], BF16),
            pltpu.VMEM((wrows, lanes), BF16),
            pltpu.VMEM((BLOCKS, n_tensor, rows, lanes), BF16),
            pltpu.VMEM((BLOCKS, rows, width), BF16),
            pltpu.VMEM(keep[0], BF16),
            pltpu.VMEM(keep[1], BF16),
            pltpu.VMEM((wrows, width), F32),
            pltpu.VMEM((rows, width), F32),
            pltpu.VMEM((rows, width), F32),
            pltpu.VMEM((rows, width), BF16),
            pltpu.VMEM((width, wrows), BF16),
            pltpu.VMEM((wrows, 3 * lanes), BF16),
            pltpu.VMEM((PAD, GROUP * PAD), F32),
            pltpu.VMEM((WINS, PAD, GROUP * PAD), F32),
        ]
        + stages
        + [pltpu.VMEM(shape, F32) for shape in small]
        + [
            dma((2,)), dma((BLOCKS, 6)), dma((4,)),
            dma((n_tensor - 1,)), dma((n_tensor - 1,)), dma((n_tensor - 1,)), dma((n_tensor - 1,)),
            dma((len(GATHER), phases)), dma((len(GATHER), phases)),
            dma((len(REDUCE), phases)), dma((len(REDUCE), phases)),
            dma((phases,)), dma((phases,)),
        ],
        compiler_params=pltpu.CompilerParams(
            has_side_effects=True, vmem_limit_bytes=127 * MIB // 2,
            collective_id=0,
        ),
    )(x, ct, counts, *mats, rel, qv, hidden, consts[0], gains, offs, *consts[1:])
    return out[:4]


def adam_kernel(*refs):
    count = 31
    ins, outs = refs[:count], refs[count : 2 * count - 2]
    held, sem = refs[2 * count - 2 : -1], refs[-1]
    copies = [
        pltpu.make_async_copy(src, dst, sem.at[j]) for j, (src, dst) in enumerate(zip(ins, held))
    ]
    for cp in copies:
        cp.start()
    passed = [pltpu.make_async_copy(held[j], outs[j], sem.at[j]) for j in range(2)]
    for j in range(2):
        copies[j].wait()
        passed[j].start()
    for cp in copies[2:]:
        cp.wait()
    gsum, total = held[2:4]
    params = [held[4 + 3 * j : 7 + 3 * j] for j in range(9)]
    news = [outs[2 + 3 * j : 5 + 3 * j] for j in range(9)]
    lanes = GROUP * HEAD_DIM
    hid = params[2][0].shape[2]

    def update(kind, place, grad, rate, decay):
        new = adam(*(p[place] for p in params[kind]), grad, rate, decay)
        for ref, val in zip(news[kind], new):
            ref[place] = val

    for b in range(BLOCKS):
        for j in range(3):
            update(0, (b, j), gsum[b, :, j * lanes : (j + 1) * lanes], MATRIX_RATE, WEIGHT_DECAY)
        update(1, (b,), gsum[b, :, 3 * lanes : 4 * lanes], MATRIX_RATE, WEIGHT_DECAY)
        update(2, (b,), gsum[b, :, 4 * lanes : 4 * lanes + hid], MATRIX_RATE, WEIGHT_DECAY)
        update(3, (b,), gsum[b, :, 4 * lanes + hid :], MATRIX_RATE, WEIGHT_DECAY)
        heads, rels = params[4][0].shape[1:]
        for h in range(heads):
            row, col = REL_AT + (b * GROUP + h) // 2, h % 2 * REL_LANES
            grad = total[row : row + 1, col : col + rels]
            update(4, (b, slice(h, h + 1)), grad, SMALL_RATE, 0.0)
        for j in range(2):
            grad = total[QV_AT : QV_AT + 1, (2 * b + j) * lanes : (2 * b + j + 1) * lanes]
            update(5, (b, slice(j, j + 1)), grad, SMALL_RATE, 0.0)
        update(6, (slice(b, b + 1),), total[HID_AT + b : HID_AT + b + 1, :], SMALL_RATE, 0.0)
        at = PART_ROWS + GAIN_AT + 2 * b
        update(7, (b,), total[at : at + 2, :], SMALL_RATE, 0.0)
        at = PART_ROWS + BIAS_AT + 4 * b
        update(8, (b,), total[at : at + 4, :], SMALL_RATE, 0.0)
    for cp in passed:
        cp.wait()


def adam_call(x, dx, gsum, total, params):
    flat = [p for group in params for p in group]
    ins = [x, dx, gsum, total] + flat
    hbm = pl.BlockSpec(memory_space=pltpu.HBM)
    vmem = pl.BlockSpec(memory_space=pltpu.VMEM)
    return pl.pallas_call(
        adam_kernel,
        out_shape=tuple(jax.ShapeDtypeStruct(p.shape, p.dtype) for p in [x, dx] + flat),
        in_specs=[hbm] * len(ins),
        out_specs=(hbm, hbm) + tuple(vmem for _ in flat),
        scratch_shapes=[pltpu.VMEM(p.shape, p.dtype) for p in ins]
        + [pltpu.SemaphoreType.DMA((len(ins),))],
        compiler_params=pltpu.CompilerParams(vmem_limit_bytes=127 * MIB // 2),
    )(*ins)


def shards(n_fsdp, n_tensor, *args):
    image_rows, cotangent, live_counts = args[:3]
    groups = [args[3 + 3 * j : 6 + 3 * j] for j in range(9)]
    turn = {0: lambda p: p.transpose(0, 2, 1, 3), 1: lambda p: p.swapaxes(1, 2), 3: lambda p: p.swapaxes(1, 2)}
    for j, f in turn.items():
        groups[j] = [f(p) for p in groups[j]]
    mats = [g[0] for g in groups[:4]]
    rel, qv, hidden, gain, bias = [g[0] for g in groups[4:]]
    x, dx, gsum, total = block_call(
        image_rows, cotangent, live_counts, mats, rel, qv, hidden, gain, bias, n_fsdp, n_tensor
    )
    new = adam_call(x, dx, gsum, total, groups)
    x, dx = new[:2]
    new = [list(new[2 + 3 * j : 5 + 3 * j]) for j in range(9)]
    for j, f in turn.items():
        new[j] = [f(p) for p in new[j]]
    return (x, dx) + tuple(p for group in new for p in group)
```
